128 devices in a mesh: section: 2 (over x_lo), tensor: 16 (over x_hi, y, core), dp: 4 (over z).
Axes of the slice: x: 4 (x_hi: 2, x_lo: 2; x = x_hi * 2 + x_lo), y: 4, z: 4, core: 2. Of those that a mesh axis runs over, the one named last changes fastest.
Arguments:
- images: bfloat16 [4, 1, 576, 1024], P(None, None, 'dp', 'tensor'), may hold values from -6 to 6
- cotangent: bfloat16 [4, 1, 576, 1024], P(None, None, 'dp', 'tensor'), may hold values from -6 to 6
- ln1_gain: float32 [2, 1024], P('section', 'tensor'), may hold values from 0.25 to 1.75
- ln1_bias: float32 [2, 1024], P('section', 'tensor'), may hold values from -3 to 3
- qkv_weight: bfloat16 [2, 1024, 16, 192], P('section', None, 'tensor'), may hold values from -0.1875 to 0.1875
- qv_bias: float32 [2, 16, 128], P('section', 'tensor'), may hold values from -3 to 3
- output_projection_weight: bfloat16 [2, 16, 64, 1024], P('section', 'tensor'), may hold values from -0.75 to 0.75
- out_bias: float32 [2, 1024], P('section', 'tensor'), may hold values from -3 to 3
- ln2_gain: float32 [2, 1024], P('section', 'tensor'), may hold values from 0.25 to 1.75
- ln2_bias: float32 [2, 1024], P('section', 'tensor'), may hold values from -3 to 3
- expand_weight: bfloat16 [2, 1024, 4096], P('section', None, 'tensor'), may hold values from -0.1875 to 0.1875
- up_bias: float32 [2, 4096], P('section', 'tensor'), may hold values from -3 to 3
- down_weight: bfloat16 [2, 4096, 1024], P('section', 'tensor'), may hold values from -0.09375 to 0.09375
- down_bias: float32 [2, 1024], P('section', 'tensor'), may hold values from -3 to 3
Outputs:
- activations: bfloat16 [2, 4, 1, 576, 1024], P('section', None, None, 'dp', 'tensor')
- input_grads: bfloat16 [2, 4, 1, 576, 1024], P('section', None, None, 'dp', 'tensor')
- ln1_gain_grad: float32 [2, 1024], P('section', ('tensor', 'dp'))
- ln1_bias_grad: float32 [2, 1024], P('section', ('tensor', 'dp'))
- qkv_grad: float32 [2, 1024, 16, 192], P('section', 'dp', 'tensor')
- qv_bias_grad: float32 [2, 16, 128], P('section', 'tensor', 'dp')
- out_weight_grad: float32 [2, 16, 64, 1024], P('section', 'tensor', None, 'dp')
- out_bias_grad: float32 [2, 1024], P('section', ('tensor', 'dp'))
- ln2_gain_grad: float32 [2, 1024], P('section', ('tensor', 'dp'))
- ln2_bias_grad: float32 [2, 1024], P('section', ('tensor', 'dp'))
- up_grad: float32 [2, 1024, 4096], P('section', 'dp', 'tensor')
- up_bias_grad: float32 [2, 4096], P('section', ('tensor', 'dp'))
- down_grad: float32 [2, 4096, 1024], P('section', 'tensor', 'dp')
- down_bias_grad: float32 [2, 1024], P('section', ('tensor', 'dp'))
The draws below stay inside these ranges and needn't reach their ends.
All inputs are finite; a program needn't handle non-finite values.
Results may differ from the reference program's by a relative error of at most 0.023.
Values may be sent and summed in bfloat16 or wider, within the bound.
A program may use at most 128 MiB of HBM per device.

```python
import jax
import jax.numpy as jnp
from jax import lax

D = 1024
HEADS = 16
HEAD_DIM = 64
FF = 4096
IMG_TOK = 576
IMGS = 1
MICRO = 4


def levels(key, dims, split, low, high):
    loudness = 1.0
    for position, parts in split:
        heights = jax.random.uniform(jax.random.fold_in(jax.random.fold_in(key, 6), position), (parts,), jnp.float32, low / len(split), high / len(split))
        loudness = loudness * jnp.repeat(jnp.exp(heights), dims[position] // parts).reshape((-1,) + (1,) * (len(dims) - 1 - position))
    return loudness


def centred(own_key, dims, scale, most, pieces=(), dtype=jnp.bfloat16):
    drawn = jax.random.normal(own_key, dims, jnp.float32) * scale
    if len(pieces) > 0:
        drawn = levels(own_key, dims, pieces, -0.22, 0.18) * drawn
    return jnp.clip(drawn, min=-most, max=most).astype(dtype)


def setup_inputs(seed: int = 0) -> dict:
    arg_keys = jax.random.split(jax.random.key(seed), 15)
    images = centred(arg_keys[0], (MICRO, IMGS, IMG_TOK, D), 1.0, 6.0, ((2, 4), (3, 16)))
    cotangent = centred(arg_keys[1], (MICRO, IMGS, IMG_TOK, D), 1.0, 6.0, ((2, 4), (3, 16)))
    ln1_gain = jnp.clip(1.0 + 0.15 * jax.random.normal(arg_keys[2], (2, D), jnp.float32), 0.25, 1.75)
    ln1_bias = centred(arg_keys[3], (2, D), 0.5, 3.0, ((0, 2), (1, 16)), jnp.float32)
    qkv_weight = centred(arg_keys[4], (2, D, HEADS, 3 * HEAD_DIM), D ** -0.5, 0.1875, ((0, 2), (2, 16)))
    qv_bias = centred(arg_keys[5], (2, HEADS, 2 * HEAD_DIM), 0.5, 3.0, ((0, 2), (1, 16)), jnp.float32)
    output_projection_weight = centred(arg_keys[6], (2, HEADS, HEAD_DIM, D), HEAD_DIM ** -0.5, 0.75, ((0, 2), (1, 16)))
    out_bias = centred(arg_keys[7], (2, D), 0.5, 3.0, ((0, 2), (1, 16)), jnp.float32)
    ln2_gain = jnp.clip(1.0 + 0.15 * jax.random.normal(arg_keys[8], (2, D), jnp.float32), 0.25, 1.75)
    ln2_bias = centred(arg_keys[9], (2, D), 0.5, 3.0, ((0, 2), (1, 16)), jnp.float32)
    expand_weight = centred(arg_keys[10], (2, D, FF), D ** -0.5, 0.1875, ((0, 2), (2, 16)))
    up_bias = centred(arg_keys[11], (2, FF), 0.5, 3.0, ((0, 2), (1, 16)), jnp.float32)
    down_weight = centred(arg_keys[12], (2, FF, D), FF ** -0.5, 0.09375, ((0, 2), (1, 16)))
    down_bias = centred(arg_keys[13], (2, D), 0.5, 3.0, ((0, 2), (1, 16)), jnp.float32)
    return dict(images=images, cotangent=cotangent, ln1_gain=ln1_gain, ln1_bias=ln1_bias, qkv_weight=qkv_weight, qv_bias=qv_bias, output_projection_weight=output_projection_weight, out_bias=out_bias, ln2_gain=ln2_gain, ln2_bias=ln2_bias, expand_weight=expand_weight, up_bias=up_bias, down_weight=down_weight, down_bias=down_bias)


epsilon = 1e-06
highest = lax.Precision.HIGHEST

@jax.custom_vjp
def low(v):
    return lax.optimization_barrier(v.astype(jnp.bfloat16)).astype(jnp.float32)

@jax.custom_vjp
def low_back(v):
    return v

def low_keep(v):
    return (low(v), None)

def low_pass(kept, grad):
    return (grad,)

def back_keep(v):
    return (v, None)

def back_low(kept, grad):
    return (low(grad),)
low.defvjp(low_keep, low_pass)
low_back.defvjp(back_keep, back_low)

def round_pair_values(value):
    return low_back(low(value))

def layer_norm(values, gain_term, bias_term):
    center = lax.optimization_barrier(jnp.mean(values, -1, keepdims=True))
    spread = lax.optimization_barrier(jnp.mean(values * values, -1, keepdims=True)) - center * center
    return (values - center) * lax.rsqrt(spread + epsilon) * gain_term + bias_term

def attend(triple):
    query_part, key_part, value_part = triple
    scores = low_back(jnp.einsum('qhe,khe->hqk', query_part, key_part, precision=highest) * HEAD_DIM ** (-0.5))
    soft_weights = low(jax.nn.softmax(scores, axis=-1))
    return jnp.einsum('hqk,khe->qhe', soft_weights, value_part, precision=highest)

def layer(layer_in, gain_one, bias_one, qkv_weight, qv_bias, output_projection_weight, out_bias, gain_two, bias_two, expand_weight, up_bias, down_weight, down_bias):
    head_width = HEAD_DIM
    count, tokens_n = (layer_in.shape[0], layer_in.shape[1])
    normalized_input = low(layer_norm(layer_in, gain_one, bias_one))
    mixed_all = jnp.einsum('ntd,dhc->nthc', normalized_input, qkv_weight, precision=highest)
    query_part = round_pair_values(mixed_all[..., :head_width] + qv_bias[:, :head_width])
    key_part = round_pair_values(mixed_all[..., head_width:2 * head_width])
    value_part = round_pair_values(mixed_all[..., 2 * head_width:] + qv_bias[:, head_width:])
    attention_result = round_pair_values(lax.map(jax.checkpoint(attend), (query_part, key_part, value_part)))
    branch = low_back(jnp.einsum('nqhe,hed->nqd', attention_result, output_projection_weight, precision=highest))
    hidden = layer_in + branch + out_bias
    second = low(layer_norm(hidden, gain_two, bias_two))
    upward = low_back(jnp.einsum('ntd,df->ntf', second, expand_weight, precision=highest) + up_bias)
    active = low(jax.nn.gelu(upward, approximate=False))
    mlp_out = low_back(jnp.einsum('ntf,fd->ntd', active, down_weight, precision=highest))
    return hidden + mlp_out + down_bias

def reference(images, cotangent, ln1_gain, ln1_bias, qkv_weight, qv_bias, output_projection_weight, out_bias, ln2_gain, ln2_bias, expand_weight, up_bias, down_weight, down_bias):
    count = MICRO * IMGS
    start_in = images.astype(jnp.float32).reshape(count, IMG_TOK, D)
    grad_in = cotangent.astype(jnp.float32).reshape(count, IMG_TOK, D)
    params = (ln1_gain, ln1_bias, qkv_weight, qv_bias, output_projection_weight, out_bias, ln2_gain, ln2_bias, expand_weight, up_bias, down_weight, down_bias)
    first_layer = tuple((item[0].astype(jnp.float32) for item in params))
    second_layer = tuple((item[1].astype(jnp.float32) for item in params))
    probe_zero = jnp.zeros_like(start_in)

    def stacked(layer_in, probe, first_w, second_w):
        middle = low_back(low(layer(layer_in, *first_w)))
        final = layer(middle + probe, *second_w)
        return (middle, final)
    (middle, final), pullback = jax.vjp(stacked, start_in, probe_zero, first_layer, second_layer)
    grad_x, grad_probe, grads_first, grads_second = pullback((jnp.zeros_like(middle), grad_in))
    shape_out = (2, MICRO, IMGS, IMG_TOK, D)
    activations = jnp.stack([middle, final]).astype(jnp.bfloat16).reshape(shape_out)
    input_grads = jnp.stack([grad_x, grad_probe]).astype(jnp.bfloat16).reshape(shape_out)
    joined = tuple((jnp.stack([first_g, second_g]) for first_g, second_g in zip(grads_first, grads_second)))
    return (activations, input_grads, joined[0], joined[1], joined[2], joined[3], joined[4], joined[5], joined[6], joined[7], joined[8], joined[9], joined[10], joined[11])
```

```python
from functools import partial

import jax
import jax.numpy as jnp
from jax import lax
from jax.sharding import PartitionSpec as P

D = 1024
HEAD_DIM = 64


epsilon = 1e-06


def from_everyone(x, axis):
    copies = jnp.broadcast_to(x, (lax.axis_size(axis), *x.shape))
    return lax.all_to_all(copies, axis, split_axis=0, concat_axis=0, tiled=True)


def of_everyone(x, axis):
    return from_everyone(x, axis).sum(axis=0)


def in_one(arrays, axis):
    ends = [0]
    for a in arrays:
        ends.append(ends[-1] + a.size)
    running = of_everyone(jnp.concatenate([a.ravel() for a in arrays]), axis)
    return tuple((running[b:e].reshape(a.shape) for a, b, e in zip(arrays, ends, ends[1:])))


def joined_along(pieces, dim):
    lengths = list(pieces.shape[1:])
    lengths[dim] *= pieces.shape[0]
    return jnp.moveaxis(pieces, 0, dim).reshape(lengths)


def gathered_copies(x, axis, dim):
    return joined_along(from_everyone(x, axis), dim)


def split_up(x, dim, peers):
    before, after = (x.shape[:dim], x.shape[dim + 1 :])
    return jnp.moveaxis(x.reshape(*before, peers, -1, *after), dim, 0)


def sum_at_owner(x, axis, dim):
    pieces = split_up(x, dim, lax.axis_size(axis))
    arrived = lax.all_to_all(pieces, axis, split_axis=0, concat_axis=0, tiled=True)
    return arrived.astype(jnp.float32).sum(axis=0)


def shifted(x, axis, by):
    peers = lax.axis_size(axis)
    pairs = [(i, i + by) for i in range(peers) if 0 <= i + by < peers]
    return lax.ppermute(x, axis, pairs)


def row_totals(first_sum, second_sum):
    return in_one((first_sum, second_sum), "tensor")


def full_rows(normalized_input):
    return gathered_copies(normalized_input, "tensor", 2)


def feature_sum(partial_rows):
    return sum_at_owner(partial_rows.astype(jnp.bfloat16), "tensor", 2)


def grad_gather(grad_part):
    return gathered_copies(grad_part, "tensor", 2)


def grad_feature_sum(partial_rows):
    return sum_at_owner(partial_rows.astype(jnp.bfloat16), "tensor", 2)


def norm_forward(values, gain_term, bias_term):
    total_one, total_two = row_totals(jnp.sum(values, -1), jnp.sum(values * values, -1))
    center = total_one / D
    spread = total_two / D - center * center
    inv_std = lax.rsqrt(spread + epsilon)
    scaled_x = (values - center[..., None]) * inv_std[..., None]
    return ((scaled_x * gain_term + bias_term).astype(jnp.bfloat16), scaled_x, inv_std)


def norm_backward(grad_norm, scaled_x, inv_std, gain_term):
    gain_grad = jnp.sum(grad_norm * scaled_x, axis=(0, 1))
    bias_grad = jnp.sum(grad_norm, axis=(0, 1))
    weighted = grad_norm * gain_term
    total_one, total_two = row_totals(jnp.sum(weighted, -1), jnp.sum(weighted * scaled_x, -1))
    grad_input = inv_std[..., None] * (
        weighted - total_one[..., None] / D - scaled_x * total_two[..., None] / D
    )
    return (grad_input, gain_grad, bias_grad)


def attention_scores(query_part, kv_image):
    head_width = query_part.shape[-1]
    raw_scores = jnp.einsum(
        "bqhe,bkhe->bhqk",
        query_part,
        kv_image[..., :head_width],
        preferred_element_type=jnp.float32,
    )
    return raw_scores * head_width ** (-0.5)


def layer_forward(layer_in, weights):
    (
        gain_one,
        bias_one,
        qkv_weight,
        qv_bias,
        output_projection_weight,
        out_bias,
        gain_two,
        bias_two,
        expand_weight,
        up_bias,
        down_weight,
        down_bias,
    ) = weights
    head_width = HEAD_DIM
    values_in = layer_in.astype(jnp.float32)
    normed_one, scaled_one, inv_one = norm_forward(values_in, gain_one, bias_one)
    rows_one = full_rows(normed_one)
    mixed_all = jnp.einsum(
        "brd,dhc->brhc", rows_one, qkv_weight, preferred_element_type=jnp.float32
    )
    query_part = (mixed_all[..., :head_width] + qv_bias[:, :head_width]).astype(jnp.bfloat16)
    kv_local = jnp.concatenate(
        [
            mixed_all[..., head_width : 2 * head_width],
            mixed_all[..., 2 * head_width :] + qv_bias[:, head_width:],
        ],
        -1,
    ).astype(jnp.bfloat16)
    kv_image = gathered_copies(kv_local, "dp", 1)
    scores = attention_scores(query_part, kv_image)
    top_score = jnp.max(scores, -1, keepdims=True)
    log_total = top_score + jnp.log(jnp.sum(jnp.exp(scores - top_score), -1, keepdims=True))
    soft_weights = jnp.exp(scores - log_total).astype(jnp.bfloat16)
    attention_result = jnp.einsum(
        "bhqk,bkhe->bqhe",
        soft_weights,
        kv_image[..., head_width:],
        preferred_element_type=jnp.float32,
    ).astype(jnp.bfloat16)
    branch_part = jnp.einsum(
        "kygo,goj->kyj",
        attention_result,
        output_projection_weight,
        preferred_element_type=jnp.float32,
    )
    hidden = values_in + feature_sum(branch_part) + out_bias
    normed_two, scaled_two, inv_two = norm_forward(hidden, gain_two, bias_two)
    rows_two = full_rows(normed_two)
    upward = (
        jnp.einsum("brd,df->brf", rows_two, expand_weight, preferred_element_type=jnp.float32)
        + up_bias
    )
    active = jax.nn.gelu(upward, approximate=False).astype(jnp.bfloat16)
    feedforward_share = jnp.einsum(
        "brf,fd->brd", active, down_weight, preferred_element_type=jnp.float32
    )
    layer_out = hidden + feature_sum(feedforward_share) + down_bias
    stash = (
        scaled_one,
        inv_one,
        rows_one,
        query_part,
        kv_image,
        log_total,
        attention_result,
        scaled_two,
        inv_two,
        rows_two,
        upward,
        active,
    )
    return (layer_out.astype(jnp.bfloat16), stash)


def layer_backward(grad_in, stash, weights):
    (
        gain_one,
        bias_one,
        qkv_weight,
        qv_bias,
        output_projection_weight,
        out_bias,
        gain_two,
        bias_two,
        expand_weight,
        up_bias,
        down_weight,
        down_bias,
    ) = weights
    (
        scaled_one,
        inv_one,
        rows_one,
        query_part,
        kv_image,
        log_total,
        attention_result,
        scaled_two,
        inv_two,
        rows_two,
        upward,
        active,
    ) = stash
    head_width = HEAD_DIM
    scale_factor = head_width ** (-0.5)
    grad_out = grad_in.astype(jnp.float32)
    down_bias_grad = jnp.sum(grad_out, axis=(0, 1))
    grad_full = grad_gather(grad_in)
    grad_active = jnp.einsum(
        "brd,fd->brf", grad_full, down_weight, preferred_element_type=jnp.float32
    )
    down_grad = jnp.einsum("brf,brd->fd", active, grad_full, preferred_element_type=jnp.float32)
    gelu_pull = jax.vjp(partial(jax.nn.gelu, approximate=False), upward)[1]
    grad_upward = gelu_pull(grad_active)[0].astype(jnp.bfloat16)
    up_bias_grad = jnp.sum(grad_upward.astype(jnp.float32), axis=(0, 1))
    up_grad = jnp.einsum("brd,brf->df", rows_two, grad_upward, preferred_element_type=jnp.float32)
    grad_normed_two = grad_feature_sum(
        jnp.einsum("brf,df->brd", grad_upward, expand_weight, preferred_element_type=jnp.float32)
    )
    grad_from_two, gain_two_grad, bias_two_grad = norm_backward(
        grad_normed_two, scaled_two, inv_two, gain_two
    )
    grad_hidden = grad_out + grad_from_two
    out_bias_grad = jnp.sum(grad_hidden, axis=(0, 1))
    hidden_token_rows = grad_gather(grad_hidden.astype(jnp.bfloat16))
    grad_attended = jnp.einsum(
        "xap,glp->xagl",
        hidden_token_rows,
        output_projection_weight,
        preferred_element_type=jnp.float32,
    ).astype(jnp.bfloat16)
    out_grad = jnp.einsum(
        "ysrp,ysz->rpz", attention_result, hidden_token_rows, preferred_element_type=jnp.float32
    )
    scores = attention_scores(query_part, kv_image)
    soft_full = jnp.exp(scores - log_total)
    soft_low = soft_full.astype(jnp.bfloat16)
    grad_soft = jnp.einsum(
        "bqhe,bkhe->bhqk",
        grad_attended,
        kv_image[..., head_width:],
        preferred_element_type=jnp.float32,
    )
    row_dot = jnp.sum(soft_full * grad_soft, -1, keepdims=True)
    grad_scores = (soft_full * (grad_soft - row_dot)).astype(jnp.bfloat16)
    grad_query = (
        jnp.einsum(
            "bhqk,bkhe->bqhe",
            grad_scores,
            kv_image[..., :head_width],
            preferred_element_type=jnp.float32,
        )
        * scale_factor
    ).astype(jnp.bfloat16)
    grad_keys = (
        jnp.einsum("bhqk,bqhe->bkhe", grad_scores, query_part, preferred_element_type=jnp.float32)
        * scale_factor
    )
    grad_values = jnp.einsum(
        "bhqk,bqhe->bkhe", soft_low, grad_attended, preferred_element_type=jnp.float32
    )
    key_value_gradient = sum_at_owner(
        jnp.concatenate([grad_keys, grad_values], -1).astype(jnp.bfloat16), "dp", 1
    ).astype(jnp.bfloat16)
    grad_mixed = jnp.concatenate([grad_query, key_value_gradient], -1)
    qv_bias_grad = jnp.concatenate(
        [
            jnp.sum(grad_query.astype(jnp.float32), axis=(0, 1)),
            jnp.sum(key_value_gradient[..., head_width:].astype(jnp.float32), axis=(0, 1)),
        ],
        -1,
    )
    qkv_grad = jnp.einsum("brd,brhc->dhc", rows_one, grad_mixed, preferred_element_type=jnp.float32)
    grad_normed_one = grad_feature_sum(
        jnp.einsum("brhc,dhc->brd", grad_mixed, qkv_weight, preferred_element_type=jnp.float32)
    )
    grad_from_one, gain_one_grad, bias_one_grad = norm_backward(
        grad_normed_one, scaled_one, inv_one, gain_one
    )
    grad_layer_in = grad_hidden + grad_from_one
    grads = (
        gain_one_grad,
        bias_one_grad,
        qkv_grad,
        qv_bias_grad,
        out_grad,
        out_bias_grad,
        gain_two_grad,
        bias_two_grad,
        up_grad,
        up_bias_grad,
        down_grad,
        down_bias_grad,
    )
    return (grad_layer_in.astype(jnp.bfloat16), grads)


def reduce_end(grads):
    (
        grad_ga,
        grad_ba,
        grad_qkv,
        grad_qvb,
        grad_out,
        grad_outb,
        grad_gb,
        grad_bb,
        grad_up,
        grad_upb,
        grad_down,
        grad_downb,
    ) = grads
    return (
        sum_at_owner(grad_ga.astype(jnp.bfloat16), "dp", 0),
        sum_at_owner(grad_ba.astype(jnp.bfloat16), "dp", 0),
        sum_at_owner(grad_qkv.astype(jnp.bfloat16), "dp", 0),
        sum_at_owner(grad_qvb.astype(jnp.bfloat16), "dp", 1),
        sum_at_owner(grad_out.astype(jnp.bfloat16), "dp", 2),
        sum_at_owner(grad_outb.astype(jnp.bfloat16), "dp", 0),
        sum_at_owner(grad_gb.astype(jnp.bfloat16), "dp", 0),
        sum_at_owner(grad_bb.astype(jnp.bfloat16), "dp", 0),
        sum_at_owner(grad_up.astype(jnp.bfloat16), "dp", 0),
        sum_at_owner(grad_upb.astype(jnp.bfloat16), "dp", 0),
        sum_at_owner(grad_down.astype(jnp.bfloat16), "dp", 1),
        sum_at_owner(grad_downb.astype(jnp.bfloat16), "dp", 0),
    )


def body(
    images,
    cotangent,
    ln1_gain,
    ln1_bias,
    qkv_weight,
    qv_bias,
    output_projection_weight,
    out_bias,
    ln2_gain,
    ln2_bias,
    expand_weight,
    up_bias,
    down_weight,
    down_bias,
):
    weights = tuple(
        (
            item[0]
            for item in (
                ln1_gain,
                ln1_bias,
                qkv_weight,
                qv_bias,
                output_projection_weight,
                out_bias,
                ln2_gain,
                ln2_bias,
                expand_weight,
                up_bias,
                down_weight,
                down_bias,
            )
        )
    )
    section = lax.axis_index("section")
    micro = images.shape[0]
    first_in = images.reshape(micro, *images.shape[2:])
    last_grad = cotangent.reshape(micro, *cotangent.shape[2:])
    early_out, early_stash = layer_forward(first_in, weights)
    received = shifted(early_out, "section", 1)
    late_out, late_stash = layer_forward(received, weights)
    own = section == 0
    activations = jnp.where(own, early_out, late_out).reshape(images.shape)[None]
    stash = jax.tree.map(lambda e, l: jnp.where(own, e, l), early_stash, late_stash)
    early_grad, early_totals = layer_backward(last_grad, stash, weights)
    returned = shifted(early_grad, "section", -1)
    late_grad, late_totals = layer_backward(returned, stash, weights)
    input_grads = jnp.where(own, late_grad, early_grad).reshape(images.shape)[None]
    totals = tuple((jnp.where(own, l, e) for e, l in zip(early_totals, late_totals)))
    totals = reduce_end(totals)
    shards = tuple((item[None] for item in totals))
    return (
        activations,
        input_grads,
        shards[0],
        shards[1],
        shards[2],
        shards[3],
        shards[4],
        shards[5],
        shards[6],
        shards[7],
        shards[8],
        shards[9],
        shards[10],
        shards[11],
    )


def solution(mesh):
    in_specs = (
        P(None, None, "dp", "tensor"),
        P(None, None, "dp", "tensor"),
        P("section", "tensor"),
        P("section", "tensor"),
        P("section", None, "tensor", None),
        P("section", "tensor", None),
        P("section", "tensor", None, None),
        P("section", "tensor"),
        P("section", "tensor"),
        P("section", "tensor"),
        P("section", None, "tensor"),
        P("section", "tensor"),
        P("section", "tensor", None),
        P("section", "tensor"),
    )
    out_specs = (
        P("section", None, None, "dp", "tensor"),
        P("section", None, None, "dp", "tensor"),
        P("section", ("tensor", "dp")),
        P("section", ("tensor", "dp")),
        P("section", "dp", "tensor", None),
        P("section", "tensor", "dp"),
        P("section", "tensor", None, "dp"),
        P("section", ("tensor", "dp")),
        P("section", ("tensor", "dp")),
        P("section", ("tensor", "dp")),
        P("section", "dp", "tensor"),
        P("section", ("tensor", "dp")),
        P("section", "tensor", "dp"),
        P("section", ("tensor", "dp")),
    )
    return jax.shard_map(body, mesh=mesh, in_specs=in_specs, out_specs=out_specs, check_vma=False)
```

```python
import jax
import jax.numpy as jnp
from jax import lax
from jax.experimental import pallas as pl
from jax.experimental.pallas import tpu as pltpu
from jax.sharding import PartitionSpec as P

BF = jnp.bfloat16
F32 = jnp.float32
D = 1024
TOK = 576
CHUNK = 144
epsilon = 1e-06

INPUTS = (
    "images",
    "cot",
    "g1",
    "b1",
    "wqkv",
    "qvb",
    "wo",
    "outb",
    "g2",
    "b2",
    "wup",
    "upb",
    "wdn",
    "downb",
)
OUTPUTS = ("o_act", "o_ig", "o_sums", "o_qkv", "o_wo", "o_up", "o_dn")


def vm(*shape, dtype=BF):
    return pltpu.VMEM(shape, dtype)


def dma(*shape):
    return pltpu.SemaphoreType.DMA(shape)


SCRATCH = dict(
    FB=vm(4, 80, 128),
    GX=vm(16, 4, 80, 128),
    BUF=vm(2, TOK, D),
    VB=vm(8, 128, dtype=F32),
    VG=vm(16, 8, 128, dtype=F32),
    VA=vm(8, D, dtype=F32),
    WO=vm(D, D),
    A1=vm(TOK, D),
    Q=vm(TOK, 64),
    K=vm(TOK, 64),
    V=vm(TOK, 64),
    PR=vm(TOK, TOK, dtype=F32),
    PH=vm(TOK, TOK),
    DS=vm(TOK, TOK),
    O=vm(TOK, 64),
    GO=vm(16, 4, 80, 128),
    GA=vm(16, 4, 80, 128),
    OA=vm(TOK, D),
    HIDQ=vm(CHUNK, D, dtype=F32),
    WUQ=vm(4, D, 256),
    WDQ=vm(4, 256, D),
    UBQ=vm(4, 1, 256, dtype=F32),
    GPQ=vm(4, CHUNK, 256, dtype=F32),
    ZQ=vm(4, CHUNK, 256),
    PQ=vm(2, CHUNK, D),
    RQ=vm(2, 4, 48, D),
    A2=vm(TOK, D),
    GP=vm(TOK, 256, dtype=F32),
    Z=vm(TOK, 256),
    DU=vm(TOK, 256),
    YR=vm(48, D),
    P0=vm(TOK, D),
    P2=vm(TOK, D),
    SB=vm(2, 8, 48, D),
    PB=vm(2, 8, 48, D),
    RB=vm(2, 8, 48, D),
    DHID=vm(48, D, dtype=F32),
    DHR=vm(48, D),
    DOR=vm(48, D),
    DB=vm(TOK, 128),
    DO=vm(TOK, 64),
    DHF=vm(TOK, D),
    DQKV=vm(TOK, 192),
    IGR=vm(48, D),
    WU=vm(D, 256),
    WD=vm(256, D),
    WQ=vm(192, D),
    WG=vm(64, D),
    WUR=vm(4, 256, 256),
    WDR=vm(4, 256, 256),
    WQR=vm(4, 192, 256),
    WGR=vm(4, 64, 256),
    EA=vm(4, CHUNK, 128),
    EI=vm(4, CHUNK, 128),
    VS=vm(8, D, dtype=F32),
    VR=vm(16, 8, 128, dtype=F32),
    FV=vm(8, 256, dtype=F32),
    FR=vm(4, 8, 256, dtype=F32),
    m_z=dma(2, 4),
    m_x=dma(4, 8),
    m_v=dma(2, 16),
    m_wo=dma(4, 8),
    m_o=dma(2, 16),
    m_ga=dma(4, 8),
    m_go=dma(4, 8),
    m_wq=dma(4, 4),
    m_q0=dma(2, 4),
    m_q1=dma(2, 4),
    m_r0=dma(4, 8),
    m_r2=dma(4, 8),
    m_y=dma(4, 8),
    m_g=dma(4, 8),
    m_do=dma(2, 16),
    m_dh=dma(4, 8),
    m_ea=dma(2, 16),
    m_ei=dma(2, 16),
    m_vs=dma(2, 16),
    m_w=dma(8, 4),
    m_f=dma(2, 4),
)


def nn(a, b):
    return lax.dot_general(a, b, (((1,), (0,)), ((), ())), preferred_element_type=F32)


def nt(a, b):
    return lax.dot_general(a, b, (((1,), (1,)), ((), ())), preferred_element_type=F32)


def tn(a, b):
    return lax.dot_general(a, b, (((0,), (0,)), ((), ())), preferred_element_type=F32)


def loop(low, high, f):
    pl.loop(low, high)(f)


def row_of(j):
    return pl.multiple_of(144 * lax.div(j, 4) + 32 * lax.rem(j, 4), 16)


def lane_of(j):
    return pl.multiple_of(128 * lax.div(j, 2), 128)


def sized(j, f):
    big = lax.rem(j, 4) == 3
    pl.when(big)(lambda: f(48))
    pl.when(jnp.logical_not(big))(lambda: f(32))


def whole(j, f):
    f(None)


def norm(v):
    mu = jnp.mean(v, -1, keepdims=True)
    var = jnp.mean(v * v, -1, keepdims=True) - mu * mu
    rstd = lax.rsqrt(var + epsilon)
    return (v - mu) * rstd, rstd


def norm_back(g, xhat, rstd, gain):
    w = g * gain
    return rstd * (
        w - jnp.mean(w, -1, keepdims=True) - xhat * jnp.mean(w * xhat, -1, keepdims=True)
    )


class Refs:
    pass


def kernel(*refs):
    R = Refs()
    for name, ref in zip((*INPUTS, *OUTPUTS, *SCRATCH), refs):
        setattr(R, name, ref)
    s = lax.axis_index("section")
    t = lax.axis_index("tensor")
    z = lax.axis_index("dp")
    k = lax.div(t, 2)
    c = lax.rem(t, 2)
    zq = lax.div(t, 4)
    p = lax.rem(t, 4)
    me_row = row_of(t)
    drains = []

    def rc(src, dst, ss, rs, s2, t2, z2):
        return pltpu.make_async_remote_copy(
            src_ref=src,
            dst_ref=dst,
            send_sem=ss,
            recv_sem=rs,
            device_id={"section": s2, "tensor": t2, "dp": z2},
            device_id_type=pl.DeviceIdType.MESH,
        )

    def arrived(dst, rs):
        rc(dst, dst, rs, rs, s, 2 * k + 1 - c, z).wait_recv()

    def left(src, ss):
        rc(src, src, ss, ss, s, 2 * k + 1 - c, z).wait_send()

    def peers(f):
        def far(d):
            f(d, 8 * (1 - lax.div(t, 8)) + lax.rem(t + d, 8))

        def near(d):
            f(8 + d, 8 * lax.div(t, 8) + lax.rem(t + d, 8))

        loop(0, 8, far)
        loop(1, 8, near)

    def far_chips(f):
        loop(0, 4, lambda d: f(4 * (1 - lax.div(k, 4)) + lax.rem(k + d, 4)))

    def near_chips(f):
        loop(1, 4, lambda d: f(4 * lax.div(k, 4) + lax.rem(k + d, 4)))

    def other_chips(f):
        far_chips(f)
        near_chips(f)

    def chips_by_arrival(f):
        near_chips(f)
        far_chips(f)

    def all_chips(f):
        loop(0, 8, f)

    def quad_chips(f):
        loop(0, 2, lambda d: f(2 * zq + d))

    def rest_chips(f):
        loop(2, 8, lambda d: f(lax.rem(2 * zq + d, 8)))

    def gather_start(src, dst, size, m, s2, chips):
        def go(k2):
            size(t, lambda n: rc(src(n), dst(t, n), m.at[0, k2], m.at[1, k], s2, 2 * k2 + c, z).start())

        chips(go)

    def gather_drain(src, size, m, chips):
        chips(lambda k2: size(t, lambda n: left(src(n), m.at[0, k2])))

    def forward_own(dst, m):
        here = dst(t, None)
        rc(here, here, m.at[2, k], m.at[3, k], s, 2 * k + 1 - c, z).start()

    def gather_forward(dst, size, m, chips):
        def go(k2):
            j = 2 * k2 + c

            def send(n):
                here = dst(j, n)
                arrived(here, m.at[1, k2])
                rc(here, here, m.at[2, k2], m.at[3, k2], s, 2 * k + 1 - c, z).start()

            size(j, send)

        chips(go)

    def gather_finish(dst, size, m, chips):
        def go(k2):
            j = 2 * k2 + 1 - c
            size(j, lambda n: arrived(dst(j, n), m.at[3, k2]))

        chips(go)

    def gather_forward_drain(dst, size, m):
        def go(k2):
            j = 2 * k2 + c
            size(j, lambda n: left(dst(j, n), m.at[2, k2]))

        loop(0, 8, go)

    def quad_start(i, m):
        def go(d):
            p2 = lax.rem(p + d, 4)
            t2 = 4 * zq + p2
            sized(
                t2,
                lambda n: rc(
                    R.PQ.at[i, pl.ds(pl.multiple_of(32 * p2, 16), n)],
                    R.RQ.at[i, p, pl.ds(0, n)],
                    m.at[0, p2],
                    m.at[1, p],
                    s,
                    t2,
                    z,
                ).start(),
            )

        loop(1, 4, go)
        R.RQ[i, p] = R.PQ[i, pl.ds(pl.multiple_of(32 * p, 16), 48), :]

    def quad_finish(i, m):
        def go(d):
            p2 = lax.rem(p + d, 4)
            sized(t, lambda n: arrived(R.RQ.at[i, p2, pl.ds(0, n)], m.at[1, p2]))

        loop(1, 4, go)
        total = R.RQ[i, 0].astype(F32)
        for p2 in range(1, 4):
            total = total + R.RQ[i, p2].astype(F32)
        return total

    def quad_drain(i, m):
        def go(d):
            p2 = lax.rem(p + d, 4)
            sized(4 * zq + p2, lambda n: left(R.PQ.at[i, pl.ds(0, n)], m.at[0, p2]))

        loop(1, 4, go)

    def reduce_start(part, i, m):
        def go(k2):
            j = 2 * k2 + 1 - c
            sized(
                j,
                lambda n: rc(
                    part.at[pl.ds(row_of(j), n)],
                    R.SB.at[i, k2, pl.ds(0, n)],
                    m.at[0, k2],
                    m.at[1, k2],
                    s,
                    2 * k + 1 - c,
                    z,
                ).start(),
            )

        other_chips(go)
        go(k)

        def mid(k2):
            j = 2 * k2 + c
            sized(j, lambda n: arrived(R.SB.at[i, k2, pl.ds(0, n)], m.at[1, k2]))
            both = part[pl.ds(row_of(j), 48), :].astype(F32) + R.SB[i, k2].astype(F32)
            R.PB[i, k2] = both.astype(BF)
            sized(
                j,
                lambda n: rc(
                    R.PB.at[i, k2, pl.ds(0, n)],
                    R.RB.at[i, k, pl.ds(0, n)],
                    m.at[2, k2],
                    m.at[3, k],
                    s,
                    j,
                    z,
                ).start(),
            )

        other_chips(mid)
        sized(t, lambda n: arrived(R.SB.at[i, k, pl.ds(0, n)], m.at[1, k]))
        both = part[pl.ds(me_row, 48), :].astype(F32) + R.SB[i, k].astype(F32)
        R.RB[i, k] = both.astype(BF)

    def reduce_finish(i, m):
        def go(d):
            k2 = lax.rem(k + d, 8)
            sized(t, lambda n: arrived(R.RB.at[i, k2, pl.ds(0, n)], m.at[3, k2]))

        loop(1, 8, go)
        total = R.RB[i, 0].astype(F32)
        for k2 in range(1, 8):
            total = total + R.RB[i, k2].astype(F32)
        return total

    def reduce_drain(part, i, m):
        def first(k2):
            j = 2 * k2 + 1 - c
            sized(j, lambda n: left(part.at[pl.ds(row_of(j), n)], m.at[0, k2]))

        loop(0, 8, first)

        def second(d):
            k2 = lax.rem(k + d, 8)
            sized(2 * k2 + c, lambda n: left(R.PB.at[i, k2, pl.ds(0, n)], m.at[2, k2]))

        loop(1, 8, second)

    def emit(rows, E, m):
        def go(d, t2):
            def send(n):
                rc(
                    rows.at[pl.ds(0, n), pl.ds(lane_of(t2), 128)],
                    E.at[z, pl.ds(pl.multiple_of(32 * p, 16), n)],
                    m.at[0, d],
                    m.at[1, 4 * z + p],
                    s,
                    t2,
                    zq,
                ).start()

            sized(t, send)

        peers(go)
        pl.when(zq != z)(lambda: go(8, t))

        def local():
            def put(n):
                E[z, pl.ds(pl.multiple_of(32 * lax.rem(t, 4), 16), n), :] = rows[
                    pl.ds(0, n), pl.ds(lane_of(t), 128)
                ]

            sized(t, put)

        pl.when(zq == z)(local)

    def emit_drain(rows, m):
        def go(d, t2):
            sized(t, lambda n: left(rows.at[pl.ds(0, n), pl.ds(0, 128)], m.at[0, d]))

        peers(go)
        pl.when(zq != z)(lambda: go(8, t))

    def emit_finish(E, m, out):
        def go(i):
            z2 = lax.div(i, 4)
            t2 = 4 * z + lax.rem(i, 4)
            mine = jnp.logical_and(t2 == t, z2 == z)
            there = pl.multiple_of(32 * lax.rem(i, 4), 16)
            pl.when(jnp.logical_not(mine))(
                lambda: sized(t2, lambda n: arrived(E.at[z2, pl.ds(there, n)], m.at[1, i]))
            )

        loop(0, 16, go)

        @pl.when(c == 0)
        def _():
            for i in range(4):
                out[i] = E[i, :, 0:64].T

        @pl.when(c == 1)
        def _():
            for i in range(4):
                out[i] = E[i, :, 64:128].T

    bar = pltpu.get_barrier_semaphore()

    def greet(s2, t2, z2):
        pl.semaphore_signal(
            bar,
            inc=1,
            device_id={"section": s2, "tensor": t2, "dp": z2},
            device_id_type=pl.DeviceIdType.MESH,
        )

    loop(1, 16, lambda d: greet(s, lax.rem(t + d, 16), z))
    loop(1, 4, lambda d: greet(s, t, lax.rem(z + d, 4)))
    loop(0, 8, lambda d: greet(1 - s, 2 * d + c, z))

    def out_to(d):
        pl.when(jnp.logical_not(jnp.logical_and(d == t, zq == z)))(lambda: greet(s, d, zq))

    def out_from(d):
        t2 = 4 * z + lax.rem(d, 4)
        z2 = lax.div(d, 4)
        pl.when(jnp.logical_not(jnp.logical_and(t2 == t, z2 == z)))(lambda: greet(s, t2, z2))

    loop(0, 16, out_to)
    loop(0, 16, out_from)

    def pack(src):
        for m in range(4):
            R.FB[m, 64:80, :] = jnp.zeros((16, 128), BF)
            rows = src[m].T
            R.FB[m, :, 0:64] = rows[0:80, :]
            R.FB[m, 0:64, 64:128] = rows[80:144, :]

    pl.when(s == 0)(lambda: pack(R.images))
    pl.when(s == 1)(lambda: pack(R.cot))
    R.VB[...] = jnp.zeros((8, 128), F32)
    vecs = (R.g1, R.b1, R.g2, R.b2, R.outb, R.downb)

    @pl.when(c == 0)
    def _():
        for i, v in enumerate(vecs):
            R.VB[i : i + 1, 0:64] = v[...]

    @pl.when(c == 1)
    def _():
        for i, v in enumerate(vecs):
            R.VB[i : i + 1, 64:128] = v[...]

    R.VB[6:7, :] = R.upb[:, 0:128]
    R.VB[7:8, :] = R.upb[:, 128:256]
    R.VG[t] = R.VB[...]
    R.GX[t, z] = R.FB[z]
    wo_piece = lambda j, n: R.WO.at[pl.ds(pl.multiple_of(64 * j, 64), 64)]
    R.WO[pl.ds(pl.multiple_of(64 * t, 64), 64), :] = R.wo[...]
    R.WUQ[zq] = R.wup[...]
    R.WDQ[zq] = R.wdn[...]
    R.FV[...] = jnp.zeros((8, 256), F32)
    R.VS[...] = jnp.zeros((8, D), F32)
    for i in range(4):
        R.GO[t, i, 64:80, :] = jnp.zeros((16, 128), BF)

    pl.semaphore_wait(bar, 58 - 2 * (zq == z).astype(jnp.int32))

    def z_send(d):
        z2 = lax.rem(z + d, 4)
        rc(R.FB.at[z2], R.GX.at[t, z], R.m_z.at[0, d], R.m_z.at[1, z], s, t, z2).start()

    loop(1, 4, z_send)

    def z_wait(d):
        z2 = lax.rem(z + d, 4)
        arrived(R.GX.at[t, z2], R.m_z.at[1, z2])

    loop(1, 4, z_wait)
    drains.append(lambda: loop(1, 4, lambda d: left(R.FB.at[0], R.m_z.at[0, d])))
    x_piece = lambda j, n: R.GX.at[j]
    gather_start(lambda n: R.GX.at[t], x_piece, whole, R.m_x, s, other_chips)
    forward_own(x_piece, R.m_x)

    def v_send(d, t2):
        rc(R.VB, R.VG.at[t], R.m_v.at[0, d], R.m_v.at[1, t], s, t2, z).start()

    peers(v_send)
    drains.append(lambda: peers(lambda d, t2: left(R.VB, R.m_v.at[0, d])))
    gather_start(lambda n: wo_piece(t, n), wo_piece, whole, R.m_wo, s, other_chips)
    gather_forward(x_piece, whole, R.m_x, chips_by_arrival)
    gather_finish(x_piece, whole, R.m_x, all_chips)
    peers(lambda d, t2: arrived(R.VG.at[t2], R.m_v.at[1, t2]))
    for kk in range(8):
        R.VA[:, 128 * kk : 128 * kk + 128] = R.VG[2 * kk] + R.VG[2 * kk + 1]
    for g in range(4):
        R.UBQ[g, :, 0:128] = R.VG[4 * g + p, 6:7, :]
        R.UBQ[g, :, 128:256] = R.VG[4 * g + p, 7:8, :]
    gain1, bias1 = R.VA[0:1, :], R.VA[1:2, :]
    gain2, bias2 = R.VA[2:3, :], R.VA[3:4, :]
    out_bias, down_bias = R.VA[4:5, :], R.VA[5:6, :]

    def unpack(G, q, put):
        row = pl.multiple_of(144 * q, 16)
        for kk in range(8):
            a, b = G[2 * kk, q], G[2 * kk + 1, q]
            lanes = slice(128 * kk, 128 * kk + 128)
            put(pl.ds(row, 80), lanes, jnp.concatenate([a[:, :64], b[:, :64]], axis=1))
            put(
                pl.ds(row + 80, 64),
                lanes,
                jnp.concatenate([a[:64, 64:], b[:64, 64:]], axis=1),
            )

    def put_first(rows, lanes, v):
        R.BUF[s, rows, lanes] = v

    loop(0, 4, lambda q: unpack(R.GX, q, put_first))
    drains.append(lambda: gather_drain(lambda n: R.GX.at[t], whole, R.m_x, other_chips))
    drains.append(lambda: gather_forward_drain(x_piece, whole, R.m_x))

    def quad_weights():
        def go(d):
            g2 = lax.rem(zq + d, 4)
            t2 = 4 * g2 + p
            rc(R.wup, R.WUQ.at[zq], R.m_wq.at[0, d], R.m_wq.at[1, zq], s, t2, z).start()
            rc(R.wdn, R.WDQ.at[zq], R.m_wq.at[2, d], R.m_wq.at[3, zq], s, t2, z).start()

        loop(1, 4, go)

    def quad_weights_wait():
        def go(d):
            g2 = lax.rem(zq + d, 4)
            arrived(R.WUQ.at[g2], R.m_wq.at[1, g2])
            arrived(R.WDQ.at[g2], R.m_wq.at[3, g2])

        loop(1, 4, go)

    def quad_weights_drain():
        def go(d):
            left(R.wup, R.m_wq.at[0, d])
            left(R.wdn, R.m_wq.at[2, d])

        loop(1, 4, go)

    y_piece = lambda j, n: R.BUF.at[0, pl.ds(row_of(j), n)]
    g_piece = lambda j, n: R.BUF.at[1, pl.ds(row_of(j), n)]

    @pl.when(s == 1)
    def _():
        quad_weights()
        gather_forward(y_piece, sized, R.m_y, all_chips)
        gather_finish(y_piece, sized, R.m_y, all_chips)

    def rows_at(i):
        return pl.ds(pl.multiple_of(CHUNK * i, 16), CHUNK)

    def project(i):
        rows = rows_at(i)
        xhat, _ = norm(R.BUF[0, rows, :].astype(F32))
        a = (xhat * gain1 + bias1).astype(BF)
        R.A1[rows, :] = a
        mixed = nt(a, R.wqkv[...])
        R.Q[rows, :] = (mixed[:, 0:64] + R.qvb[:, 0:64]).astype(BF)
        R.K[rows, :] = mixed[:, 64:128].astype(BF)
        R.V[rows, :] = (mixed[:, 128:192] + R.qvb[:, 64:128]).astype(BF)

    loop(0, 4, project)

    def attend(i):
        rows = rows_at(i)
        sc = nt(R.Q[rows, :], R.K[...]) * 0.125
        e = jnp.exp(sc - jnp.max(sc, -1, keepdims=True))
        prob = e / jnp.sum(e, -1, keepdims=True)
        R.PR[rows, :] = prob
        ph = prob.astype(BF)
        R.PH[rows, :] = ph
        o = nn(ph, R.V[...]).astype(BF)
        R.O[rows, :] = o
        R.GO[t, i, :, 0:64] = o[0:80, :]
        R.GO[t, i, 0:64, 64:128] = o[80:144, :]

    loop(0, 4, attend)
    o_piece = lambda j, n: R.GO.at[j]
    a_piece = lambda j, n: R.GA.at[j]

    def put_o(rows, lanes, v):
        R.OA[rows, lanes] = v

    def mid_norm(i):
        rows = rows_at(i)
        hidden = R.BUF[0, rows, :].astype(F32) + nn(R.OA[rows, :], R.WO[...]) + out_bias
        xhat, _ = norm(hidden)
        R.A2[rows, :] = (xhat * gain2 + bias2).astype(BF)

        @pl.when(i == zq)
        def _():
            R.HIDQ[...] = hidden

    def wo_forward():
        forward_own(wo_piece, R.m_wo)
        gather_forward(wo_piece, whole, R.m_wo, chips_by_arrival)

    drains.append(lambda: gather_drain(lambda n: wo_piece(t, n), whole, R.m_wo, other_chips))
    drains.append(lambda: gather_forward_drain(wo_piece, whole, R.m_wo))

    def expand(i):
        rows = rows_at(i)
        u = nn(R.A2[rows, :], R.wup[...]) + R.upb[...]
        half = 0.5 * (1.0 + lax.erf(u * 0.7071067811865476))
        R.Z[rows, :] = (u * half).astype(BF)
        R.GP[rows, :] = half + u * (0.3989422804014327 * jnp.exp(-0.5 * u * u))

    def quad_expand(g):
        u = nn(R.A2[rows_at(zq), :], R.WUQ[g]) + R.UBQ[g]
        half = 0.5 * (1.0 + lax.erf(u * 0.7071067811865476))
        R.ZQ[g] = (u * half).astype(BF)
        R.GPQ[g] = half + u * (0.3989422804014327 * jnp.exp(-0.5 * u * u))

    y_own = lambda n: R.YR.at[pl.ds(0, n)]
    me_quad = pl.ds(pl.multiple_of(32 * p, 16), 48)

    def contract(i):
        rows = rows_at(i)
        R.P0[rows, :] = nn(R.Z[rows, :], R.wdn[...]).astype(BF)

    def o_wide_start(piece, m):
        gather_start(lambda n: piece(t, n), piece, whole, m, s, other_chips)
        forward_own(piece, m)

    def o_wide_finish(piece, m):
        gather_forward(piece, whole, m, chips_by_arrival)
        gather_finish(piece, whole, m, all_chips)

    @pl.when(s == 0)
    def _():
        o_wide_start(o_piece, R.m_go)
        wo_forward()
        o_wide_finish(o_piece, R.m_go)
        gather_finish(wo_piece, whole, R.m_wo, all_chips)
        loop(0, 4, lambda q: unpack(R.GO, q, put_o))
        loop(0, 4, mid_norm)
        loop(0, 4, expand)
        loop(0, 4, contract)
        reduce_start(R.P0, 0, R.m_r0)
        total = reduce_finish(0, R.m_r0)
        R.YR[...] = (R.HIDQ[me_quad, :] + total + down_bias).astype(BF)
        gather_start(y_own, y_piece, sized, R.m_y, 1, all_chips)
        emit(R.YR, R.EA, R.m_ea)
        quad_weights()
        quad_weights_wait()
        loop(0, 4, quad_expand)
        gather_forward(g_piece, sized, R.m_g, quad_chips)
        gather_finish(g_piece, sized, R.m_g, quad_chips)

    @pl.when(s == 1)
    def _():
        def send(d, t2):
            g2 = lax.div(t2, 4)
            rc(
                R.GO.at[t, g2], R.GO.at[t, g2], R.m_o.at[0, d], R.m_o.at[1, t], s, t2, z
            ).start()

        peers(send)
        wo_forward()
        quad_weights_wait()
        gather_finish(wo_piece, whole, R.m_wo, all_chips)
        peers(lambda d, t2: arrived(R.GO.at[t2, zq], R.m_o.at[1, t2]))
        unpack(R.GO, zq, put_o)
        mid_norm(zq)
        loop(0, 4, quad_expand)

    dy = R.BUF[1, rows_at(zq), :]
    partial = None
    for g in range(4):
        du = (nt(dy, R.WDQ[g]) * R.GPQ[g]).astype(BF)
        term = nt(du, R.WUQ[g])
        partial = term if partial is None else partial + term
    R.PQ[1] = partial.astype(BF)
    quad_start(1, R.m_q1)

    def cols(ref, z2):
        return ref.at[:, pl.ds(pl.multiple_of(256 * z2, 256), 256)]

    def lines(ref, z2):
        return ref.at[pl.ds(pl.multiple_of(256 * z2, 256), 256)]

    def weight_send(cut, stage, land, row):
        def go(d):
            z2 = lax.rem(z + d, 4)
            rc(
                cut(stage, z2), land.at[z], R.m_w.at[row, d], R.m_w.at[row + 1, z], s, t, z2
            ).start()

        loop(1, 4, go)
        land[z] = cut(stage, z)[...]

    def weight_drain(cut, stage, row):
        loop(1, 4, lambda d: left(cut(stage, 0), R.m_w.at[row, d]))

    def weight_finish(land, row, out):
        def go(d):
            z2 = lax.rem(z + d, 4)
            arrived(land.at[z2], R.m_w.at[row + 1, z2])

        loop(1, 4, go)
        total = land[0].astype(F32)
        for z2 in range(1, 4):
            total = total + land[z2].astype(F32)
        out[...] = total

    def back_units(i):
        rows = rows_at(i)
        R.DU[rows, :] = (nt(R.BUF[1, rows, :], R.wdn[...]) * R.GP[rows, :]).astype(BF)

    def mlp_grads():
        loop(0, 4, back_units)
        R.WU[...] = tn(R.A2[...], R.DU[...]).astype(BF)
        weight_send(lines, R.WU, R.WUR, 0)
        R.WD[...] = tn(R.Z[...], R.BUF[1]).astype(BF)
        weight_send(cols, R.WD, R.WDR, 2)
        R.FV[6:7, :] = jnp.sum(R.DU[...].astype(F32), axis=0, keepdims=True)

    valid = lax.broadcasted_iota(jnp.int32, (48, 1), 0) < jnp.where(lax.rem(t, 4) == 3, 48, 32)

    def over_rows(v):
        return jnp.sum(jnp.where(valid, v, 0.0), axis=0, keepdims=True)

    me_rows = pl.ds(me_row, 48)
    da2 = quad_finish(1, R.m_q1)
    xhat2b, rstd2 = norm(R.HIDQ[me_quad, :])
    R.VS[2:3, :] = over_rows(da2 * xhat2b)
    R.VS[3:4, :] = over_rows(da2)
    dhid = R.BUF[1, me_rows, :].astype(F32) + norm_back(da2, xhat2b, rstd2, gain2)
    R.DHID[...] = dhid
    R.DHR[...] = dhid.astype(BF)
    R.DOR[...] = nt(R.DHR[...], R.WO[...]).astype(BF)

    def do_send(d, t2):
        sized(
            t,
            lambda n: rc(
                R.DOR.at[pl.ds(0, n), pl.ds(lane_of(t2), 128)],
                R.DB.at[pl.ds(me_row, n)],
                R.m_do.at[0, d],
                R.m_do.at[1, t],
                s,
                t2,
                z,
            ).start(),
        )

    peers(do_send)

    def do_drain(d, t2):
        sized(t, lambda n: left(R.DOR.at[pl.ds(0, n), pl.ds(0, 128)], R.m_do.at[0, d]))

    drains.append(lambda: peers(do_drain))

    def own_do(n):
        R.DB[pl.ds(me_row, n), :] = R.DOR[0:n, pl.ds(lane_of(t), 128)]
        R.DHF[pl.ds(me_row, n), :] = R.DHR[0:n, :]

    sized(t, own_do)
    dh_piece = lambda j, n: R.DHF.at[pl.ds(row_of(j), n)]
    dh_own = lambda n: R.DHR.at[pl.ds(0, n)]

    @pl.when(s == 0)
    def _():
        gather_forward(g_piece, sized, R.m_g, rest_chips)
        gather_finish(g_piece, sized, R.m_g, rest_chips)
        mlp_grads()

    def do_wait(d, t2):
        sized(t2, lambda n: arrived(R.DB.at[pl.ds(row_of(t2), n)], R.m_do.at[1, t2]))

    peers(do_wait)
    gather_start(dh_own, dh_piece, sized, R.m_dh, s, other_chips)

    def forward_dh(n):
        here = dh_piece(t, n)
        rc(here, here, R.m_dh.at[2, k], R.m_dh.at[3, k], s, 2 * k + 1 - c, z).start()

    sized(t, forward_dh)

    @pl.when(c == 0)
    def _():
        R.DO[...] = R.DB[:, 0:64]

    @pl.when(c == 1)
    def _():
        R.DO[...] = R.DB[:, 64:128]

    def back_attend(i):
        rows = rows_at(i)
        dp = nt(R.DO[rows, :], R.V[...])
        prob = R.PR[rows, :]
        ds = (prob * (dp - jnp.sum(prob * dp, -1, keepdims=True))).astype(BF)
        R.DS[rows, :] = ds
        R.DQKV[rows, 0:64] = (nn(ds, R.K[...]) * 0.125).astype(BF)

    loop(0, 4, back_attend)
    R.DQKV[:, 64:128] = (tn(R.Q[...], R.DS[...]).T * 0.125).astype(BF)
    R.DQKV[:, 128:192] = tn(R.DO[...], R.PH[...]).T.astype(BF)

    def back_qkv(i):
        rows = rows_at(i)
        R.P2[rows, :] = nn(R.DQKV[rows, :], R.wqkv[...]).astype(BF)

    loop(0, 4, back_qkv)
    reduce_start(R.P2, 1, R.m_r2)

    def norm_sums(i):
        rows = rows_at(i)
        xhat, _ = norm(R.BUF[0, rows, :].astype(F32))
        g = R.P2[rows, :].astype(F32)
        R.VS[0:1, :] += jnp.sum(g * xhat, axis=0, keepdims=True)
        R.VS[1:2, :] += jnp.sum(g, axis=0, keepdims=True)

    loop(0, 4, norm_sums)

    def s_send(d, t2):
        rc(
            R.VS.at[:, pl.ds(lane_of(t2), 128)],
            R.VR.at[t],
            R.m_vs.at[0, d],
            R.m_vs.at[1, t],
            s,
            t2,
            z,
        ).start()

    peers(s_send)
    drains.append(lambda: peers(lambda d, t2: left(R.VS.at[:, pl.ds(0, 128)], R.m_vs.at[0, d])))
    R.VR[t] = R.VS[:, pl.ds(lane_of(t), 128)]
    R.WQ[...] = tn(R.DQKV[...], R.A1[...]).astype(BF)
    weight_send(cols, R.WQ, R.WQR, 4)
    qkv_sum = jnp.sum(R.DQKV[...].astype(F32), axis=0, keepdims=True)
    R.FV[7:8, 0:64] = qkv_sum[:, 0:64]
    R.FV[7:8, 64:128] = qkv_sum[:, 128:192]
    gather_forward(dh_piece, sized, R.m_dh, chips_by_arrival)
    gather_finish(dh_piece, sized, R.m_dh, all_chips)
    drains.append(lambda: gather_drain(dh_own, sized, R.m_dh, other_chips))
    drains.append(lambda: gather_forward_drain(dh_piece, sized, R.m_dh))
    R.WG[...] = tn(R.O[...], R.DHF[...]).astype(BF)
    weight_send(cols, R.WG, R.WGR, 6)

    def vector_sums():
        peers(lambda d, t2: arrived(R.VR.at[t2], R.m_vs.at[1, t2]))
        mine = pl.ds(lane_of(t), 128)
        vec = R.VR[0]
        for t2 in range(1, 16):
            vec = vec + R.VR[t2]
        out_sum = jnp.sum(R.DHF[:, mine].astype(F32), axis=0, keepdims=True)
        down_sum = jnp.sum(R.BUF[1, :, mine].astype(F32), axis=0, keepdims=True)

        def place(lanes):
            R.FV[0:4, 0:64] = vec[0:4, lanes]
            R.FV[4:5, 0:64] = out_sum[:, lanes]
            R.FV[5:6, 0:64] = down_sum[:, lanes]

        pl.when(c == 0)(lambda: place(slice(0, 64)))
        pl.when(c == 1)(lambda: place(slice(64, 128)))

        def f_send(d):
            z2 = lax.rem(z + d, 4)
            rc(R.FV, R.FR.at[z], R.m_f.at[0, d], R.m_f.at[1, z], s, t, z2).start()

        loop(1, 4, f_send)
        R.FR[z] = R.FV[...]

    @pl.when(s == 0)
    def _():
        vector_sums()
        emit_finish(R.EA, R.m_ea, R.o_act)

    da1 = reduce_finish(1, R.m_r2)
    xhat1, rstd1 = norm(R.BUF[0, me_rows, :].astype(F32))
    R.IGR[...] = (R.DHID[...] + norm_back(da1, xhat1, rstd1, gain1)).astype(BF)
    g_own = lambda n: R.IGR.at[pl.ds(0, n)]

    @pl.when(s == 1)
    def _():
        gather_start(g_own, g_piece, sized, R.m_g, 0, quad_chips)
        gather_start(g_own, g_piece, sized, R.m_g, 0, rest_chips)

    emit(R.IGR, R.EI, R.m_ei)

    @pl.when(s == 1)
    def _():
        acc = None
        for g in range(4):
            term = nn(R.ZQ[g], R.WDQ[g])
            acc = term if acc is None else acc + term
        R.PQ[0] = acc.astype(BF)
        quad_start(0, R.m_q0)
        R.GA[t] = R.GO[t]
        o_wide_start(a_piece, R.m_ga)
        total = quad_finish(0, R.m_q0)
        R.YR[...] = (R.HIDQ[me_quad, :] + total + down_bias).astype(BF)
        emit(R.YR, R.EA, R.m_ea)
        o_wide_finish(a_piece, R.m_ga)
        loop(0, 4, lambda q: unpack(R.GA, q, put_o))
        loop(0, 4, mid_norm)
        loop(0, 4, expand)
        mlp_grads()
        vector_sums()
        emit_finish(R.EA, R.m_ea, R.o_act)

    drains.append(lambda: loop(1, 4, lambda d: left(R.FV, R.m_f.at[0, d])))
    weight_finish(R.WUR, 0, R.o_up)
    weight_finish(R.WDR, 2, R.o_dn)
    weight_finish(R.WQR, 4, R.o_qkv)
    weight_finish(R.WGR, 6, R.o_wo)

    def f_wait(d):
        z2 = lax.rem(z + d, 4)
        arrived(R.FR.at[z2], R.m_f.at[1, z2])

    loop(1, 4, f_wait)
    R.o_sums[...] = R.FR[0] + R.FR[1] + R.FR[2] + R.FR[3]
    emit_finish(R.EI, R.m_ei, R.o_ig)
    for f in drains:
        f()
    emit_drain(R.YR, R.m_ea)
    emit_drain(R.IGR, R.m_ei)
    reduce_drain(R.P2, 1, R.m_r2)
    quad_drain(1, R.m_q1)
    quad_weights_drain()
    weight_drain(lines, R.WU, 0)
    weight_drain(cols, R.WD, 2)
    weight_drain(cols, R.WQ, 4)
    weight_drain(cols, R.WG, 6)

    @pl.when(s == 0)
    def _():
        reduce_drain(R.P0, 0, R.m_r0)
        gather_drain(lambda n: o_piece(t, n), whole, R.m_go, other_chips)
        gather_forward_drain(o_piece, whole, R.m_go)
        gather_drain(y_own, sized, R.m_y, all_chips)
        gather_forward_drain(g_piece, sized, R.m_g)

    @pl.when(s == 1)
    def _():
        quad_drain(0, R.m_q0)
        gather_drain(lambda n: a_piece(t, n), whole, R.m_ga, other_chips)
        gather_forward_drain(a_piece, whole, R.m_ga)
        peers(lambda d, t2: left(R.GO.at[t, 0], R.m_o.at[0, d]))
        gather_drain(g_own, sized, R.m_g, all_chips)
        gather_forward_drain(y_piece, sized, R.m_y)


def finish(*refs):
    act, ig, sums, qkv, wo, up, dn = refs[:7]
    act2, ig2, g1, b1, qkv2, qvb, wo2, outb, g2, b2, up2, upb, dn2, downb = refs[7:]
    z = lax.axis_index("dp")

    def own(row, width):
        out = sums[row : row + 1, 0:width]
        for z2 in range(1, 4):
            out = jnp.where(z == z2, sums[row : row + 1, z2 * width : (z2 + 1) * width], out)
        return out

    for row, out in enumerate((g1, b1, g2, b2, outb, downb)):
        out[...] = own(row, 16)
    upb[...] = own(6, 64)
    qvb[...] = own(7, 32)
    for a, b in ((act, act2), (ig, ig2), (qkv, qkv2), (wo, wo2), (up, up2), (dn, dn2)):
        b[...] = a[...]


def body(images, cot, g1, b1, wqkv, qvb, wo, outb, g2, b2, wup, upb, wdn, downb):
    flat = ((1, 16), F32)
    act = ((4, 64, CHUNK), BF)
    square = ((256, 256), F32)
    qkv, owo = ((192, 256), F32), ((64, 256), F32)
    kept = [act, act, ((8, 256), F32), qkv, owo, square, square]
    final = [act, act, flat, flat, qkv, ((1, 32), F32), owo]
    final += [flat, flat, flat, square, ((1, 64), F32), square, flat]
    space = pl.BlockSpec(memory_space=pltpu.VMEM)
    outs = pl.pallas_call(
        kernel,
        name="two_layers",
        out_shape=[jax.ShapeDtypeStruct(*x) for x in kept],
        in_specs=[space] * 14,
        out_specs=[space] * 7,
        scratch_shapes=list(SCRATCH.values()),
        compiler_params=pltpu.CompilerParams(
            collective_id=0, has_side_effects=True, vmem_limit_bytes=60 * 1024 * 1024
        ),
    )(
        images.reshape(4, CHUNK, 64).transpose(0, 2, 1),
        cot.reshape(4, CHUNK, 64).transpose(0, 2, 1),
        g1,
        b1,
        wqkv.reshape(D, 192).T,
        qvb.reshape(1, 128),
        wo.reshape(64, D),
        outb,
        g2,
        b2,
        wup.reshape(D, 256),
        upb,
        wdn.reshape(256, D),
        downb,
    )
    outs = pl.pallas_call(
        finish,
        name="finish",
        out_shape=[jax.ShapeDtypeStruct(*x) for x in final],
        in_specs=[space] * 7,
        out_specs=[space] * 14,
    )(*outs)
    act, ig, og1, ob1, oqkv, oqvb, owo, ooutb, og2, ob2, oup, oupb, odn, odownb = outs
    return (
        act.transpose(0, 2, 1).reshape(1, 4, 1, CHUNK, 64),
        ig.transpose(0, 2, 1).reshape(1, 4, 1, CHUNK, 64),
        og1,
        ob1,
        oqkv.T.reshape(1, 256, 1, 192),
        oqvb.reshape(1, 1, 32),
        owo.reshape(1, 1, 64, 256),
        ooutb,
        og2,
        ob2,
        oup.reshape(1, 256, 256),
        oupb,
        odn.reshape(1, 256, 256),
        odownb,
    )


def solution(mesh):
    in_specs = (
        P(None, None, "dp", "tensor"),
        P(None, None, "dp", "tensor"),
        P("section", "tensor"),
        P("section", "tensor"),
        P("section", None, "tensor", None),
        P("section", "tensor", None),
        P("section", "tensor", None, None),
        P("section", "tensor"),
        P("section", "tensor"),
        P("section", "tensor"),
        P("section", None, "tensor"),
        P("section", "tensor"),
        P("section", "tensor", None),
        P("section", "tensor"),
    )
    out_specs = (
        P("section", None, None, "dp", "tensor"),
        P("section", None, None, "dp", "tensor"),
        P("section", ("tensor", "dp")),
        P("section", ("tensor", "dp")),
        P("section", "dp", "tensor", None),
        P("section", "tensor", "dp"),
        P("section", "tensor", None, "dp"),
        P("section", ("tensor", "dp")),
        P("section", ("tensor", "dp")),
        P("section", ("tensor", "dp")),
        P("section", "dp", "tensor"),
        P("section", ("tensor", "dp")),
        P("section", "tensor", "dp"),
        P("section", ("tensor", "dp")),
    )
    return jax.shard_map(body, mesh=mesh, in_specs=in_specs, out_specs=out_specs, check_vma=False)
```

```python
import jax
import jax.numpy as jnp
from jax import lax
from jax.experimental import pallas as pl
from jax.experimental.pallas import tpu as pltpu
from jax.sharding import PartitionSpec as P

BF = jnp.bfloat16
F32 = jnp.float32
D = 1024
TOK = 576
CHUNK = 144
epsilon = 1e-06

INPUTS = (
    "images",
    "cot",
    "g1",
    "b1",
    "wqkv",
    "qvb",
    "wo",
    "outb",
    "g2",
    "b2",
    "wup",
    "upb",
    "wdn",
    "downb",
)
OUTPUTS = ("o_act", "o_ig", "o_sums", "o_qkv", "o_wo", "o_up", "o_dn")


def vm(*shape, dtype=BF):
    return pltpu.VMEM(shape, dtype)


def dma(*shape):
    return pltpu.SemaphoreType.DMA(shape)


SCRATCH = dict(
    FB=vm(4, 80, 128),
    GX=vm(16, 4, 80, 128),
    BUF=vm(2, TOK, D),
    VB=vm(8, 128, dtype=F32),
    VG=vm(16, 8, 128, dtype=F32),
    VA=vm(8, D, dtype=F32),
    WO=vm(8, 2, 4, 16, D),
    A1=vm(TOK, D),
    Q=vm(TOK, 64),
    K=vm(TOK, 64),
    V=vm(TOK, 64),
    PR=vm(TOK, TOK, dtype=F32),
    PH=vm(TOK, TOK),
    DS=vm(TOK, TOK),
    O=vm(TOK, 64),
    GO=vm(16, 4, 80, 128),
    GA=vm(16, 4, 80, 128),
    OA=vm(TOK, D),
    HIDQ=vm(CHUNK, D, dtype=F32),
    WUQ=vm(4, D, 256),
    WDQ=vm(4, 256, D),
    UBQ=vm(4, 1, 256, dtype=F32),
    GPQ=vm(4, CHUNK, 256, dtype=F32),
    ZQ=vm(4, CHUNK, 256),
    PQ=vm(2, CHUNK, D),
    RQ=vm(2, 4, 48, D),
    A2=vm(TOK, D),
    GP=vm(TOK, 256, dtype=F32),
    Z=vm(TOK, 256),
    DU=vm(TOK, 256),
    YR=vm(48, D),
    P0=vm(TOK, D),
    P2=vm(TOK, D),
    SB=vm(2, 8, 48, D),
    PB=vm(2, 8, 48, D),
    RB=vm(2, 8, 48, D),
    DHID=vm(48, D, dtype=F32),
    DHR=vm(48, D),
    DOR=vm(48, D),
    DB=vm(TOK, 128),
    DO=vm(TOK, 64),
    DHF=vm(TOK, D),
    DQKV=vm(TOK, 192),
    IGR=vm(48, D),
    WU=vm(D, 256),
    WD=vm(256, D),
    WQ=vm(192, D),
    WG=vm(64, D),
    WUR=vm(4, 256, 256),
    WDR=vm(4, 256, 256),
    WQR=vm(4, 192, 256),
    WGR=vm(4, 64, 256),
    EA=vm(4, CHUNK, 128),
    EI=vm(4, CHUNK, 128),
    VS=vm(8, D, dtype=F32),
    VR=vm(16, 8, 128, dtype=F32),
    FV=vm(8, 256, dtype=F32),
    FR=vm(4, 8, 256, dtype=F32),
    m_z=dma(2, 4),
    m_x=dma(4, 8),
    m_v=dma(2, 16),
    m_wo=dma(4, 8),
    m_o=dma(2, 16),
    m_ga=dma(4, 8),
    m_go=dma(4, 8),
    m_wq=dma(4, 4),
    m_q0=dma(2, 4),
    m_q1=dma(2, 4),
    m_r0=dma(4, 8),
    m_r2=dma(4, 8),
    m_y=dma(4, 8),
    m_g=dma(4, 8),
    m_do=dma(2, 16),
    m_dh=dma(4, 8),
    m_ea=dma(2, 16),
    m_ei=dma(2, 16),
    m_vs=dma(2, 16),
    m_w=dma(8, 4),
    m_f=dma(2, 4),
    clear=pltpu.SemaphoreType.REGULAR,
)


def nn(a, b):
    return lax.dot_general(a, b, (((1,), (0,)), ((), ())), preferred_element_type=F32)


def nt(a, b):
    return lax.dot_general(a, b, (((1,), (1,)), ((), ())), preferred_element_type=F32)


def tn(a, b):
    return lax.dot_general(a, b, (((0,), (0,)), ((), ())), preferred_element_type=F32)


def loop(low, high, f):
    pl.loop(low, high)(f)


def quad_of(j):
    return lax.div(lax.rem(j, 8), 2)


def place_of(j):
    return 2 * lax.div(j, 8) + lax.rem(j, 2)


def member(quad, place):
    return 8 * lax.div(place, 2) + 2 * quad + lax.rem(place, 2)


def row_of(j):
    return pl.multiple_of(144 * quad_of(j) + 32 * place_of(j), 16)


def lane_of(j):
    return pl.multiple_of(128 * lax.div(j, 2), 128)


def sized(j, f):
    big = place_of(j) == 3
    pl.when(big)(lambda: f(48))
    pl.when(jnp.logical_not(big))(lambda: f(32))


def whole(j, f):
    f(None)


def norm(v):
    mu = jnp.mean(v, -1, keepdims=True)
    var = jnp.mean(v * v, -1, keepdims=True) - mu * mu
    rstd = lax.rsqrt(var + epsilon)
    return (v - mu) * rstd, rstd


def norm_back(g, xhat, rstd, gain):
    w = g * gain
    return rstd * (
        w - jnp.mean(w, -1, keepdims=True) - xhat * jnp.mean(w * xhat, -1, keepdims=True)
    )


class Refs:
    pass


def kernel(*refs):
    R = Refs()
    for name, ref in zip((*INPUTS, *OUTPUTS, *SCRATCH), refs):
        setattr(R, name, ref)
    s = lax.axis_index("section")
    t = lax.axis_index("tensor")
    z = lax.axis_index("dp")
    k = lax.div(t, 2)
    c = lax.rem(t, 2)
    zq = quad_of(t)
    p = place_of(t)
    me_row = row_of(t)
    drains = []

    def rc(src, dst, ss, rs, s2, t2, z2):
        return pltpu.make_async_remote_copy(
            src_ref=src,
            dst_ref=dst,
            send_sem=ss,
            recv_sem=rs,
            device_id={"section": s2, "tensor": t2, "dp": z2},
            device_id_type=pl.DeviceIdType.MESH,
        )

    def arrived(dst, rs):
        rc(dst, dst, rs, rs, s, 2 * k + 1 - c, z).wait_recv()

    def left(src, ss):
        rc(src, src, ss, ss, s, 2 * k + 1 - c, z).wait_send()

    def peers(f):
        def far(d):
            f(d, 8 * (1 - lax.div(t, 8)) + lax.rem(t + d, 8))

        def near(d):
            f(8 + d, 8 * lax.div(t, 8) + lax.rem(t + d, 8))

        loop(0, 8, far)
        loop(1, 8, near)

    def far_chips(f):
        loop(0, 4, lambda d: f(4 * (1 - lax.div(k, 4)) + lax.rem(k + d, 4)))

    def near_chips(f):
        loop(1, 4, lambda d: f(4 * lax.div(k, 4) + lax.rem(k + d, 4)))

    def other_chips(f):
        far_chips(f)
        near_chips(f)

    def chips_by_arrival(f):
        near_chips(f)
        far_chips(f)

    def all_chips(f):
        loop(0, 8, f)

    def quad_chips(f):
        loop(0, 2, lambda d: f(4 * d + zq))

    def rest_chips(f):
        loop(0, 6, lambda d: f(4 * lax.div(d, 3) + lax.rem(zq + 1 + lax.rem(d, 3), 4)))

    def per_core(f):
        pl.when(c == 0)(lambda: f(64, 80))
        pl.when(c == 1)(lambda: f(80, 64))

    def gather_start(src, dst, size, m, s2, chips):
        def go(k2):
            size(t, lambda n: rc(src(n), dst(t, n), m.at[0, 0], m.at[1, k], s2, 2 * k2 + c, z).start())

        chips(go)

    def forward_own(dst, m):
        here = dst(t, None)
        rc(here, here, m.at[2, 0], m.at[3, 0], s, 2 * k + 1 - c, z).start()

    def gather_forward(dst, size, m, chips, part=0):
        def go(k2):
            j = 2 * k2 + c

            def send(n):
                here = dst(j, n)
                arrived(here, m.at[1, k2])
                rc(here, here, m.at[2, 0], m.at[3, part], s, 2 * k + 1 - c, z).start()

            size(j, send)

        chips(go)

    def finish_rows(buf, m, quads, part=0):
        per_core(lambda mine, other: arrived(buf.at[pl.ds(0, other * quads)], m.at[3, part]))

    def drain_rows(buf, m, count):
        sized(t, lambda n: left(R.SB.at[0, pl.ds(0, count), pl.ds(0, n)], m.at[0, 0]))

    def drain_forward_rows(buf, m):
        per_core(lambda mine, other: left(buf.at[pl.ds(0, mine * 4)], m.at[2, 0]))

    def quad_start(i, m):
        def go(p2):
            t2 = member(zq, p2)
            sized(
                t2,
                lambda n: rc(
                    R.PQ.at[i, pl.ds(pl.multiple_of(32 * p2, 16), n)],
                    R.RQ.at[i, p, pl.ds(0, n)],
                    m.at[0, p2],
                    m.at[1, p],
                    s,
                    t2,
                    z,
                ).start(),
            )

        far = 2 - 2 * lax.div(p, 2)
        loop(0, 2, lambda d: go(far + lax.rem(c + d, 2)))
        go(2 - far + 1 - c)
        R.RQ[i, p] = R.PQ[i, pl.ds(pl.multiple_of(32 * p, 16), 48), :]

    def quad_finish(i, m):
        def go(d):
            p2 = lax.rem(p + d, 4)
            sized(t, lambda n: arrived(R.RQ.at[i, p2, pl.ds(0, n)], m.at[1, p2]))

        loop(1, 4, go)
        total = R.RQ[i, 0].astype(F32)
        for p2 in range(1, 4):
            total = total + R.RQ[i, p2].astype(F32)
        return total

    def quad_drain(i, m):
        def go(d):
            p2 = lax.rem(p + d, 4)
            sized(member(zq, p2), lambda n: left(R.PQ.at[i, pl.ds(0, n)], m.at[0, p2]))

        loop(1, 4, go)

    def reduce_over(part, i, m, compute):
        def sibling(q, d):
            k2 = 4 * d + q
            j = 2 * k2 + 1 - c
            sized(
                j,
                lambda n: rc(
                    part.at[pl.ds(row_of(j), n)],
                    R.SB.at[i, k2, pl.ds(0, n)],
                    m.at[0, 0],
                    m.at[1, k2],
                    s,
                    2 * k + 1 - c,
                    z,
                ).start(),
            )

        def mid(q, d):
            k2 = 4 * d + q
            j = 2 * k2 + c
            sized(j, lambda n: arrived(R.SB.at[i, k2, pl.ds(0, n)], m.at[1, k2]))
            both = part[pl.ds(row_of(j), 48), :].astype(F32) + R.SB[i, k2].astype(F32)
            R.PB[i, k2] = both.astype(BF)

            def send(n):
                rc(
                    R.PB.at[i, k2, pl.ds(0, n)],
                    R.RB.at[i, k, pl.ds(0, n)],
                    m.at[2, 0],
                    m.at[3, 0],
                    s,
                    j,
                    z,
                ).start()

            pl.when(k2 != k)(lambda: sized(j, send))

        def go(a):
            q = lax.rem(zq + 1 + a, 4)
            compute(q)
            loop(0, 2, lambda d: sibling(q, d))
            pl.when(a > 0)(lambda: loop(0, 2, lambda d: mid(lax.rem(zq + a, 4), d)))

        loop(0, 4, go)
        loop(0, 2, lambda d: mid(zq, d))

    def reduce_finish(i, m):
        sized(t, lambda n: arrived(R.RB.at[i, pl.ds(0, 7), pl.ds(0, n)], m.at[3, 0]))
        R.RB[i, k] = R.PB[i, k]
        total = R.RB[i, 0].astype(F32)
        for k2 in range(1, 8):
            total = total + R.RB[i, k2].astype(F32)
        return total

    def reduce_drain(part, i, m):
        per_core(lambda mine, other: left(part.at[pl.ds(0, other * 4)], m.at[0, 0]))
        per_core(
            lambda mine, other: sized(t, lambda n: left(part.at[pl.ds(0, mine * 4 - n)], m.at[2, 0]))
        )

    def emit(rows, E, m):
        def go(d, t2):
            def send(n):
                rc(
                    rows.at[pl.ds(0, n), pl.ds(lane_of(t2), 128)],
                    E.at[z, pl.ds(pl.multiple_of(32 * p, 16), n)],
                    m.at[0, 0],
                    m.at[1, 0],
                    s,
                    t2,
                    zq,
                ).start()

            sized(t, send)

        peers(go)
        pl.when(zq != z)(lambda: go(8, t))

        def local():
            def put(n):
                E[z, pl.ds(pl.multiple_of(32 * p, 16), n), :] = rows[
                    pl.ds(0, n), pl.ds(lane_of(t), 128)
                ]

            sized(t, put)

        pl.when(zq == z)(local)

    def emit_drain(rows, m):
        def taken(count):
            sized(t, lambda n: left(R.GX.at[pl.ds(0, count), 0, pl.ds(0, n)], m.at[0, 0]))

        pl.when(zq != z)(lambda: taken(16))
        pl.when(zq == z)(lambda: taken(15))

    def emit_finish(E, m, out):
        pl.when(zq != z)(lambda: arrived(E, m.at[1, 0]))
        pl.when(zq == z)(
            lambda: sized(t, lambda n: arrived(R.DB.at[pl.ds(0, TOK - n)], m.at[1, 0]))
        )

        @pl.when(c == 0)
        def _():
            for i in range(4):
                out[i] = E[i, :, 0:64].T

        @pl.when(c == 1)
        def _():
            for i in range(4):
                out[i] = E[i, :, 64:128].T

    bar = pltpu.get_barrier_semaphore()

    def greet(s2, t2, z2):
        pl.semaphore_signal(
            bar,
            inc=1,
            device_id={"section": s2, "tensor": t2, "dp": z2},
            device_id_type=pl.DeviceIdType.MESH,
        )

    loop(1, 16, lambda d: greet(s, lax.rem(t + d, 16), z))
    loop(1, 4, lambda d: greet(s, t, lax.rem(z + d, 4)))
    loop(0, 8, lambda d: greet(1 - s, 2 * d + c, z))

    def out_to(d):
        pl.when(jnp.logical_not(jnp.logical_and(d == t, zq == z)))(lambda: greet(s, d, zq))

    def out_from(d):
        t2 = member(z, lax.rem(d, 4))
        z2 = lax.div(d, 4)
        pl.when(jnp.logical_not(jnp.logical_and(t2 == t, z2 == z)))(lambda: greet(s, t2, z2))

    loop(0, 16, out_to)
    loop(0, 16, out_from)

    def pack(src):
        for m in range(4):
            R.FB[m, 64:80, :] = jnp.zeros((16, 128), BF)
            rows = src[m].T
            R.FB[m, :, 0:64] = rows[0:80, :]
            R.FB[m, 0:64, 64:128] = rows[80:144, :]

    pl.when(s == 0)(lambda: pack(R.images))
    pl.when(s == 1)(lambda: pack(R.cot))
    R.VB[...] = jnp.zeros((8, 128), F32)
    vecs = (R.g1, R.b1, R.g2, R.b2, R.outb, R.downb)

    @pl.when(c == 0)
    def _():
        for i, v in enumerate(vecs):
            R.VB[i : i + 1, 0:64] = v[...]

    @pl.when(c == 1)
    def _():
        for i, v in enumerate(vecs):
            R.VB[i : i + 1, 64:128] = v[...]

    R.VB[6:7, :] = R.upb[:, 0:128]
    R.VB[7:8, :] = R.upb[:, 128:256]
    R.VG[t] = R.VB[...]
    R.GX[t, z] = R.FB[z]
    R.WO[k, c, z] = R.wo[pl.ds(pl.multiple_of(16 * z, 16), 16), :]
    R.WUQ[zq] = R.wup[...]
    R.WDQ[zq] = R.wdn[...]
    R.FV[...] = jnp.zeros((8, 256), F32)
    R.VS[...] = jnp.zeros((8, D), F32)
    for i in range(4):
        R.GO[t, i, 64:80, :] = jnp.zeros((16, 128), BF)

    pl.semaphore_wait(bar, 58 - 2 * (zq == z).astype(jnp.int32))

    def z_send(d):
        z2 = lax.rem(z + d, 4)
        rc(R.FB.at[z2], R.GX.at[t, z], R.m_z.at[0, d], R.m_z.at[1, z], s, t, z2).start()

    loop(1, 4, z_send)

    def z_wait(d):
        z2 = lax.rem(z + d, 4)
        arrived(R.GX.at[t, z2], R.m_z.at[1, z2])

    loop(1, 4, z_wait)
    drains.append(lambda: loop(1, 4, lambda d: left(R.FB.at[0], R.m_z.at[0, d])))
    x_piece = lambda j, n: R.GX.at[j]
    def by_plane(f):
        pl.when(lax.rem(z, 2) == 0)(lambda: f(R.wup, R.WUQ, R.WDQ, 512))
        pl.when(lax.rem(z, 2) == 1)(lambda: f(R.wdn, R.WDQ, R.WUQ, 128))

    def quad_weights():
        def fetch(src, own, other, half):
            def go(d):
                t2 = member(lax.rem(zq + d, 4), p)
                rc(src, own.at[zq], R.m_wq.at[0, 0], R.m_wq.at[1, zq], s, t2, z).start()

            loop(1, 4, go)

        by_plane(fetch)

    def quad_weights_pass():
        def give(src, own, other, half):
            def go(d):
                g2 = lax.rem(zq + d, 4)
                arrived(own.at[g2], R.m_wq.at[1, g2])
                for first, z2 in ((0, lax.rem(z + 1, 4)), (half, lax.rem(z + 3, 4))):
                    piece = own.at[g2, pl.ds(first, half)]
                    rc(piece, piece, R.m_wq.at[2, 0], R.m_wq.at[3, 0], s, t, z2).start()

            loop(1, 4, go)

        by_plane(give)

    def quad_weights_wait():
        by_plane(lambda src, own, other, half: arrived(other.at[pl.ds(0, 3)], R.m_wq.at[3, 0]))

    def quad_weights_drain():
        def sent(src, own, other, half):
            left(own.at[pl.ds(0, 3)], R.m_wq.at[0, 0])
            left(own.at[pl.ds(0, 3)], R.m_wq.at[2, 0])

        by_plane(sent)

    def v_send(d, t2):
        rc(R.VB, R.VG.at[t], R.m_v.at[0, 0], R.m_v.at[1, 0], s, t2, z).start()

    @pl.when(s == 1)
    def _():
        quad_weights()
        quad_weights_pass()
        pl.semaphore_wait(R.clear, 1)

    gather_start(lambda n: R.GX.at[t], x_piece, whole, R.m_x, s, other_chips)
    forward_own(x_piece, R.m_x)
    peers(v_send)
    drains.append(lambda: left(R.VG.at[pl.ds(0, 15)], R.m_v.at[0, 0]))

    def wo_send(k2):
        here = R.WO.at[k, c, z]
        rc(here, here, R.m_wo.at[0, 0], R.m_wo.at[1, 0], s, 2 * k2 + c, z).start()

    other_chips(wo_send)
    gather_forward(x_piece, whole, R.m_x, chips_by_arrival)
    arrived(R.GX.at[pl.ds(0, 8)], R.m_x.at[3, 0])
    arrived(R.WO.at[pl.ds(0, 7), 0, 0], R.m_wo.at[1, 0])

    def wo_planes(d):
        here = R.WO.at[:, c, z]
        rc(here, here, R.m_wo.at[0, 1], R.m_wo.at[1, 1], s, t, lax.rem(z + d, 4)).start()

    loop(1, 4, wo_planes)
    arrived(R.VG.at[pl.ds(0, 15)], R.m_v.at[1, 0])
    for kk in range(8):
        R.VA[:, 128 * kk : 128 * kk + 128] = R.VG[2 * kk] + R.VG[2 * kk + 1]
    for g in range(4):
        R.UBQ[g, :, 0:128] = R.VG[member(g, p), 6:7, :]
        R.UBQ[g, :, 128:256] = R.VG[member(g, p), 7:8, :]
    gain1, bias1 = R.VA[0:1, :], R.VA[1:2, :]
    gain2, bias2 = R.VA[2:3, :], R.VA[3:4, :]
    out_bias, down_bias = R.VA[4:5, :], R.VA[5:6, :]

    def unpack(G, q, put):
        row = pl.multiple_of(144 * q, 16)
        for kk in range(8):
            a, b = G[2 * kk, q], G[2 * kk + 1, q]
            lanes = slice(128 * kk, 128 * kk + 128)
            put(pl.ds(row, 80), lanes, jnp.concatenate([a[:, :64], b[:, :64]], axis=1))
            put(
                pl.ds(row + 80, 64),
                lanes,
                jnp.concatenate([a[:64, 64:], b[:64, 64:]], axis=1),
            )

    def put_first(rows, lanes, v):
        R.BUF[s, rows, lanes] = v

    loop(0, 4, lambda q: unpack(R.GX, q, put_first))
    drains.append(lambda: left(R.GX.at[pl.ds(0, 7)], R.m_x.at[0, 0]))
    drains.append(lambda: left(R.GX.at[pl.ds(0, 8)], R.m_x.at[2, 0]))

    y_piece = lambda j, n: R.BUF.at[0, pl.ds(row_of(j), n)]
    g_piece = lambda j, n: R.BUF.at[1, pl.ds(row_of(j), n)]

    @pl.when(s == 1)
    def _():
        gather_forward(y_piece, sized, R.m_y, all_chips)
        finish_rows(R.BUF.at[0], R.m_y, 4)

    def rows_at(i):
        return pl.ds(pl.multiple_of(CHUNK * i, 16), CHUNK)

    def project(i):
        rows = rows_at(i)
        xhat, _ = norm(R.BUF[0, rows, :].astype(F32))
        a = (xhat * gain1 + bias1).astype(BF)
        R.A1[rows, :] = a
        mixed = nt(a, R.wqkv[...])
        R.Q[rows, :] = (mixed[:, 0:64] + R.qvb[:, 0:64]).astype(BF)
        R.K[rows, :] = mixed[:, 64:128].astype(BF)
        R.V[rows, :] = (mixed[:, 128:192] + R.qvb[:, 64:128]).astype(BF)

    loop(0, 4, project)

    def attend(i):
        rows = rows_at(i)
        sc = nt(R.Q[rows, :], R.K[...]) * 0.125
        e = jnp.exp(sc - jnp.max(sc, -1, keepdims=True))
        prob = e / jnp.sum(e, -1, keepdims=True)
        R.PR[rows, :] = prob
        ph = prob.astype(BF)
        R.PH[rows, :] = ph
        o = nn(ph, R.V[...]).astype(BF)
        R.O[rows, :] = o
        R.GO[t, i, :, 0:64] = o[0:80, :]
        R.GO[t, i, 0:64, 64:128] = o[80:144, :]

    loop(0, 4, attend)
    o_piece = lambda j, n: R.GO.at[j]
    a_piece = lambda j, n: R.GA.at[j]

    def put_o(rows, lanes, v):
        R.OA[rows, lanes] = v

    def mid_norm(i):
        rows = rows_at(i)
        hidden = R.BUF[0, rows, :].astype(F32) + nn(R.OA[rows, :], R.WO[...].reshape(D, D)) + out_bias
        xhat, _ = norm(hidden)
        R.A2[rows, :] = (xhat * gain2 + bias2).astype(BF)

        @pl.when(i == zq)
        def _():
            R.HIDQ[...] = hidden

    def wo_cores():
        arrived(R.WO.at[:, 0, pl.ds(0, 3)], R.m_wo.at[1, 1])
        here = R.WO.at[:, c]
        rc(here, here, R.m_wo.at[2, 0], R.m_wo.at[3, 0], s, 2 * k + 1 - c, z).start()

    drains.append(lambda: left(R.WO.at[pl.ds(0, 7), 0, 0], R.m_wo.at[0, 0]))
    drains.append(lambda: left(R.WO.at[:, 0, pl.ds(0, 3)], R.m_wo.at[0, 1]))
    drains.append(lambda: left(R.WO.at[:, 0], R.m_wo.at[2, 0]))

    def expand(i):
        rows = rows_at(i)
        u = nn(R.A2[rows, :], R.wup[...]) + R.upb[...]
        half = 0.5 * (1.0 + lax.erf(u * 0.7071067811865476))
        R.Z[rows, :] = (u * half).astype(BF)
        R.GP[rows, :] = half + u * (0.3989422804014327 * jnp.exp(-0.5 * u * u))

    def quad_expand(g):
        u = nn(R.A2[rows_at(zq), :], R.WUQ[g]) + R.UBQ[g]
        half = 0.5 * (1.0 + lax.erf(u * 0.7071067811865476))
        R.ZQ[g] = (u * half).astype(BF)
        R.GPQ[g] = half + u * (0.3989422804014327 * jnp.exp(-0.5 * u * u))

    y_own = lambda n: R.YR.at[pl.ds(0, n)]
    me_quad = pl.ds(pl.multiple_of(32 * p, 16), 48)

    def contract(i):
        rows = rows_at(i)
        R.P0[rows, :] = nn(R.Z[rows, :], R.wdn[...]).astype(BF)

    def o_wide_start(piece, m):
        gather_start(lambda n: piece(t, n), piece, whole, m, s, other_chips)
        forward_own(piece, m)

    def o_wide_finish(piece, m):
        gather_forward(piece, whole, m, chips_by_arrival)
        arrived(R.GX.at[pl.ds(0, 8)], m.at[3, 0])

    @pl.when(s == 0)
    def _():
        o_wide_start(o_piece, R.m_go)
        wo_cores()
        o_wide_finish(o_piece, R.m_go)
        pl.semaphore_signal(
            R.clear,
            inc=1,
            device_id={"section": 1, "tensor": t, "dp": z},
            device_id_type=pl.DeviceIdType.MESH,
        )
        arrived(R.WO.at[:, 0], R.m_wo.at[3, 0])

        def forward_quad(q):
            unpack(R.GO, q, put_o)
            mid_norm(q)
            expand(q)
            contract(q)

        reduce_over(R.P0, 0, R.m_r0, forward_quad)
        total = reduce_finish(0, R.m_r0)
        R.YR[...] = (R.HIDQ[me_quad, :] + total + down_bias).astype(BF)
        gather_start(y_own, y_piece, sized, R.m_y, 1, all_chips)
        emit(R.YR, R.EA, R.m_ea)
        quad_weights()
        quad_weights_pass()
        quad_weights_wait()
        loop(0, 4, quad_expand)
        gather_forward(g_piece, sized, R.m_g, quad_chips)
        finish_rows(R.BUF.at[1], R.m_g, 1)

    @pl.when(s == 1)
    def _():
        def send(d, t2):
            g2 = quad_of(t2)
            rc(
                R.GO.at[t, g2], R.GO.at[t, g2], R.m_o.at[0, 0], R.m_o.at[1, 0], s, t2, z
            ).start()

        peers(send)
        wo_cores()
        quad_weights_wait()
        arrived(R.WO.at[:, 0], R.m_wo.at[3, 0])
        arrived(R.GO.at[pl.ds(0, 15), 0], R.m_o.at[1, 0])
        unpack(R.GO, zq, put_o)
        mid_norm(zq)
        loop(0, 4, quad_expand)

    dy = R.BUF[1, rows_at(zq), :]
    partial = None
    for g in range(4):
        du = (nt(dy, R.WDQ[g]) * R.GPQ[g]).astype(BF)
        term = nt(du, R.WUQ[g])
        partial = term if partial is None else partial + term
    R.PQ[1] = partial.astype(BF)
    quad_start(1, R.m_q1)

    def cols(ref, z2):
        return ref.at[:, pl.ds(pl.multiple_of(256 * z2, 256), 256)]

    def lines(ref, z2):
        return ref.at[pl.ds(pl.multiple_of(256 * z2, 256), 256)]

    def weight_send(cut, stage, land, row):
        def go(d):
            z2 = lax.rem(z + d, 4)
            rc(
                cut(stage, z2), land.at[z], R.m_w.at[row, d], R.m_w.at[row + 1, z], s, t, z2
            ).start()

        loop(1, 4, go)
        land[z] = cut(stage, z)[...]

    def weight_drain(cut, stage, row):
        loop(1, 4, lambda d: left(cut(stage, 0), R.m_w.at[row, d]))

    def weight_finish(land, row, out):
        def go(d):
            z2 = lax.rem(z + d, 4)
            arrived(land.at[z2], R.m_w.at[row + 1, z2])

        loop(1, 4, go)
        total = land[0].astype(F32)
        for z2 in range(1, 4):
            total = total + land[z2].astype(F32)
        out[...] = total

    def back_units(i):
        rows = rows_at(i)
        R.DU[rows, :] = (nt(R.BUF[1, rows, :], R.wdn[...]) * R.GP[rows, :]).astype(BF)

    def mlp_grads():
        loop(0, 4, back_units)
        R.WU[...] = tn(R.A2[...], R.DU[...]).astype(BF)
        weight_send(lines, R.WU, R.WUR, 0)
        R.WD[...] = tn(R.Z[...], R.BUF[1]).astype(BF)
        weight_send(cols, R.WD, R.WDR, 2)
        R.FV[6:7, :] = jnp.sum(R.DU[...].astype(F32), axis=0, keepdims=True)

    valid = lax.broadcasted_iota(jnp.int32, (48, 1), 0) < jnp.where(p == 3, 48, 32)

    def over_rows(v):
        return jnp.sum(jnp.where(valid, v, 0.0), axis=0, keepdims=True)

    me_rows = pl.ds(me_row, 48)
    da2 = quad_finish(1, R.m_q1)
    xhat2b, rstd2 = norm(R.HIDQ[me_quad, :])
    R.VS[2:3, :] = over_rows(da2 * xhat2b)
    R.VS[3:4, :] = over_rows(da2)
    dhid = R.BUF[1, me_rows, :].astype(F32) + norm_back(da2, xhat2b, rstd2, gain2)
    R.DHID[...] = dhid
    R.DHR[...] = dhid.astype(BF)
    R.DOR[...] = nt(R.DHR[...], R.WO[...].reshape(D, D)).astype(BF)

    def do_send(d, t2):
        sized(
            t,
            lambda n: rc(
                R.DOR.at[pl.ds(0, n), pl.ds(lane_of(t2), 128)],
                R.DB.at[pl.ds(me_row, n)],
                R.m_do.at[0, 0],
                R.m_do.at[1, 0],
                s,
                t2,
                z,
            ).start(),
        )

    peers(do_send)

    drains.append(
        lambda: sized(t, lambda n: left(R.GX.at[pl.ds(0, 15), 0, pl.ds(0, n)], R.m_do.at[0, 0]))
    )

    def own_do(n):
        R.DB[pl.ds(me_row, n), :] = R.DOR[0:n, pl.ds(lane_of(t), 128)]
        R.DHF[pl.ds(me_row, n), :] = R.DHR[0:n, :]

    sized(t, own_do)
    dh_piece = lambda j, n: R.DHF.at[pl.ds(row_of(j), n)]
    dh_own = lambda n: R.DHR.at[pl.ds(0, n)]

    @pl.when(s == 0)
    def _():
        gather_forward(g_piece, sized, R.m_g, rest_chips, 1)
        finish_rows(R.BUF.at[1], R.m_g, 3, 1)
        mlp_grads()

    sized(t, lambda n: arrived(R.DB.at[pl.ds(0, TOK - n)], R.m_do.at[1, 0]))
    gather_start(dh_own, dh_piece, sized, R.m_dh, s, other_chips)

    def forward_dh(n):
        here = dh_piece(t, n)
        rc(here, here, R.m_dh.at[2, 0], R.m_dh.at[3, 0], s, 2 * k + 1 - c, z).start()

    sized(t, forward_dh)

    @pl.when(c == 0)
    def _():
        R.DO[...] = R.DB[:, 0:64]

    @pl.when(c == 1)
    def _():
        R.DO[...] = R.DB[:, 64:128]

    def back_attend(i):
        rows = rows_at(i)
        dp = nt(R.DO[rows, :], R.V[...])
        prob = R.PR[rows, :]
        ds = (prob * (dp - jnp.sum(prob * dp, -1, keepdims=True))).astype(BF)
        R.DS[rows, :] = ds
        R.DQKV[rows, 0:64] = (nn(ds, R.K[...]) * 0.125).astype(BF)

    loop(0, 4, back_attend)
    R.DQKV[:, 64:128] = (tn(R.Q[...], R.DS[...]).T * 0.125).astype(BF)
    R.DQKV[:, 128:192] = tn(R.DO[...], R.PH[...]).T.astype(BF)

    def back_qkv(i):
        rows = rows_at(i)
        R.P2[rows, :] = nn(R.DQKV[rows, :], R.wqkv[...]).astype(BF)

    reduce_over(R.P2, 1, R.m_r2, back_qkv)

    def norm_sums(i):
        rows = rows_at(i)
        xhat, _ = norm(R.BUF[0, rows, :].astype(F32))
        g = R.P2[rows, :].astype(F32)
        R.VS[0:1, :] += jnp.sum(g * xhat, axis=0, keepdims=True)
        R.VS[1:2, :] += jnp.sum(g, axis=0, keepdims=True)

    loop(0, 4, norm_sums)

    def s_send(d, t2):
        rc(
            R.VS.at[:, pl.ds(lane_of(t2), 128)],
            R.VR.at[t],
            R.m_vs.at[0, 0],
            R.m_vs.at[1, 0],
            s,
            t2,
            z,
        ).start()

    peers(s_send)
    R.VR[t] = R.VS[:, pl.ds(lane_of(t), 128)]
    R.WQ[...] = tn(R.DQKV[...], R.A1[...]).astype(BF)
    weight_send(cols, R.WQ, R.WQR, 4)
    qkv_sum = jnp.sum(R.DQKV[...].astype(F32), axis=0, keepdims=True)
    R.FV[7:8, 0:64] = qkv_sum[:, 0:64]
    R.FV[7:8, 64:128] = qkv_sum[:, 128:192]
    gather_forward(dh_piece, sized, R.m_dh, chips_by_arrival)
    finish_rows(R.DHF, R.m_dh, 4)
    drains.append(lambda: drain_rows(R.DHF, R.m_dh, 7))
    drains.append(lambda: drain_forward_rows(R.DHF, R.m_dh))
    R.WG[...] = tn(R.O[...], R.DHF[...]).astype(BF)
    weight_send(cols, R.WG, R.WGR, 6)

    def vector_sums():
        arrived(R.VR.at[pl.ds(0, 15)], R.m_vs.at[1, 0])
        mine = pl.ds(lane_of(t), 128)
        vec = R.VR[0]
        for t2 in range(1, 16):
            vec = vec + R.VR[t2]
        out_sum = jnp.sum(R.DHF[:, mine].astype(F32), axis=0, keepdims=True)
        down_sum = jnp.sum(R.BUF[1, :, mine].astype(F32), axis=0, keepdims=True)

        def place(lanes):
            R.FV[0:4, 0:64] = vec[0:4, lanes]
            R.FV[4:5, 0:64] = out_sum[:, lanes]
            R.FV[5:6, 0:64] = down_sum[:, lanes]

        pl.when(c == 0)(lambda: place(slice(0, 64)))
        pl.when(c == 1)(lambda: place(slice(64, 128)))

        def f_send(d):
            z2 = lax.rem(z + d, 4)
            rc(R.FV, R.FR.at[z], R.m_f.at[0, d], R.m_f.at[1, z], s, t, z2).start()

        loop(1, 4, f_send)
        R.FR[z] = R.FV[...]

    @pl.when(s == 0)
    def _():
        vector_sums()
        emit_finish(R.EA, R.m_ea, R.o_act)

    for f in drains:
        f()
    quad_drain(1, R.m_q1)
    quad_weights_drain()

    @pl.when(s == 0)
    def _():
        reduce_drain(R.P0, 0, R.m_r0)
        left(R.GX.at[pl.ds(0, 7)], R.m_go.at[0, 0])
        left(R.GX.at[pl.ds(0, 8)], R.m_go.at[2, 0])
        drain_rows(R.BUF.at[0], R.m_y, 8)
        drain_forward_rows(R.BUF.at[1], R.m_g)
        emit_drain(R.YR, R.m_ea)

    @pl.when(s == 1)
    def _():
        left(R.GO.at[pl.ds(0, 15), 0], R.m_o.at[0, 0])
        drain_forward_rows(R.BUF.at[0], R.m_y)

    da1 = reduce_finish(1, R.m_r2)
    xhat1, rstd1 = norm(R.BUF[0, me_rows, :].astype(F32))
    R.IGR[...] = (R.DHID[...] + norm_back(da1, xhat1, rstd1, gain1)).astype(BF)
    g_own = lambda n: R.IGR.at[pl.ds(0, n)]

    @pl.when(s == 1)
    def _():
        gather_start(g_own, g_piece, sized, R.m_g, 0, quad_chips)
        gather_start(g_own, g_piece, sized, R.m_g, 0, rest_chips)

    emit(R.IGR, R.EI, R.m_ei)

    @pl.when(s == 1)
    def _():
        acc = None
        for g in range(4):
            term = nn(R.ZQ[g], R.WDQ[g])
            acc = term if acc is None else acc + term
        R.PQ[0] = acc.astype(BF)
        quad_start(0, R.m_q0)
        R.GA[t] = R.GO[t]
        o_wide_start(a_piece, R.m_ga)
        total = quad_finish(0, R.m_q0)
        R.YR[...] = (R.HIDQ[me_quad, :] + total + down_bias).astype(BF)
        emit(R.YR, R.EA, R.m_ea)
        o_wide_finish(a_piece, R.m_ga)
        loop(0, 4, lambda q: unpack(R.GA, q, put_o))
        loop(0, 4, mid_norm)
        loop(0, 4, expand)
        mlp_grads()
        vector_sums()
        emit_finish(R.EA, R.m_ea, R.o_act)

    weight_finish(R.WUR, 0, R.o_up)
    weight_finish(R.WDR, 2, R.o_dn)
    weight_finish(R.WQR, 4, R.o_qkv)
    weight_finish(R.WGR, 6, R.o_wo)

    def f_wait(d):
        z2 = lax.rem(z + d, 4)
        arrived(R.FR.at[z2], R.m_f.at[1, z2])

    loop(1, 4, f_wait)
    R.o_sums[...] = R.FR[0] + R.FR[1] + R.FR[2] + R.FR[3]
    emit_finish(R.EI, R.m_ei, R.o_ig)
    emit_drain(R.IGR, R.m_ei)
    reduce_drain(R.P2, 1, R.m_r2)
    left(R.VR.at[pl.ds(0, 15)], R.m_vs.at[0, 0])
    loop(1, 4, lambda d: left(R.FV, R.m_f.at[0, d]))
    weight_drain(lines, R.WU, 0)
    weight_drain(cols, R.WD, 2)
    weight_drain(cols, R.WQ, 4)
    weight_drain(cols, R.WG, 6)

    @pl.when(s == 1)
    def _():
        quad_drain(0, R.m_q0)
        left(R.GX.at[pl.ds(0, 7)], R.m_ga.at[0, 0])
        left(R.GX.at[pl.ds(0, 8)], R.m_ga.at[2, 0])
        drain_rows(R.BUF.at[1], R.m_g, 8)
        emit_drain(R.YR, R.m_ea)


def finish(*refs):
    act, ig, sums, qkv, wo, up, dn = refs[:7]
    act2, ig2, g1, b1, qkv2, qvb, wo2, outb, g2, b2, up2, upb, dn2, downb = refs[7:]
    z = lax.axis_index("dp")

    def own(row, width):
        out = sums[row : row + 1, 0:width]
        for z2 in range(1, 4):
            out = jnp.where(z == z2, sums[row : row + 1, z2 * width : (z2 + 1) * width], out)
        return out

    for row, out in enumerate((g1, b1, g2, b2, outb, downb)):
        out[...] = own(row, 16)
    upb[...] = own(6, 64)
    qvb[...] = own(7, 32)
    for a, b in ((act, act2), (ig, ig2), (qkv, qkv2), (wo, wo2), (up, up2), (dn, dn2)):
        b[...] = a[...]


def body(images, cot, g1, b1, wqkv, qvb, wo, outb, g2, b2, wup, upb, wdn, downb):
    flat = ((1, 16), F32)
    act = ((4, 64, CHUNK), BF)
    square = ((256, 256), F32)
    qkv, owo = ((192, 256), F32), ((64, 256), F32)
    kept = [act, act, ((8, 256), F32), qkv, owo, square, square]
    final = [act, act, flat, flat, qkv, ((1, 32), F32), owo]
    final += [flat, flat, flat, square, ((1, 64), F32), square, flat]
    space = pl.BlockSpec(memory_space=pltpu.VMEM)
    outs = pl.pallas_call(
        kernel,
        name="two_layers",
        out_shape=[jax.ShapeDtypeStruct(*x) for x in kept],
        in_specs=[space] * 14,
        out_specs=[space] * 7,
        scratch_shapes=list(SCRATCH.values()),
        compiler_params=pltpu.CompilerParams(
            collective_id=0, has_side_effects=True, vmem_limit_bytes=60 * 1024 * 1024
        ),
    )(
        images.reshape(4, CHUNK, 64).transpose(0, 2, 1),
        cot.reshape(4, CHUNK, 64).transpose(0, 2, 1),
        g1,
        b1,
        wqkv.reshape(D, 192).T,
        qvb.reshape(1, 128),
        wo.reshape(64, D),
        outb,
        g2,
        b2,
        wup.reshape(D, 256),
        upb,
        wdn.reshape(256, D),
        downb,
    )
    outs = pl.pallas_call(
        finish,
        name="finish",
        out_shape=[jax.ShapeDtypeStruct(*x) for x in final],
        in_specs=[space] * 7,
        out_specs=[space] * 14,
    )(*outs)
    act, ig, og1, ob1, oqkv, oqvb, owo, ooutb, og2, ob2, oup, oupb, odn, odownb = outs
    return (
        act.transpose(0, 2, 1).reshape(1, 4, 1, CHUNK, 64),
        ig.transpose(0, 2, 1).reshape(1, 4, 1, CHUNK, 64),
        og1,
        ob1,
        oqkv.T.reshape(1, 256, 1, 192),
        oqvb.reshape(1, 1, 32),
        owo.reshape(1, 1, 64, 256),
        ooutb,
        og2,
        ob2,
        oup.reshape(1, 256, 256),
        oupb,
        odn.reshape(1, 256, 256),
        odownb,
    )


def solution(mesh):
    in_specs = (
        P(None, None, "dp", "tensor"),
        P(None, None, "dp", "tensor"),
        P("section", "tensor"),
        P("section", "tensor"),
        P("section", None, "tensor", None),
        P("section", "tensor", None),
        P("section", "tensor", None, None),
        P("section", "tensor"),
        P("section", "tensor"),
        P("section", "tensor"),
        P("section", None, "tensor"),
        P("section", "tensor"),
        P("section", "tensor", None),
        P("section", "tensor"),
    )
    out_specs = (
        P("section", None, None, "dp", "tensor"),
        P("section", None, None, "dp", "tensor"),
        P("section", ("tensor", "dp")),
        P("section", ("tensor", "dp")),
        P("section", "dp", "tensor", None),
        P("section", "tensor", "dp"),
        P("section", "tensor", None, "dp"),
        P("section", ("tensor", "dp")),
        P("section", ("tensor", "dp")),
        P("section", ("tensor", "dp")),
        P("section", "dp", "tensor"),
        P("section", ("tensor", "dp")),
        P("section", "tensor", "dp"),
        P("section", ("tensor", "dp")),
    )
    return jax.shard_map(body, mesh=mesh, in_specs=in_specs, out_specs=out_specs, check_vma=False)
```

```python
import jax
import jax.numpy as jnp
from jax import lax
from jax.experimental import pallas as pl
from jax.experimental.pallas import tpu as pltpu
from jax.sharding import PartitionSpec as P

BF = jnp.bfloat16
F32 = jnp.float32
D = 1024
TOK = 576
CHUNK = 144
epsilon = 1e-06

INPUTS = (
    "images",
    "cot",
    "g1",
    "b1",
    "wqkv",
    "qvb",
    "wo",
    "outb",
    "g2",
    "b2",
    "wup",
    "upb",
    "wdn",
    "downb",
)
OUTPUTS = ("o_act", "o_ig", "o_sums", "o_qkv", "o_wo", "o_up", "o_dn")


def vm(*shape, dtype=BF):
    return pltpu.VMEM(shape, dtype)


def dma(*shape):
    return pltpu.SemaphoreType.DMA(shape)


SCRATCH = dict(
    FB=vm(4, 80, 128),
    GX=vm(16, 4, 80, 128),
    BUF=vm(2, TOK, D),
    VB=vm(8, 128, dtype=F32),
    VG=vm(16, 8, 128, dtype=F32),
    VA=vm(8, D, dtype=F32),
    WO=vm(8, 2, 4, 16, D),
    A1=vm(TOK, D),
    Q=vm(TOK, 64),
    K=vm(TOK, 64),
    V=vm(TOK, 64),
    PR=vm(TOK, TOK, dtype=F32),
    PH=vm(TOK, TOK),
    DS=vm(TOK, TOK),
    O=vm(TOK, 64),
    GO=vm(16, 4, 80, 128),
    GA=vm(16, 4, 80, 128),
    OA=vm(TOK, D),
    HIDQ=vm(CHUNK, D, dtype=F32),
    WUQ=vm(4, D, 256),
    WDQ=vm(4, 256, D),
    UBQ=vm(4, 1, 256, dtype=F32),
    GPQ=vm(4, CHUNK, 256, dtype=F32),
    ZQ=vm(4, CHUNK, 256),
    DZQ=vm(4, CHUNK, 256, dtype=F32),
    PQ=vm(2, CHUNK, D),
    RQ=vm(2, 4, 48, D),
    A2=vm(TOK, D),
    GP=vm(TOK, 256, dtype=F32),
    Z=vm(TOK, 256),
    DU=vm(TOK, 256),
    YR=vm(48, D),
    P0=vm(TOK, D),
    P2=vm(TOK, D),
    SB=vm(2, 8, 48, D),
    PB=vm(2, 8, 48, D),
    RB=vm(2, 8, 48, D),
    DHID=vm(48, D, dtype=F32),
    DHR=vm(48, D),
    DOR=vm(48, D),
    DB=vm(TOK, 128),
    DO=vm(TOK, 64),
    DHF=vm(TOK, D),
    DQKV=vm(TOK, 192),
    IGR=vm(48, D),
    WU=vm(D, 256),
    WD=vm(256, D),
    WQ=vm(192, D),
    WG=vm(64, D),
    WUR=vm(4, 256, 256),
    WDR=vm(4, 256, 256),
    WQR=vm(4, 192, 256),
    WGR=vm(4, 64, 256),
    EA=vm(4, CHUNK, 128),
    EI=vm(4, CHUNK, 128),
    VS=vm(8, D, dtype=F32),
    VR=vm(16, 8, 128, dtype=F32),
    FV=vm(8, 256, dtype=F32),
    FR=vm(4, 8, 256, dtype=F32),
    m_z=dma(2, 4),
    m_x=dma(4, 8),
    m_v=dma(2, 16),
    m_wo=dma(4, 8),
    m_o=dma(2, 16),
    m_ga=dma(4, 8),
    m_go=dma(4, 8),
    m_wq=dma(4, 4),
    m_q0=dma(2, 4),
    m_q1=dma(2, 4),
    m_r0=dma(4, 8),
    m_r2=dma(4, 8),
    m_y=dma(4, 8),
    m_g=dma(4, 8),
    m_do=dma(2, 16),
    m_dh=dma(4, 8),
    m_ea=dma(2, 16),
    m_ei=dma(2, 16),
    m_vs=dma(2, 16),
    m_w=dma(8, 4),
    m_f=dma(2, 4),
    clear=pltpu.SemaphoreType.REGULAR,
)


def nn(a, b):
    return lax.dot_general(a, b, (((1,), (0,)), ((), ())), preferred_element_type=F32)


def nt(a, b):
    return lax.dot_general(a, b, (((1,), (1,)), ((), ())), preferred_element_type=F32)


def tn(a, b):
    return lax.dot_general(a, b, (((0,), (0,)), ((), ())), preferred_element_type=F32)


def loop(low, high, f):
    pl.loop(low, high)(f)


def quad_of(j):
    return lax.div(lax.rem(j, 8), 2)


def place_of(j):
    return 2 * lax.div(j, 8) + lax.rem(j, 2)


def member(quad, place):
    return 8 * lax.div(place, 2) + 2 * quad + lax.rem(place, 2)


def row_of(j):
    return pl.multiple_of(144 * quad_of(j) + 32 * place_of(j), 16)


def lane_of(j):
    return pl.multiple_of(128 * lax.div(j, 2), 128)


def sized(j, f):
    big = place_of(j) == 3
    pl.when(big)(lambda: f(48))
    pl.when(jnp.logical_not(big))(lambda: f(32))


def whole(j, f):
    f(None)


def norm(v):
    mu = jnp.mean(v, -1, keepdims=True)
    var = jnp.mean(v * v, -1, keepdims=True) - mu * mu
    rstd = lax.rsqrt(var + epsilon)
    return (v - mu) * rstd, rstd


def norm_back(g, xhat, rstd, gain):
    w = g * gain
    return rstd * (
        w - jnp.mean(w, -1, keepdims=True) - xhat * jnp.mean(w * xhat, -1, keepdims=True)
    )


class Refs:
    pass


def kernel(*refs):
    R = Refs()
    for name, ref in zip((*INPUTS, *OUTPUTS, *SCRATCH), refs):
        setattr(R, name, ref)
    s = lax.axis_index("section")
    t = lax.axis_index("tensor")
    z = lax.axis_index("dp")
    k = lax.div(t, 2)
    c = lax.rem(t, 2)
    zq = quad_of(t)
    p = place_of(t)
    me_row = row_of(t)
    drains = []

    def rc(src, dst, ss, rs, s2, t2, z2):
        return pltpu.make_async_remote_copy(
            src_ref=src,
            dst_ref=dst,
            send_sem=ss,
            recv_sem=rs,
            device_id={"section": s2, "tensor": t2, "dp": z2},
            device_id_type=pl.DeviceIdType.MESH,
        )

    def arrived(dst, rs):
        rc(dst, dst, rs, rs, s, 2 * k + 1 - c, z).wait_recv()

    def left(src, ss):
        rc(src, src, ss, ss, s, 2 * k + 1 - c, z).wait_send()

    def peers(f):
        def far(d):
            f(d, 8 * (1 - lax.div(t, 8)) + lax.rem(t + d, 8))

        def near(d):
            f(8 + d, 8 * lax.div(t, 8) + lax.rem(t + d, 8))

        loop(0, 8, far)
        loop(1, 8, near)

    def far_chips(f):
        loop(0, 4, lambda d: f(4 * (1 - lax.div(k, 4)) + lax.rem(k + d, 4)))

    def near_chips(f):
        loop(1, 4, lambda d: f(4 * lax.div(k, 4) + lax.rem(k + d, 4)))

    def other_chips(f):
        far_chips(f)
        near_chips(f)

    def chips_by_arrival(f):
        near_chips(f)
        far_chips(f)

    def all_chips(f):
        loop(0, 8, f)

    def quad_chips(f):
        loop(0, 2, lambda d: f(4 * d + zq))

    def rest_chips(f):
        loop(0, 6, lambda d: f(4 * lax.div(d, 3) + lax.rem(zq + 1 + lax.rem(d, 3), 4)))

    def per_core(f):
        pl.when(c == 0)(lambda: f(64, 80))
        pl.when(c == 1)(lambda: f(80, 64))

    def gather_start(src, dst, size, m, s2, chips):
        def go(k2):
            size(t, lambda n: rc(src(n), dst(t, n), m.at[0, 0], m.at[1, k], s2, 2 * k2 + c, z).start())

        chips(go)

    def forward_own(dst, m):
        here = dst(t, None)
        rc(here, here, m.at[2, 0], m.at[3, 0], s, 2 * k + 1 - c, z).start()

    def gather_forward(dst, size, m, chips, part=0):
        def go(k2):
            j = 2 * k2 + c

            def send(n):
                here = dst(j, n)
                arrived(here, m.at[1, k2])
                rc(here, here, m.at[2, 0], m.at[3, part], s, 2 * k + 1 - c, z).start()

            size(j, send)

        chips(go)

    def finish_rows(buf, m, quads, part=0):
        per_core(lambda mine, other: arrived(buf.at[pl.ds(0, other * quads)], m.at[3, part]))

    def drain_rows(buf, m, count):
        sized(t, lambda n: left(R.SB.at[0, pl.ds(0, count), pl.ds(0, n)], m.at[0, 0]))

    def drain_forward_rows(buf, m):
        per_core(lambda mine, other: left(buf.at[pl.ds(0, mine * 4)], m.at[2, 0]))

    def quad_start(i, m):
        def go(p2):
            t2 = member(zq, p2)
            sized(
                t2,
                lambda n: rc(
                    R.PQ.at[i, pl.ds(pl.multiple_of(32 * p2, 16), n)],
                    R.RQ.at[i, p, pl.ds(0, n)],
                    m.at[0, p2],
                    m.at[1, p],
                    s,
                    t2,
                    z,
                ).start(),
            )

        far = 2 - 2 * lax.div(p, 2)
        loop(0, 2, lambda d: go(far + lax.rem(c + d, 2)))
        go(2 - far + 1 - c)
        R.RQ[i, p] = R.PQ[i, pl.ds(pl.multiple_of(32 * p, 16), 48), :]

    def quad_finish(i, m):
        def go(d):
            p2 = lax.rem(p + d, 4)
            sized(t, lambda n: arrived(R.RQ.at[i, p2, pl.ds(0, n)], m.at[1, p2]))

        loop(1, 4, go)
        total = R.RQ[i, 0].astype(F32)
        for p2 in range(1, 4):
            total = total + R.RQ[i, p2].astype(F32)
        return total

    def quad_drain(i, m):
        def go(d):
            p2 = lax.rem(p + d, 4)
            sized(member(zq, p2), lambda n: left(R.PQ.at[i, pl.ds(0, n)], m.at[0, p2]))

        loop(1, 4, go)

    def reduce_over(part, i, m, compute):
        def sibling(q, d):
            k2 = 4 * d + q
            j = 2 * k2 + 1 - c
            sized(
                j,
                lambda n: rc(
                    part.at[pl.ds(row_of(j), n)],
                    R.SB.at[i, k2, pl.ds(0, n)],
                    m.at[0, 0],
                    m.at[1, k2],
                    s,
                    2 * k + 1 - c,
                    z,
                ).start(),
            )

        def mid(q, d):
            k2 = 4 * d + q
            j = 2 * k2 + c
            sized(j, lambda n: arrived(R.SB.at[i, k2, pl.ds(0, n)], m.at[1, k2]))
            both = part[pl.ds(row_of(j), 48), :].astype(F32) + R.SB[i, k2].astype(F32)
            R.PB[i, k2] = both.astype(BF)

            def send(n):
                rc(
                    R.PB.at[i, k2, pl.ds(0, n)],
                    R.RB.at[i, k, pl.ds(0, n)],
                    m.at[2, 0],
                    m.at[3, 0],
                    s,
                    j,
                    z,
                ).start()

            pl.when(k2 != k)(lambda: sized(j, send))

        def go(a):
            q = lax.rem(zq + 1 + a, 4)
            compute(q)
            loop(0, 2, lambda d: sibling(q, d))
            pl.when(a > 0)(lambda: loop(0, 2, lambda d: mid(lax.rem(zq + a, 4), d)))

        loop(0, 4, go)
        loop(0, 2, lambda d: mid(zq, d))

    def reduce_finish(i, m):
        sized(t, lambda n: arrived(R.RB.at[i, pl.ds(0, 7), pl.ds(0, n)], m.at[3, 0]))
        R.RB[i, k] = R.PB[i, k]
        total = R.RB[i, 0].astype(F32)
        for k2 in range(1, 8):
            total = total + R.RB[i, k2].astype(F32)
        return total

    def reduce_drain(part, i, m):
        per_core(lambda mine, other: left(part.at[pl.ds(0, other * 4)], m.at[0, 0]))
        per_core(
            lambda mine, other: sized(t, lambda n: left(part.at[pl.ds(0, mine * 4 - n)], m.at[2, 0]))
        )

    def emit(rows, E, m):
        def go(d, t2):
            def send(n):
                rc(
                    rows.at[pl.ds(0, n), pl.ds(lane_of(t2), 128)],
                    E.at[z, pl.ds(pl.multiple_of(32 * p, 16), n)],
                    m.at[0, 0],
                    m.at[1, 0],
                    s,
                    t2,
                    zq,
                ).start()

            sized(t, send)

        peers(go)
        pl.when(zq != z)(lambda: go(8, t))

        def local():
            def put(n):
                E[z, pl.ds(pl.multiple_of(32 * p, 16), n), :] = rows[
                    pl.ds(0, n), pl.ds(lane_of(t), 128)
                ]

            sized(t, put)

        pl.when(zq == z)(local)

    def emit_drain(rows, m):
        def taken(count):
            sized(t, lambda n: left(R.GX.at[pl.ds(0, count), 0, pl.ds(0, n)], m.at[0, 0]))

        pl.when(zq != z)(lambda: taken(16))
        pl.when(zq == z)(lambda: taken(15))

    def emit_finish(E, m, out):
        pl.when(zq != z)(lambda: arrived(E, m.at[1, 0]))
        pl.when(zq == z)(
            lambda: sized(t, lambda n: arrived(R.DB.at[pl.ds(0, TOK - n)], m.at[1, 0]))
        )

        @pl.when(c == 0)
        def _():
            for i in range(4):
                out[i] = E[i, :, 0:64].T

        @pl.when(c == 1)
        def _():
            for i in range(4):
                out[i] = E[i, :, 64:128].T

    bar = pltpu.get_barrier_semaphore()

    def greet(s2, t2, z2):
        pl.semaphore_signal(
            bar,
            inc=1,
            device_id={"section": s2, "tensor": t2, "dp": z2},
            device_id_type=pl.DeviceIdType.MESH,
        )

    loop(1, 16, lambda d: greet(s, lax.rem(t + d, 16), z))
    loop(1, 4, lambda d: greet(s, t, lax.rem(z + d, 4)))
    loop(0, 8, lambda d: greet(1 - s, 2 * d + c, z))

    def out_to(d):
        pl.when(jnp.logical_not(jnp.logical_and(d == t, zq == z)))(lambda: greet(s, d, zq))

    def out_from(d):
        t2 = member(z, lax.rem(d, 4))
        z2 = lax.div(d, 4)
        pl.when(jnp.logical_not(jnp.logical_and(t2 == t, z2 == z)))(lambda: greet(s, t2, z2))

    loop(0, 16, out_to)
    loop(0, 16, out_from)

    def pack(src):
        for m in range(4):
            R.FB[m, 64:80, :] = jnp.zeros((16, 128), BF)
            rows = src[m].T
            R.FB[m, :, 0:64] = rows[0:80, :]
            R.FB[m, 0:64, 64:128] = rows[80:144, :]

    pl.when(s == 0)(lambda: pack(R.images))
    pl.when(s == 1)(lambda: pack(R.cot))
    R.VB[...] = jnp.zeros((8, 128), F32)
    vecs = (R.g1, R.b1, R.g2, R.b2, R.outb, R.downb)

    @pl.when(c == 0)
    def _():
        for i, v in enumerate(vecs):
            R.VB[i : i + 1, 0:64] = v[...]

    @pl.when(c == 1)
    def _():
        for i, v in enumerate(vecs):
            R.VB[i : i + 1, 64:128] = v[...]

    R.VB[6:7, :] = R.upb[:, 0:128]
    R.VB[7:8, :] = R.upb[:, 128:256]
    R.VG[t] = R.VB[...]
    R.GX[t, z] = R.FB[z]
    R.WO[k, c, z] = R.wo[pl.ds(pl.multiple_of(16 * z, 16), 16), :]
    R.WUQ[zq] = R.wup[...]
    R.WDQ[zq] = R.wdn[...]
    R.FV[...] = jnp.zeros((8, 256), F32)
    R.VS[...] = jnp.zeros((8, D), F32)
    for i in range(4):
        R.GO[t, i, 64:80, :] = jnp.zeros((16, 128), BF)

    pl.semaphore_wait(bar, 58 - 2 * (zq == z).astype(jnp.int32))

    def z_send(d):
        z2 = lax.rem(z + d, 4)
        rc(R.FB.at[z2], R.GX.at[t, z], R.m_z.at[0, d], R.m_z.at[1, z], s, t, z2).start()

    loop(1, 4, z_send)

    def z_wait(d):
        z2 = lax.rem(z + d, 4)
        arrived(R.GX.at[t, z2], R.m_z.at[1, z2])

    loop(1, 4, z_wait)
    drains.append(lambda: loop(1, 4, lambda d: left(R.FB.at[0], R.m_z.at[0, d])))
    x_piece = lambda j, n: R.GX.at[j]
    def by_plane(f):
        pl.when(lax.rem(z, 2) == 0)(lambda: f(R.wup, R.WUQ, R.WDQ, 512))
        pl.when(lax.rem(z, 2) == 1)(lambda: f(R.wdn, R.WDQ, R.WUQ, 128))

    def quad_weights():
        def fetch(src, own, other, half):
            def go(d):
                t2 = member(lax.rem(zq + d, 4), p)
                rc(src, own.at[zq], R.m_wq.at[0, 0], R.m_wq.at[1, zq], s, t2, z).start()

            loop(1, 4, go)

        by_plane(fetch)

    def quad_weights_pass():
        def give(src, own, other, half):
            def go(d):
                g2 = lax.rem(zq + d, 4)
                arrived(own.at[g2], R.m_wq.at[1, g2])
                for first, z2 in ((0, lax.rem(z + 1, 4)), (half, lax.rem(z + 3, 4))):
                    piece = own.at[g2, pl.ds(first, half)]
                    rc(piece, piece, R.m_wq.at[2, 0], R.m_wq.at[3, 0], s, t, z2).start()

            loop(1, 4, go)

        by_plane(give)

    def quad_weights_wait():
        by_plane(lambda src, own, other, half: arrived(other.at[pl.ds(0, 3)], R.m_wq.at[3, 0]))

    def quad_weights_drain():
        def sent(src, own, other, half):
            left(own.at[pl.ds(0, 3)], R.m_wq.at[0, 0])
            left(own.at[pl.ds(0, 3)], R.m_wq.at[2, 0])

        by_plane(sent)

    def v_send(d, t2):
        rc(R.VB, R.VG.at[t], R.m_v.at[0, 0], R.m_v.at[1, 0], s, t2, z).start()

    @pl.when(s == 1)
    def _():
        quad_weights()
        quad_weights_pass()
        pl.semaphore_wait(R.clear, 1)

    gather_start(lambda n: R.GX.at[t], x_piece, whole, R.m_x, s, other_chips)
    forward_own(x_piece, R.m_x)
    peers(v_send)
    drains.append(lambda: left(R.VG.at[pl.ds(0, 15)], R.m_v.at[0, 0]))

    def wo_send(k2):
        here = R.WO.at[k, c, z]
        rc(here, here, R.m_wo.at[0, 0], R.m_wo.at[1, 0], s, 2 * k2 + c, z).start()

    other_chips(wo_send)
    gather_forward(x_piece, whole, R.m_x, chips_by_arrival)
    arrived(R.GX.at[pl.ds(0, 8)], R.m_x.at[3, 0])
    arrived(R.WO.at[pl.ds(0, 7), 0, 0], R.m_wo.at[1, 0])

    def wo_planes(d):
        here = R.WO.at[:, c, z]
        rc(here, here, R.m_wo.at[0, 1], R.m_wo.at[1, 1], s, t, lax.rem(z + d, 4)).start()

    loop(1, 4, wo_planes)
    arrived(R.VG.at[pl.ds(0, 15)], R.m_v.at[1, 0])
    for kk in range(8):
        R.VA[:, 128 * kk : 128 * kk + 128] = R.VG[2 * kk] + R.VG[2 * kk + 1]
    for g in range(4):
        R.UBQ[g, :, 0:128] = R.VG[member(g, p), 6:7, :]
        R.UBQ[g, :, 128:256] = R.VG[member(g, p), 7:8, :]
    gain1, bias1 = R.VA[0:1, :], R.VA[1:2, :]
    gain2, bias2 = R.VA[2:3, :], R.VA[3:4, :]
    out_bias, down_bias = R.VA[4:5, :], R.VA[5:6, :]

    def unpack(G, q, put):
        row = pl.multiple_of(144 * q, 16)
        for kk in range(8):
            a, b = G[2 * kk, q], G[2 * kk + 1, q]
            lanes = slice(128 * kk, 128 * kk + 128)
            put(pl.ds(row, 80), lanes, jnp.concatenate([a[:, :64], b[:, :64]], axis=1))
            put(
                pl.ds(row + 80, 64),
                lanes,
                jnp.concatenate([a[:64, 64:], b[:64, 64:]], axis=1),
            )

    def put_first(rows, lanes, v):
        R.BUF[s, rows, lanes] = v

    loop(0, 4, lambda q: unpack(R.GX, q, put_first))
    drains.append(lambda: left(R.GX.at[pl.ds(0, 7)], R.m_x.at[0, 0]))
    drains.append(lambda: left(R.GX.at[pl.ds(0, 8)], R.m_x.at[2, 0]))

    y_piece = lambda j, n: R.BUF.at[0, pl.ds(row_of(j), n)]
    g_piece = lambda j, n: R.BUF.at[1, pl.ds(row_of(j), n)]

    def quad_dz(g):
        dy = R.BUF[1, pl.ds(pl.multiple_of(CHUNK * zq, 16), CHUNK), :]
        R.DZQ[g] = nt(dy, R.WDQ[g])

    @pl.when(s == 1)
    def _():
        quad_weights_wait()
        loop(0, 4, quad_dz)
        gather_forward(y_piece, sized, R.m_y, all_chips)
        finish_rows(R.BUF.at[0], R.m_y, 4)

    def rows_at(i):
        return pl.ds(pl.multiple_of(CHUNK * i, 16), CHUNK)

    def project(i):
        rows = rows_at(i)
        xhat, _ = norm(R.BUF[0, rows, :].astype(F32))
        a = (xhat * gain1 + bias1).astype(BF)
        R.A1[rows, :] = a
        mixed = nt(a, R.wqkv[...])
        R.Q[rows, :] = (mixed[:, 0:64] + R.qvb[:, 0:64]).astype(BF) * jnp.asarray(0.125, BF)
        R.K[rows, :] = mixed[:, 64:128].astype(BF)
        R.V[rows, :] = (mixed[:, 128:192] + R.qvb[:, 64:128]).astype(BF)

    loop(0, 4, project)

    def attend(i):
        rows = rows_at(i)
        sc = nt(R.Q[rows, :], R.K[...])
        e = jnp.exp(sc - jnp.max(sc, -1, keepdims=True))
        prob = e * (1.0 / jnp.sum(e, -1, keepdims=True))
        R.PR[rows, :] = prob
        ph = prob.astype(BF)
        R.PH[rows, :] = ph
        o = nn(ph, R.V[...]).astype(BF)
        R.O[rows, :] = o
        R.GO[t, i, :, 0:64] = o[0:80, :]
        R.GO[t, i, 0:64, 64:128] = o[80:144, :]

    loop(0, 4, attend)
    o_piece = lambda j, n: R.GO.at[j]
    a_piece = lambda j, n: R.GA.at[j]

    def put_o(rows, lanes, v):
        R.OA[rows, lanes] = v

    def mid_norm(i):
        rows = rows_at(i)
        hidden = R.BUF[0, rows, :].astype(F32) + nn(R.OA[rows, :], R.WO[...].reshape(D, D)) + out_bias
        xhat, _ = norm(hidden)
        R.A2[rows, :] = (xhat * gain2 + bias2).astype(BF)

        @pl.when(i == zq)
        def _():
            R.HIDQ[...] = hidden

    def wo_cores():
        arrived(R.WO.at[:, 0, pl.ds(0, 3)], R.m_wo.at[1, 1])
        here = R.WO.at[:, c]
        rc(here, here, R.m_wo.at[2, 0], R.m_wo.at[3, 0], s, 2 * k + 1 - c, z).start()

    drains.append(lambda: left(R.WO.at[pl.ds(0, 7), 0, 0], R.m_wo.at[0, 0]))
    drains.append(lambda: left(R.WO.at[:, 0, pl.ds(0, 3)], R.m_wo.at[0, 1]))
    drains.append(lambda: left(R.WO.at[:, 0], R.m_wo.at[2, 0]))

    def expand(i):
        rows = rows_at(i)
        u = nn(R.A2[rows, :], R.wup[...]) + R.upb[...]
        half = 0.5 * (1.0 + lax.erf(u * 0.7071067811865476))
        R.Z[rows, :] = (u * half).astype(BF)
        R.GP[rows, :] = half + u * (0.3989422804014327 * jnp.exp(-0.5 * u * u))

    def quad_expand(g):
        u = nn(R.A2[rows_at(zq), :], R.WUQ[g]) + R.UBQ[g]
        half = 0.5 * (1.0 + lax.erf(u * 0.7071067811865476))
        R.ZQ[g] = (u * half).astype(BF)
        R.GPQ[g] = half + u * (0.3989422804014327 * jnp.exp(-0.5 * u * u))

    y_own = lambda n: R.YR.at[pl.ds(0, n)]
    me_quad = pl.ds(pl.multiple_of(32 * p, 16), 48)

    def contract(i):
        rows = rows_at(i)
        R.P0[rows, :] = nn(R.Z[rows, :], R.wdn[...]).astype(BF)

    def o_wide_start(piece, m):
        gather_start(lambda n: piece(t, n), piece, whole, m, s, other_chips)
        forward_own(piece, m)

    def o_wide_finish(piece, m):
        gather_forward(piece, whole, m, chips_by_arrival)
        arrived(R.GX.at[pl.ds(0, 8)], m.at[3, 0])

    @pl.when(s == 0)
    def _():
        o_wide_start(o_piece, R.m_go)
        wo_cores()
        o_wide_finish(o_piece, R.m_go)
        pl.semaphore_signal(
            R.clear,
            inc=1,
            device_id={"section": 1, "tensor": t, "dp": z},
            device_id_type=pl.DeviceIdType.MESH,
        )
        arrived(R.WO.at[:, 0], R.m_wo.at[3, 0])

        def forward_quad(q):
            unpack(R.GO, q, put_o)
            mid_norm(q)
            expand(q)
            contract(q)

        reduce_over(R.P0, 0, R.m_r0, forward_quad)
        total = reduce_finish(0, R.m_r0)
        R.YR[...] = (R.HIDQ[me_quad, :] + total + down_bias).astype(BF)
        gather_start(y_own, y_piece, sized, R.m_y, 1, all_chips)
        emit(R.YR, R.EA, R.m_ea)
        quad_weights()
        quad_weights_pass()
        quad_weights_wait()
        loop(0, 4, quad_expand)
        gather_forward(g_piece, sized, R.m_g, quad_chips)
        finish_rows(R.BUF.at[1], R.m_g, 1)
        loop(0, 4, quad_dz)

    @pl.when(s == 1)
    def _():
        def send(d, t2):
            g2 = quad_of(t2)
            rc(
                R.GO.at[t, g2], R.GO.at[t, g2], R.m_o.at[0, 0], R.m_o.at[1, 0], s, t2, z
            ).start()

        peers(send)
        wo_cores()
        arrived(R.WO.at[:, 0], R.m_wo.at[3, 0])
        arrived(R.GO.at[pl.ds(0, 15), 0], R.m_o.at[1, 0])
        unpack(R.GO, zq, put_o)
        mid_norm(zq)
        loop(0, 4, quad_expand)

    partial = None
    for g in range(4):
        du = (R.DZQ[g] * R.GPQ[g]).astype(BF)
        term = nt(du, R.WUQ[g])
        partial = term if partial is None else partial + term
    R.PQ[1] = partial.astype(BF)
    quad_start(1, R.m_q1)

    def cols(ref, z2):
        return ref.at[:, pl.ds(pl.multiple_of(256 * z2, 256), 256)]

    def lines(ref, z2):
        return ref.at[pl.ds(pl.multiple_of(256 * z2, 256), 256)]

    def weight_send(cut, stage, land, row):
        def go(d):
            z2 = lax.rem(z + d, 4)
            rc(
                cut(stage, z2), land.at[z], R.m_w.at[row, d], R.m_w.at[row + 1, z], s, t, z2
            ).start()

        loop(1, 4, go)
        land[z] = cut(stage, z)[...]

    def weight_drain(cut, stage, row):
        loop(1, 4, lambda d: left(cut(stage, 0), R.m_w.at[row, d]))

    def weight_finish(land, row, out):
        def go(d):
            z2 = lax.rem(z + d, 4)
            arrived(land.at[z2], R.m_w.at[row + 1, z2])

        loop(1, 4, go)
        total = land[0].astype(F32)
        for z2 in range(1, 4):
            total = total + land[z2].astype(F32)
        out[...] = total

    def back_units(i):
        rows = rows_at(i)
        R.DU[rows, :] = (nt(R.BUF[1, rows, :], R.wdn[...]) * R.GP[rows, :]).astype(BF)

    def mlp_grads():
        loop(0, 4, back_units)
        R.WU[...] = tn(R.A2[...], R.DU[...]).astype(BF)
        weight_send(lines, R.WU, R.WUR, 0)
        R.WD[...] = tn(R.Z[...], R.BUF[1]).astype(BF)
        weight_send(cols, R.WD, R.WDR, 2)
        R.FV[6:7, :] = jnp.sum(R.DU[...].astype(F32), axis=0, keepdims=True)

    valid = lax.broadcasted_iota(jnp.int32, (48, 1), 0) < jnp.where(p == 3, 48, 32)

    def over_rows(v):
        return jnp.sum(jnp.where(valid, v, 0.0), axis=0, keepdims=True)

    me_rows = pl.ds(me_row, 48)
    da2 = quad_finish(1, R.m_q1)
    xhat2b, rstd2 = norm(R.HIDQ[me_quad, :])
    R.VS[2:3, :] = over_rows(da2 * xhat2b)
    R.VS[3:4, :] = over_rows(da2)
    dhid = R.BUF[1, me_rows, :].astype(F32) + norm_back(da2, xhat2b, rstd2, gain2)
    R.DHID[...] = dhid
    R.DHR[...] = dhid.astype(BF)
    R.DOR[...] = nt(R.DHR[...], R.WO[...].reshape(D, D)).astype(BF)

    def do_send(d, t2):
        sized(
            t,
            lambda n: rc(
                R.DOR.at[pl.ds(0, n), pl.ds(lane_of(t2), 128)],
                R.DB.at[pl.ds(me_row, n)],
                R.m_do.at[0, 0],
                R.m_do.at[1, 0],
                s,
                t2,
                z,
            ).start(),
        )

    peers(do_send)

    drains.append(
        lambda: sized(t, lambda n: left(R.GX.at[pl.ds(0, 15), 0, pl.ds(0, n)], R.m_do.at[0, 0]))
    )

    def own_do(n):
        R.DB[pl.ds(me_row, n), :] = R.DOR[0:n, pl.ds(lane_of(t), 128)]
        R.DHF[pl.ds(me_row, n), :] = R.DHR[0:n, :]

    sized(t, own_do)
    dh_piece = lambda j, n: R.DHF.at[pl.ds(row_of(j), n)]
    dh_own = lambda n: R.DHR.at[pl.ds(0, n)]

    def forward_dh(n):
        here = dh_piece(t, n)
        rc(here, here, R.m_dh.at[2, 0], R.m_dh.at[3, 0], s, 2 * k + 1 - c, z).start()

    def dh_start():
        gather_start(dh_own, dh_piece, sized, R.m_dh, s, other_chips)
        sized(t, forward_dh)

    @pl.when(s == 1)
    def _():
        R.GA[t] = R.GO[t]
        o_wide_start(a_piece, R.m_ga)

    @pl.when(s == 0)
    def _():
        dh_start()
        gather_forward(g_piece, sized, R.m_g, rest_chips, 1)
        finish_rows(R.BUF.at[1], R.m_g, 3, 1)
        mlp_grads()

    sized(t, lambda n: arrived(R.DB.at[pl.ds(0, TOK - n)], R.m_do.at[1, 0]))
    @pl.when(c == 0)
    def _():
        R.DO[...] = R.DB[:, 0:64]

    @pl.when(c == 1)
    def _():
        R.DO[...] = R.DB[:, 64:128]

    def back_attend(i):
        rows = rows_at(i)
        dp = nt(R.DO[rows, :], R.V[...])
        prob = R.PR[rows, :]
        ds = (prob * (dp - jnp.sum(prob * dp, -1, keepdims=True))).astype(BF)
        R.DS[rows, :] = ds
        R.DQKV[rows, 0:64] = (nn(ds, R.K[...]) * 0.125).astype(BF)

    loop(0, 4, back_attend)
    R.DQKV[:, 64:128] = tn(R.Q[...], R.DS[...]).T.astype(BF)
    R.DQKV[:, 128:192] = tn(R.DO[...], R.PH[...]).T.astype(BF)

    def back_qkv(i):
        rows = rows_at(i)
        R.P2[rows, :] = nn(R.DQKV[rows, :], R.wqkv[...]).astype(BF)

    reduce_over(R.P2, 1, R.m_r2, back_qkv)

    def norm_sums(i):
        rows = rows_at(i)
        xhat, _ = norm(R.BUF[0, rows, :].astype(F32))
        g = R.P2[rows, :].astype(F32)
        R.VS[0:1, :] += jnp.sum(g * xhat, axis=0, keepdims=True)
        R.VS[1:2, :] += jnp.sum(g, axis=0, keepdims=True)

    def vector_sums():
        arrived(R.VR.at[pl.ds(0, 15)], R.m_vs.at[1, 0])
        mine = pl.ds(lane_of(t), 128)
        vec = R.VR[0]
        for t2 in range(1, 16):
            vec = vec + R.VR[t2]
        out_sum = jnp.sum(R.DHF[:, mine].astype(F32), axis=0, keepdims=True)
        down_sum = jnp.sum(R.BUF[1, :, mine].astype(F32), axis=0, keepdims=True)

        def place(lanes):
            R.FV[0:4, 0:64] = vec[0:4, lanes]
            R.FV[4:5, 0:64] = out_sum[:, lanes]
            R.FV[5:6, 0:64] = down_sum[:, lanes]

        pl.when(c == 0)(lambda: place(slice(0, 64)))
        pl.when(c == 1)(lambda: place(slice(64, 128)))

        def f_send(d):
            z2 = lax.rem(z + d, 4)
            rc(R.FV, R.FR.at[z], R.m_f.at[0, d], R.m_f.at[1, z], s, t, z2).start()

        loop(1, 4, f_send)
        R.FR[z] = R.FV[...]


    def s_send(d, t2):
        rc(
            R.VS.at[:, pl.ds(lane_of(t2), 128)],
            R.VR.at[t],
            R.m_vs.at[0, 0],
            R.m_vs.at[1, 0],
            s,
            t2,
            z,
        ).start()

    def side_work():
        loop(0, 4, norm_sums)
        peers(s_send)
        R.VR[t] = R.VS[:, pl.ds(lane_of(t), 128)]
        R.WQ[...] = tn(R.DQKV[...], R.A1[...]).astype(BF)
        weight_send(cols, R.WQ, R.WQR, 4)
        qkv_sum = jnp.sum(R.DQKV[...].astype(F32), axis=0, keepdims=True)
        R.FV[7:8, 0:64] = qkv_sum[:, 0:64]
        R.FV[7:8, 64:128] = qkv_sum[:, 128:192]
        gather_forward(dh_piece, sized, R.m_dh, chips_by_arrival)
        finish_rows(R.DHF, R.m_dh, 4)
        R.WG[...] = tn(R.O[...], R.DHF[...]).astype(BF)
        weight_send(cols, R.WG, R.WGR, 6)

    @pl.when(s == 1)
    def _():
        o_wide_finish(a_piece, R.m_ga)

        def forward_units(q):
            unpack(R.GA, q, put_o)
            mid_norm(q)
            expand(q)

        loop(0, 4, forward_units)
        mlp_grads()

    @pl.when(s == 0)
    def _():
        side_work()
        vector_sums()
        emit_finish(R.EA, R.m_ea, R.o_act)

    da1 = reduce_finish(1, R.m_r2)
    xhat1, rstd1 = norm(R.BUF[0, me_rows, :].astype(F32))
    R.IGR[...] = (R.DHID[...] + norm_back(da1, xhat1, rstd1, gain1)).astype(BF)
    g_own = lambda n: R.IGR.at[pl.ds(0, n)]

    @pl.when(s == 1)
    def _():
        gather_start(g_own, g_piece, sized, R.m_g, 0, quad_chips)
        gather_start(g_own, g_piece, sized, R.m_g, 0, rest_chips)

    emit(R.IGR, R.EI, R.m_ei)

    @pl.when(s == 1)
    def _():
        acc = None
        for g in range(4):
            term = nn(R.ZQ[g], R.WDQ[g])
            acc = term if acc is None else acc + term
        R.PQ[0] = acc.astype(BF)
        quad_start(0, R.m_q0)
        dh_start()
        total = quad_finish(0, R.m_q0)
        R.YR[...] = (R.HIDQ[me_quad, :] + total + down_bias).astype(BF)
        emit(R.YR, R.EA, R.m_ea)
        side_work()
        vector_sums()
        emit_finish(R.EA, R.m_ea, R.o_act)

    for f in drains:
        f()
    drain_rows(R.DHF, R.m_dh, 7)
    drain_forward_rows(R.DHF, R.m_dh)
    quad_drain(1, R.m_q1)
    quad_weights_drain()

    @pl.when(s == 0)
    def _():
        reduce_drain(R.P0, 0, R.m_r0)
        left(R.GX.at[pl.ds(0, 7)], R.m_go.at[0, 0])
        left(R.GX.at[pl.ds(0, 8)], R.m_go.at[2, 0])
        drain_rows(R.BUF.at[0], R.m_y, 8)
        drain_forward_rows(R.BUF.at[1], R.m_g)
        emit_drain(R.YR, R.m_ea)

    @pl.when(s == 1)
    def _():
        left(R.GO.at[pl.ds(0, 15), 0], R.m_o.at[0, 0])
        drain_forward_rows(R.BUF.at[0], R.m_y)

    weight_finish(R.WUR, 0, R.o_up)
    weight_finish(R.WDR, 2, R.o_dn)
    weight_finish(R.WQR, 4, R.o_qkv)
    weight_finish(R.WGR, 6, R.o_wo)

    def f_wait(d):
        z2 = lax.rem(z + d, 4)
        arrived(R.FR.at[z2], R.m_f.at[1, z2])

    loop(1, 4, f_wait)
    R.o_sums[...] = R.FR[0] + R.FR[1] + R.FR[2] + R.FR[3]
    emit_finish(R.EI, R.m_ei, R.o_ig)
    emit_drain(R.IGR, R.m_ei)
    reduce_drain(R.P2, 1, R.m_r2)
    left(R.VR.at[pl.ds(0, 15)], R.m_vs.at[0, 0])
    loop(1, 4, lambda d: left(R.FV, R.m_f.at[0, d]))
    weight_drain(lines, R.WU, 0)
    weight_drain(cols, R.WD, 2)
    weight_drain(cols, R.WQ, 4)
    weight_drain(cols, R.WG, 6)

    @pl.when(s == 1)
    def _():
        quad_drain(0, R.m_q0)
        left(R.GX.at[pl.ds(0, 7)], R.m_ga.at[0, 0])
        left(R.GX.at[pl.ds(0, 8)], R.m_ga.at[2, 0])
        drain_rows(R.BUF.at[1], R.m_g, 8)
        emit_drain(R.YR, R.m_ea)


def finish(*refs):
    act, ig, sums, qkv, wo, up, dn = refs[:7]
    act2, ig2, g1, b1, qkv2, qvb, wo2, outb, g2, b2, up2, upb, dn2, downb = refs[7:]
    z = lax.axis_index("dp")

    def own(row, width):
        out = sums[row : row + 1, 0:width]
        for z2 in range(1, 4):
            out = jnp.where(z == z2, sums[row : row + 1, z2 * width : (z2 + 1) * width], out)
        return out

    for row, out in enumerate((g1, b1, g2, b2, outb, downb)):
        out[...] = own(row, 16)
    upb[...] = own(6, 64)
    qvb[...] = own(7, 32)
    for a, b in ((act, act2), (ig, ig2), (qkv, qkv2), (wo, wo2), (up, up2), (dn, dn2)):
        b[...] = a[...]


def body(images, cot, g1, b1, wqkv, qvb, wo, outb, g2, b2, wup, upb, wdn, downb):
    flat = ((1, 16), F32)
    act = ((4, 64, CHUNK), BF)
    square = ((256, 256), F32)
    qkv, owo = ((192, 256), F32), ((64, 256), F32)
    kept = [act, act, ((8, 256), F32), qkv, owo, square, square]
    final = [act, act, flat, flat, qkv, ((1, 32), F32), owo]
    final += [flat, flat, flat, square, ((1, 64), F32), square, flat]
    space = pl.BlockSpec(memory_space=pltpu.VMEM)
    outs = pl.pallas_call(
        kernel,
        name="two_layers",
        out_shape=[jax.ShapeDtypeStruct(*x) for x in kept],
        in_specs=[space] * 14,
        out_specs=[space] * 7,
        scratch_shapes=list(SCRATCH.values()),
        compiler_params=pltpu.CompilerParams(
            collective_id=0, has_side_effects=True, vmem_limit_bytes=60 * 1024 * 1024
        ),
    )(
        images.reshape(4, CHUNK, 64).transpose(0, 2, 1),
        cot.reshape(4, CHUNK, 64).transpose(0, 2, 1),
        g1,
        b1,
        wqkv.reshape(D, 192).T,
        qvb.reshape(1, 128),
        wo.reshape(64, D),
        outb,
        g2,
        b2,
        wup.reshape(D, 256),
        upb,
        wdn.reshape(256, D),
        downb,
    )
    outs = pl.pallas_call(
        finish,
        name="finish",
        out_shape=[jax.ShapeDtypeStruct(*x) for x in final],
        in_specs=[space] * 7,
        out_specs=[space] * 14,
    )(*outs)
    act, ig, og1, ob1, oqkv, oqvb, owo, ooutb, og2, ob2, oup, oupb, odn, odownb = outs
    return (
        act.transpose(0, 2, 1).reshape(1, 4, 1, CHUNK, 64),
        ig.transpose(0, 2, 1).reshape(1, 4, 1, CHUNK, 64),
        og1,
        ob1,
        oqkv.T.reshape(1, 256, 1, 192),
        oqvb.reshape(1, 1, 32),
        owo.reshape(1, 1, 64, 256),
        ooutb,
        og2,
        ob2,
        oup.reshape(1, 256, 256),
        oupb,
        odn.reshape(1, 256, 256),
        odownb,
    )


def solution(mesh):
    in_specs = (
        P(None, None, "dp", "tensor"),
        P(None, None, "dp", "tensor"),
        P("section", "tensor"),
        P("section", "tensor"),
        P("section", None, "tensor", None),
        P("section", "tensor", None),
        P("section", "tensor", None, None),
        P("section", "tensor"),
        P("section", "tensor"),
        P("section", "tensor"),
        P("section", None, "tensor"),
        P("section", "tensor"),
        P("section", "tensor", None),
        P("section", "tensor"),
    )
    out_specs = (
        P("section", None, None, "dp", "tensor"),
        P("section", None, None, "dp", "tensor"),
        P("section", ("tensor", "dp")),
        P("section", ("tensor", "dp")),
        P("section", "dp", "tensor", None),
        P("section", "tensor", "dp"),
        P("section", "tensor", None, "dp"),
        P("section", ("tensor", "dp")),
        P("section", ("tensor", "dp")),
        P("section", ("tensor", "dp")),
        P("section", "dp", "tensor"),
        P("section", ("tensor", "dp")),
        P("section", "tensor", "dp"),
        P("section", ("tensor", "dp")),
    )
    return jax.shard_map(body, mesh=mesh, in_specs=in_specs, out_specs=out_specs, check_vma=False)
```

```python
import jax
import jax.numpy as jnp
from jax import lax
from jax.experimental import pallas as pl
from jax.experimental.pallas import tpu as pltpu
from jax.sharding import PartitionSpec as P

BF = jnp.bfloat16
F32 = jnp.float32
D = 1024
TOK = 576
CHUNK = 144
epsilon = 1e-06

INPUTS = (
    "images",
    "cot",
    "g1",
    "b1",
    "wqkv",
    "qvb",
    "wo",
    "outb",
    "g2",
    "b2",
    "wup",
    "upb",
    "wdn",
    "downb",
)
OUTPUTS = ("o_act", "o_ig", "o_sums", "o_qkv", "o_wo", "o_up", "o_dn")


def vm(*shape, dtype=BF):
    return pltpu.VMEM(shape, dtype)


def dma(*shape):
    return pltpu.SemaphoreType.DMA(shape)


SCRATCH = dict(
    FB=vm(4, 80, 128),
    GX=vm(16, 4, 80, 128),
    BUF=vm(2, TOK, D),
    VB=vm(8, 128, dtype=F32),
    VG=vm(16, 8, 128, dtype=F32),
    VA=vm(8, D, dtype=F32),
    WO=vm(8, 2, 4, 16, D),
    A1=vm(TOK, D),
    Q=vm(TOK, 64),
    K=vm(TOK, 64),
    V=vm(TOK, 64),
    PR=vm(TOK, TOK, dtype=F32),
    PH=vm(TOK, TOK),
    DS=vm(TOK, TOK),
    O=vm(TOK, 64),
    GO=vm(16, 4, 80, 128),
    GA=vm(16, 4, 80, 128),
    OA=vm(TOK, D),
    HIDQ=vm(CHUNK, D, dtype=F32),
    WUQ=vm(4, D, 256),
    WDQ=vm(4, 256, D),
    UBQ=vm(4, 1, 256, dtype=F32),
    GPQ=vm(4, CHUNK, 256, dtype=F32),
    ZQ=vm(4, CHUNK, 256),
    DZQ=vm(4, CHUNK, 256, dtype=F32),
    PQ=vm(2, CHUNK, D),
    RQ=vm(2, 4, 48, D),
    A2=vm(TOK, D),
    GP=vm(TOK, 256, dtype=F32),
    Z=vm(TOK, 256),
    DU=vm(TOK, 256),
    YR=vm(48, D),
    P0=vm(TOK, D),
    P2=vm(TOK, D),
    SB=vm(2, 8, 48, D),
    PB=vm(2, 8, 48, D),
    RB=vm(2, 8, 48, D),
    DHID=vm(48, D, dtype=F32),
    DHR=vm(48, D),
    DOR=vm(48, D),
    DB=vm(TOK, 128),
    DO=vm(TOK, 64),
    DHF=vm(TOK, D),
    DQKV=vm(TOK, 192),
    IGR=vm(48, D),
    WU=vm(D, 256),
    WD=vm(256, D),
    WQ=vm(192, D),
    WG=vm(64, D),
    WUR=vm(4, 256, 256),
    WDR=vm(4, 256, 256),
    WQR=vm(4, 192, 256),
    WGR=vm(4, 64, 256),
    EA=vm(4, CHUNK, 128),
    EI=vm(4, CHUNK, 128),
    VS=vm(8, D, dtype=F32),
    VR=vm(16, 8, 128, dtype=F32),
    FV=vm(8, 256, dtype=F32),
    FR=vm(4, 8, 256, dtype=F32),
    m_z=dma(2, 4),
    m_x=dma(4, 8),
    m_v=dma(2, 16),
    m_wo=dma(4, 8),
    m_o=dma(2, 16),
    m_ga=dma(4, 8),
    m_go=dma(4, 8),
    m_wq=dma(4, 4),
    m_q0=dma(2, 4),
    m_q1=dma(2, 4),
    m_r0=dma(4, 8),
    m_r2=dma(4, 8),
    m_y=dma(4, 8),
    m_g=dma(4, 8),
    m_do=dma(2, 16),
    m_dh=dma(4, 8),
    m_ea=dma(2, 16),
    m_ei=dma(2, 16),
    m_vs=dma(2, 16),
    m_w=dma(8, 4),
    m_f=dma(2, 4),
    clear=pltpu.SemaphoreType.REGULAR,
)


def nn(a, b):
    return lax.dot_general(a, b, (((1,), (0,)), ((), ())), preferred_element_type=F32)


def nt(a, b):
    return lax.dot_general(a, b, (((1,), (1,)), ((), ())), preferred_element_type=F32)


def tn(a, b):
    return lax.dot_general(a, b, (((0,), (0,)), ((), ())), preferred_element_type=F32)


def loop(low, high, f):
    pl.loop(low, high)(f)


def quad_of(j):
    return lax.div(lax.rem(j, 8), 2)


def place_of(j):
    return 2 * lax.div(j, 8) + lax.rem(j, 2)


def member(quad, place):
    return 8 * lax.div(place, 2) + 2 * quad + lax.rem(place, 2)


def row_of(j):
    return pl.multiple_of(144 * quad_of(j) + 32 * place_of(j), 16)


def lane_of(j):
    return pl.multiple_of(128 * lax.div(j, 2), 128)


def sized(j, f):
    big = place_of(j) == 3
    pl.when(big)(lambda: f(48))
    pl.when(jnp.logical_not(big))(lambda: f(32))


def whole(j, f):
    f(None)


def norm(v):
    mu = jnp.mean(v, -1, keepdims=True)
    var = jnp.mean(v * v, -1, keepdims=True) - mu * mu
    rstd = lax.rsqrt(var + epsilon)
    return (v - mu) * rstd, rstd


def norm_back(g, xhat, rstd, gain):
    w = g * gain
    return rstd * (
        w - jnp.mean(w, -1, keepdims=True) - xhat * jnp.mean(w * xhat, -1, keepdims=True)
    )


class Refs:
    pass


def kernel(*refs):
    R = Refs()
    for name, ref in zip((*INPUTS, *OUTPUTS, *SCRATCH), refs):
        setattr(R, name, ref)
    s = lax.axis_index("section")
    t = lax.axis_index("tensor")
    z = lax.axis_index("dp")
    k = lax.div(t, 2)
    c = lax.rem(t, 2)
    zq = quad_of(t)
    p = place_of(t)
    me_row = row_of(t)
    drains = []

    def rc(src, dst, ss, rs, s2, t2, z2):
        return pltpu.make_async_remote_copy(
            src_ref=src,
            dst_ref=dst,
            send_sem=ss,
            recv_sem=rs,
            device_id={"section": s2, "tensor": t2, "dp": z2},
            device_id_type=pl.DeviceIdType.MESH,
        )

    def arrived(dst, rs):
        rc(dst, dst, rs, rs, s, 2 * k + 1 - c, z).wait_recv()

    def left(src, ss):
        rc(src, src, ss, ss, s, 2 * k + 1 - c, z).wait_send()

    def peers(f):
        def far(d):
            f(d, 8 * (1 - lax.div(t, 8)) + lax.rem(t + d, 8))

        def near(d):
            f(8 + d, 8 * lax.div(t, 8) + lax.rem(t + d, 8))

        loop(0, 8, far)
        loop(1, 8, near)

    def far_chips(f):
        loop(0, 4, lambda d: f(4 * (1 - lax.div(k, 4)) + lax.rem(k + d, 4)))

    def near_chips(f):
        loop(1, 4, lambda d: f(4 * lax.div(k, 4) + lax.rem(k + d, 4)))

    def other_chips(f):
        far_chips(f)
        near_chips(f)

    def chips_by_arrival(f):
        near_chips(f)
        far_chips(f)

    def all_chips(f):
        loop(0, 8, f)

    def quad_chips(f):
        loop(0, 2, lambda d: f(4 * d + zq))

    def rest_chips(f):
        loop(0, 6, lambda d: f(4 * lax.div(d, 3) + lax.rem(zq + 1 + lax.rem(d, 3), 4)))

    def per_core(f):
        pl.when(c == 0)(lambda: f(64, 80))
        pl.when(c == 1)(lambda: f(80, 64))

    def gather_start(src, dst, size, m, s2, chips):
        def go(k2):
            size(t, lambda n: rc(src(n), dst(t, n), m.at[0, 0], m.at[1, k], s2, 2 * k2 + c, z).start())

        chips(go)

    def forward_own(dst, m):
        here = dst(t, None)
        rc(here, here, m.at[2, 0], m.at[3, 0], s, 2 * k + 1 - c, z).start()

    def gather_forward(dst, size, m, chips, part=0):
        def go(k2):
            j = 2 * k2 + c

            def send(n):
                here = dst(j, n)
                arrived(here, m.at[1, k2])
                rc(here, here, m.at[2, 0], m.at[3, part], s, 2 * k + 1 - c, z).start()

            size(j, send)

        chips(go)

    def finish_rows(buf, m, quads, part=0):
        per_core(lambda mine, other: arrived(buf.at[pl.ds(0, other * quads)], m.at[3, part]))

    def drain_rows(buf, m, count):
        sized(t, lambda n: left(R.SB.at[0, pl.ds(0, count), pl.ds(0, n)], m.at[0, 0]))

    def drain_forward_rows(buf, m):
        per_core(lambda mine, other: left(buf.at[pl.ds(0, mine * 4)], m.at[2, 0]))

    def quad_start(i, m):
        def go(p2):
            t2 = member(zq, p2)
            sized(
                t2,
                lambda n: rc(
                    R.PQ.at[i, pl.ds(pl.multiple_of(32 * p2, 16), n)],
                    R.RQ.at[i, p, pl.ds(0, n)],
                    m.at[0, p2],
                    m.at[1, p],
                    s,
                    t2,
                    z,
                ).start(),
            )

        far = 2 - 2 * lax.div(p, 2)
        loop(0, 2, lambda d: go(far + lax.rem(c + d, 2)))
        go(2 - far + 1 - c)
        R.RQ[i, p] = R.PQ[i, pl.ds(pl.multiple_of(32 * p, 16), 48), :]

    def quad_finish(i, m):
        def go(d):
            p2 = lax.rem(p + d, 4)
            sized(t, lambda n: arrived(R.RQ.at[i, p2, pl.ds(0, n)], m.at[1, p2]))

        loop(1, 4, go)
        total = R.RQ[i, 0].astype(F32)
        for p2 in range(1, 4):
            total = total + R.RQ[i, p2].astype(F32)
        return total

    def quad_drain(i, m):
        def go(d):
            p2 = lax.rem(p + d, 4)
            sized(member(zq, p2), lambda n: left(R.PQ.at[i, pl.ds(0, n)], m.at[0, p2]))

        loop(1, 4, go)

    def reduce_over(part, i, m, compute):
        def sibling(q, d):
            k2 = 4 * d + q
            j = 2 * k2 + 1 - c
            sized(
                j,
                lambda n: rc(
                    part.at[pl.ds(row_of(j), n)],
                    R.SB.at[i, k2, pl.ds(0, n)],
                    m.at[0, 0],
                    m.at[1, k2],
                    s,
                    2 * k + 1 - c,
                    z,
                ).start(),
            )

        def mid(q, d):
            k2 = 4 * d + q
            j = 2 * k2 + c
            sized(j, lambda n: arrived(R.SB.at[i, k2, pl.ds(0, n)], m.at[1, k2]))
            both = part[pl.ds(row_of(j), 48), :].astype(F32) + R.SB[i, k2].astype(F32)
            R.PB[i, k2] = both.astype(BF)

            def send(n):
                rc(
                    R.PB.at[i, k2, pl.ds(0, n)],
                    R.RB.at[i, k, pl.ds(0, n)],
                    m.at[2, 0],
                    m.at[3, 0],
                    s,
                    j,
                    z,
                ).start()

            pl.when(k2 != k)(lambda: sized(j, send))

        def go(a):
            q = lax.rem(zq + 1 + a, 4)
            compute(q)
            loop(0, 2, lambda d: sibling(q, d))
            pl.when(a > 0)(lambda: loop(0, 2, lambda d: mid(lax.rem(zq + a, 4), d)))

        loop(0, 4, go)
        loop(0, 2, lambda d: mid(zq, d))

    def reduce_finish(i, m):
        sized(t, lambda n: arrived(R.RB.at[i, pl.ds(0, 7), pl.ds(0, n)], m.at[3, 0]))
        R.RB[i, k] = R.PB[i, k]
        total = R.RB[i, 0].astype(F32)
        for k2 in range(1, 8):
            total = total + R.RB[i, k2].astype(F32)
        return total

    def reduce_drain(part, i, m):
        per_core(lambda mine, other: left(part.at[pl.ds(0, other * 4)], m.at[0, 0]))
        per_core(
            lambda mine, other: sized(t, lambda n: left(part.at[pl.ds(0, mine * 4 - n)], m.at[2, 0]))
        )

    def emit(rows, E, m):
        def go(d, t2):
            def send(n):
                rc(
                    rows.at[pl.ds(0, n), pl.ds(lane_of(t2), 128)],
                    E.at[z, pl.ds(pl.multiple_of(32 * p, 16), n)],
                    m.at[0, 0],
                    m.at[1, 0],
                    s,
                    t2,
                    zq,
                ).start()

            sized(t, send)

        peers(go)
        pl.when(zq != z)(lambda: go(8, t))

        def local():
            def put(n):
                E[z, pl.ds(pl.multiple_of(32 * p, 16), n), :] = rows[
                    pl.ds(0, n), pl.ds(lane_of(t), 128)
                ]

            sized(t, put)

        pl.when(zq == z)(local)

    def emit_drain(rows, m):
        def taken(count):
            sized(t, lambda n: left(R.GX.at[pl.ds(0, count), 0, pl.ds(0, n)], m.at[0, 0]))

        pl.when(zq != z)(lambda: taken(16))
        pl.when(zq == z)(lambda: taken(15))

    def emit_finish(E, m, out):
        pl.when(zq != z)(lambda: arrived(E, m.at[1, 0]))
        pl.when(zq == z)(
            lambda: sized(t, lambda n: arrived(R.DB.at[pl.ds(0, TOK - n)], m.at[1, 0]))
        )

        @pl.when(c == 0)
        def _():
            for i in range(4):
                out[i] = E[i, :, 0:64].T

        @pl.when(c == 1)
        def _():
            for i in range(4):
                out[i] = E[i, :, 64:128].T

    bar = pltpu.get_barrier_semaphore()

    def greet(s2, t2, z2):
        pl.semaphore_signal(
            bar,
            inc=1,
            device_id={"section": s2, "tensor": t2, "dp": z2},
            device_id_type=pl.DeviceIdType.MESH,
        )

    loop(1, 16, lambda d: greet(s, lax.rem(t + d, 16), z))
    loop(1, 4, lambda d: greet(s, t, lax.rem(z + d, 4)))
    loop(0, 8, lambda d: greet(1 - s, 2 * d + c, z))

    def pack(src):
        for m in range(4):
            R.FB[m, 64:80, :] = jnp.zeros((16, 128), BF)
            rows = src[m].T
            R.FB[m, :, 0:64] = rows[0:80, :]
            R.FB[m, 0:64, 64:128] = rows[80:144, :]

    pl.when(s == 0)(lambda: pack(R.images))
    pl.when(s == 1)(lambda: pack(R.cot))
    R.VB[...] = jnp.zeros((8, 128), F32)
    vecs = (R.g1, R.b1, R.g2, R.b2, R.outb, R.downb)

    @pl.when(c == 0)
    def _():
        for i, v in enumerate(vecs):
            R.VB[i : i + 1, 0:64] = v[...]

    @pl.when(c == 1)
    def _():
        for i, v in enumerate(vecs):
            R.VB[i : i + 1, 64:128] = v[...]

    R.VB[6:7, :] = R.upb[:, 0:128]
    R.VB[7:8, :] = R.upb[:, 128:256]
    R.VG[t] = R.VB[...]
    R.GX[t, z] = R.FB[z]
    R.WO[k, c, z] = R.wo[pl.ds(pl.multiple_of(16 * z, 16), 16), :]
    R.WUQ[zq] = R.wup[...]
    R.WDQ[zq] = R.wdn[...]
    R.FV[...] = jnp.zeros((8, 256), F32)
    R.VS[...] = jnp.zeros((8, D), F32)
    for i in range(4):
        R.GO[t, i, 64:80, :] = jnp.zeros((16, 128), BF)

    pl.semaphore_wait(bar, 26)

    def z_send(d):
        z2 = lax.rem(z + d, 4)
        rc(R.FB.at[z2], R.GX.at[t, z], R.m_z.at[0, d], R.m_z.at[1, z], s, t, z2).start()

    loop(1, 4, z_send)

    def z_wait(d):
        z2 = lax.rem(z + d, 4)
        arrived(R.GX.at[t, z2], R.m_z.at[1, z2])

    loop(1, 4, z_wait)
    drains.append(lambda: loop(1, 4, lambda d: left(R.FB.at[0], R.m_z.at[0, d])))
    x_piece = lambda j, n: R.GX.at[j]
    def by_plane(f):
        pl.when(lax.rem(z, 2) == 0)(lambda: f(R.wup, R.WUQ, R.WDQ, 512))
        pl.when(lax.rem(z, 2) == 1)(lambda: f(R.wdn, R.WDQ, R.WUQ, 128))

    def quad_weights():
        def fetch(src, own, other, half):
            def go(d):
                t2 = member(lax.rem(zq + d, 4), p)
                rc(src, own.at[zq], R.m_wq.at[0, 0], R.m_wq.at[1, zq], s, t2, z).start()

            loop(1, 4, go)

        by_plane(fetch)

    def quad_weights_pass():
        def give(src, own, other, half):
            def go(d):
                g2 = lax.rem(zq + d, 4)
                arrived(own.at[g2], R.m_wq.at[1, g2])
                for first, z2 in ((0, lax.rem(z + 1, 4)), (half, lax.rem(z + 3, 4))):
                    piece = own.at[g2, pl.ds(first, half)]
                    rc(piece, piece, R.m_wq.at[2, 0], R.m_wq.at[3, 0], s, t, z2).start()

            loop(1, 4, go)

        by_plane(give)

    def quad_weights_wait():
        by_plane(lambda src, own, other, half: arrived(other.at[pl.ds(0, 3)], R.m_wq.at[3, 0]))

    def quad_weights_drain():
        def sent(src, own, other, half):
            left(own.at[pl.ds(0, 3)], R.m_wq.at[0, 0])
            left(own.at[pl.ds(0, 3)], R.m_wq.at[2, 0])

        by_plane(sent)

    def v_send(d, t2):
        rc(R.VB, R.VG.at[t], R.m_v.at[0, 0], R.m_v.at[1, 0], s, t2, z).start()

    @pl.when(s == 1)
    def _():
        quad_weights()
        quad_weights_pass()
        pl.semaphore_wait(R.clear, 1)

    gather_start(lambda n: R.GX.at[t], x_piece, whole, R.m_x, s, other_chips)
    forward_own(x_piece, R.m_x)
    peers(v_send)
    drains.append(lambda: left(R.VG.at[pl.ds(0, 15)], R.m_v.at[0, 0]))

    def wo_send(k2):
        here = R.WO.at[k, c, z]
        rc(here, here, R.m_wo.at[0, 0], R.m_wo.at[1, 0], s, 2 * k2 + c, z).start()

    other_chips(wo_send)
    gather_forward(x_piece, whole, R.m_x, chips_by_arrival)
    arrived(R.GX.at[pl.ds(0, 8)], R.m_x.at[3, 0])
    arrived(R.WO.at[pl.ds(0, 7), 0, 0], R.m_wo.at[1, 0])

    def wo_planes(d):
        here = R.WO.at[:, c, z]
        rc(here, here, R.m_wo.at[0, 1], R.m_wo.at[1, 1], s, t, lax.rem(z + d, 4)).start()

    loop(1, 4, wo_planes)
    arrived(R.VG.at[pl.ds(0, 15)], R.m_v.at[1, 0])
    for kk in range(8):
        R.VA[:, 128 * kk : 128 * kk + 128] = R.VG[2 * kk] + R.VG[2 * kk + 1]
    for g in range(4):
        R.UBQ[g, :, 0:128] = R.VG[member(g, p), 6:7, :]
        R.UBQ[g, :, 128:256] = R.VG[member(g, p), 7:8, :]
    gain1, bias1 = R.VA[0:1, :], R.VA[1:2, :]
    gain2, bias2 = R.VA[2:3, :], R.VA[3:4, :]
    out_bias, down_bias = R.VA[4:5, :], R.VA[5:6, :]

    def unpack(G, q, put):
        row = pl.multiple_of(144 * q, 16)
        for kk in range(8):
            a, b = G[2 * kk, q], G[2 * kk + 1, q]
            lanes = slice(128 * kk, 128 * kk + 128)
            put(pl.ds(row, 80), lanes, jnp.concatenate([a[:, :64], b[:, :64]], axis=1))
            put(
                pl.ds(row + 80, 64),
                lanes,
                jnp.concatenate([a[:64, 64:], b[:64, 64:]], axis=1),
            )

    def put_first(rows, lanes, v):
        R.BUF[s, rows, lanes] = v

    loop(0, 4, lambda q: unpack(R.GX, q, put_first))
    drains.append(lambda: left(R.GX.at[pl.ds(0, 7)], R.m_x.at[0, 0]))
    drains.append(lambda: left(R.GX.at[pl.ds(0, 8)], R.m_x.at[2, 0]))

    y_piece = lambda j, n: R.BUF.at[0, pl.ds(row_of(j), n)]
    g_piece = lambda j, n: R.BUF.at[1, pl.ds(row_of(j), n)]

    def quad_dz(g):
        dy = R.BUF[1, pl.ds(pl.multiple_of(CHUNK * zq, 16), CHUNK), :]
        R.DZQ[g] = nt(dy, R.WDQ[g])

    @pl.when(s == 1)
    def _():
        quad_weights_wait()
        loop(0, 4, quad_dz)
        gather_forward(y_piece, sized, R.m_y, all_chips)
        finish_rows(R.BUF.at[0], R.m_y, 4)

    def rows_at(i):
        return pl.ds(pl.multiple_of(CHUNK * i, 16), CHUNK)

    def project(i):
        rows = rows_at(i)
        xhat, _ = norm(R.BUF[0, rows, :].astype(F32))
        a = (xhat * gain1 + bias1).astype(BF)
        R.A1[rows, :] = a
        mixed = nt(a, R.wqkv[...])
        R.Q[rows, :] = (mixed[:, 0:64] + R.qvb[:, 0:64]).astype(BF) * jnp.asarray(0.125, BF)
        R.K[rows, :] = mixed[:, 64:128].astype(BF)
        R.V[rows, :] = (mixed[:, 128:192] + R.qvb[:, 64:128]).astype(BF)

    loop(0, 4, project)

    def attend(i):
        rows = rows_at(i)
        sc = nt(R.Q[rows, :], R.K[...])
        e = jnp.exp(sc - jnp.max(sc, -1, keepdims=True))
        prob = e * (1.0 / jnp.sum(e, -1, keepdims=True))
        R.PR[rows, :] = prob
        ph = prob.astype(BF)
        R.PH[rows, :] = ph
        o = nn(ph, R.V[...]).astype(BF)
        R.O[rows, :] = o
        R.GO[t, i, :, 0:64] = o[0:80, :]
        R.GO[t, i, 0:64, 64:128] = o[80:144, :]

    loop(0, 4, attend)
    o_piece = lambda j, n: R.GO.at[j]
    a_piece = lambda j, n: R.GA.at[j]

    def put_o(rows, lanes, v):
        R.OA[rows, lanes] = v

    def mid_norm(i):
        rows = rows_at(i)
        hidden = R.BUF[0, rows, :].astype(F32) + nn(R.OA[rows, :], R.WO[...].reshape(D, D)) + out_bias
        xhat, _ = norm(hidden)
        R.A2[rows, :] = (xhat * gain2 + bias2).astype(BF)

        @pl.when(i == zq)
        def _():
            R.HIDQ[...] = hidden

    def wo_cores():
        arrived(R.WO.at[:, 0, pl.ds(0, 3)], R.m_wo.at[1, 1])
        here = R.WO.at[:, c]
        rc(here, here, R.m_wo.at[2, 0], R.m_wo.at[3, 0], s, 2 * k + 1 - c, z).start()

    drains.append(lambda: left(R.WO.at[pl.ds(0, 7), 0, 0], R.m_wo.at[0, 0]))
    drains.append(lambda: left(R.WO.at[:, 0, pl.ds(0, 3)], R.m_wo.at[0, 1]))
    drains.append(lambda: left(R.WO.at[:, 0], R.m_wo.at[2, 0]))

    def expand(i):
        rows = rows_at(i)
        u = nn(R.A2[rows, :], R.wup[...]) + R.upb[...]
        half = 0.5 * (1.0 + lax.erf(u * 0.7071067811865476))
        R.Z[rows, :] = (u * half).astype(BF)
        R.GP[rows, :] = half + u * (0.3989422804014327 * jnp.exp(-0.5 * u * u))

    def quad_expand(g):
        u = nn(R.A2[rows_at(zq), :], R.WUQ[g]) + R.UBQ[g]
        half = 0.5 * (1.0 + lax.erf(u * 0.7071067811865476))
        R.ZQ[g] = (u * half).astype(BF)
        R.GPQ[g] = half + u * (0.3989422804014327 * jnp.exp(-0.5 * u * u))

    y_own = lambda n: R.YR.at[pl.ds(0, n)]
    me_quad = pl.ds(pl.multiple_of(32 * p, 16), 48)

    def contract(i):
        rows = rows_at(i)
        R.P0[rows, :] = nn(R.Z[rows, :], R.wdn[...]).astype(BF)

    def o_wide_start(piece, m):
        gather_start(lambda n: piece(t, n), piece, whole, m, s, other_chips)
        forward_own(piece, m)

    def o_wide_finish(piece, m):
        gather_forward(piece, whole, m, chips_by_arrival)
        arrived(R.GX.at[pl.ds(0, 8)], m.at[3, 0])

    @pl.when(s == 0)
    def _():
        o_wide_start(o_piece, R.m_go)
        wo_cores()
        o_wide_finish(o_piece, R.m_go)
        pl.semaphore_signal(
            R.clear,
            inc=1,
            device_id={"section": 1, "tensor": t, "dp": z},
            device_id_type=pl.DeviceIdType.MESH,
        )
        arrived(R.WO.at[:, 0], R.m_wo.at[3, 0])

        def forward_quad(q):
            unpack(R.GO, q, put_o)
            mid_norm(q)
            expand(q)
            contract(q)

        reduce_over(R.P0, 0, R.m_r0, forward_quad)
        total = reduce_finish(0, R.m_r0)
        R.YR[...] = (R.HIDQ[me_quad, :] + total + down_bias).astype(BF)
        gather_start(y_own, y_piece, sized, R.m_y, 1, all_chips)
        emit(R.YR, R.EA, R.m_ea)
        quad_weights()
        quad_weights_pass()
        quad_weights_wait()
        loop(0, 4, quad_expand)
        gather_forward(g_piece, sized, R.m_g, quad_chips)
        finish_rows(R.BUF.at[1], R.m_g, 1)
        loop(0, 4, quad_dz)

    @pl.when(s == 1)
    def _():
        def send(d, t2):
            g2 = quad_of(t2)
            rc(
                R.GO.at[t, g2], R.GO.at[t, g2], R.m_o.at[0, 0], R.m_o.at[1, 0], s, t2, z
            ).start()

        peers(send)
        wo_cores()
        arrived(R.WO.at[:, 0], R.m_wo.at[3, 0])
        arrived(R.GO.at[pl.ds(0, 15), 0], R.m_o.at[1, 0])
        unpack(R.GO, zq, put_o)
        mid_norm(zq)
        loop(0, 4, quad_expand)

    partial = None
    for g in range(4):
        du = (R.DZQ[g] * R.GPQ[g]).astype(BF)
        term = nt(du, R.WUQ[g])
        partial = term if partial is None else partial + term
    R.PQ[1] = partial.astype(BF)
    quad_start(1, R.m_q1)

    def cols(ref, z2):
        return ref.at[:, pl.ds(pl.multiple_of(256 * z2, 256), 256)]

    def lines(ref, z2):
        return ref.at[pl.ds(pl.multiple_of(256 * z2, 256), 256)]

    def weight_send(cut, stage, land, row):
        def go(d):
            z2 = lax.rem(z + d, 4)
            rc(
                cut(stage, z2), land.at[z], R.m_w.at[row, d], R.m_w.at[row + 1, z], s, t, z2
            ).start()

        loop(1, 4, go)
        land[z] = cut(stage, z)[...]

    def weight_drain(cut, stage, row):
        loop(1, 4, lambda d: left(cut(stage, 0), R.m_w.at[row, d]))

    def weight_finish(land, row, out):
        def go(d):
            z2 = lax.rem(z + d, 4)
            arrived(land.at[z2], R.m_w.at[row + 1, z2])

        loop(1, 4, go)
        total = land[0].astype(F32)
        for z2 in range(1, 4):
            total = total + land[z2].astype(F32)
        out[...] = total

    def back_units(i):
        rows = rows_at(i)
        R.DU[rows, :] = (nt(R.BUF[1, rows, :], R.wdn[...]) * R.GP[rows, :]).astype(BF)

    def mlp_grads():
        loop(0, 4, back_units)
        R.WU[...] = tn(R.A2[...], R.DU[...]).astype(BF)
        weight_send(lines, R.WU, R.WUR, 0)
        R.WD[...] = tn(R.Z[...], R.BUF[1]).astype(BF)
        weight_send(cols, R.WD, R.WDR, 2)
        R.FV[6:7, :] = jnp.sum(R.DU[...].astype(F32), axis=0, keepdims=True)

    valid = lax.broadcasted_iota(jnp.int32, (48, 1), 0) < jnp.where(p == 3, 48, 32)

    def over_rows(v):
        return jnp.sum(jnp.where(valid, v, 0.0), axis=0, keepdims=True)

    me_rows = pl.ds(me_row, 48)
    da2 = quad_finish(1, R.m_q1)
    xhat2b, rstd2 = norm(R.HIDQ[me_quad, :])
    R.VS[2:3, :] = over_rows(da2 * xhat2b)
    R.VS[3:4, :] = over_rows(da2)
    dhid = R.BUF[1, me_rows, :].astype(F32) + norm_back(da2, xhat2b, rstd2, gain2)
    R.DHID[...] = dhid
    R.DHR[...] = dhid.astype(BF)
    R.DOR[...] = nt(R.DHR[...], R.WO[...].reshape(D, D)).astype(BF)

    def do_send(d, t2):
        sized(
            t,
            lambda n: rc(
                R.DOR.at[pl.ds(0, n), pl.ds(lane_of(t2), 128)],
                R.DB.at[pl.ds(me_row, n)],
                R.m_do.at[0, 0],
                R.m_do.at[1, 0],
                s,
                t2,
                z,
            ).start(),
        )

    peers(do_send)

    drains.append(
        lambda: sized(t, lambda n: left(R.GX.at[pl.ds(0, 15), 0, pl.ds(0, n)], R.m_do.at[0, 0]))
    )

    def own_do(n):
        R.DB[pl.ds(me_row, n), :] = R.DOR[0:n, pl.ds(lane_of(t), 128)]
        R.DHF[pl.ds(me_row, n), :] = R.DHR[0:n, :]

    sized(t, own_do)
    dh_piece = lambda j, n: R.DHF.at[pl.ds(row_of(j), n)]
    dh_own = lambda n: R.DHR.at[pl.ds(0, n)]

    def forward_dh(n):
        here = dh_piece(t, n)
        rc(here, here, R.m_dh.at[2, 0], R.m_dh.at[3, 0], s, 2 * k + 1 - c, z).start()

    def dh_start():
        gather_start(dh_own, dh_piece, sized, R.m_dh, s, other_chips)
        sized(t, forward_dh)

    @pl.when(s == 1)
    def _():
        R.GA[t] = R.GO[t]
        o_wide_start(a_piece, R.m_ga)

    @pl.when(s == 0)
    def _():
        dh_start()
        gather_forward(g_piece, sized, R.m_g, rest_chips, 1)
        finish_rows(R.BUF.at[1], R.m_g, 3, 1)
        mlp_grads()

    sized(t, lambda n: arrived(R.DB.at[pl.ds(0, TOK - n)], R.m_do.at[1, 0]))
    @pl.when(c == 0)
    def _():
        R.DO[...] = R.DB[:, 0:64]

    @pl.when(c == 1)
    def _():
        R.DO[...] = R.DB[:, 64:128]

    def back_attend(i):
        rows = rows_at(i)
        dp = nt(R.DO[rows, :], R.V[...])
        prob = R.PR[rows, :]
        ds = (prob * (dp - jnp.sum(prob * dp, -1, keepdims=True))).astype(BF)
        R.DS[rows, :] = ds
        R.DQKV[rows, 0:64] = (nn(ds, R.K[...]) * 0.125).astype(BF)

    loop(0, 4, back_attend)
    R.DQKV[:, 64:128] = tn(R.Q[...], R.DS[...]).T.astype(BF)
    R.DQKV[:, 128:192] = tn(R.DO[...], R.PH[...]).T.astype(BF)

    def back_qkv(i):
        rows = rows_at(i)
        R.P2[rows, :] = nn(R.DQKV[rows, :], R.wqkv[...]).astype(BF)

    reduce_over(R.P2, 1, R.m_r2, back_qkv)

    def norm_sums(i):
        rows = rows_at(i)
        xhat, _ = norm(R.BUF[0, rows, :].astype(F32))
        g = R.P2[rows, :].astype(F32)
        R.VS[0:1, :] += jnp.sum(g * xhat, axis=0, keepdims=True)
        R.VS[1:2, :] += jnp.sum(g, axis=0, keepdims=True)

    def vector_sums():
        arrived(R.VR.at[pl.ds(0, 15)], R.m_vs.at[1, 0])
        mine = pl.ds(lane_of(t), 128)
        vec = R.VR[0]
        for t2 in range(1, 16):
            vec = vec + R.VR[t2]
        out_sum = jnp.sum(R.DHF[:, mine].astype(F32), axis=0, keepdims=True)
        down_sum = jnp.sum(R.BUF[1, :, mine].astype(F32), axis=0, keepdims=True)

        def place(lanes):
            R.FV[0:4, 0:64] = vec[0:4, lanes]
            R.FV[4:5, 0:64] = out_sum[:, lanes]
            R.FV[5:6, 0:64] = down_sum[:, lanes]

        pl.when(c == 0)(lambda: place(slice(0, 64)))
        pl.when(c == 1)(lambda: place(slice(64, 128)))

        def f_send(d):
            z2 = lax.rem(z + d, 4)
            rc(R.FV, R.FR.at[z], R.m_f.at[0, d], R.m_f.at[1, z], s, t, z2).start()

        loop(1, 4, f_send)
        R.FR[z] = R.FV[...]


    def s_send(d, t2):
        rc(
            R.VS.at[:, pl.ds(lane_of(t2), 128)],
            R.VR.at[t],
            R.m_vs.at[0, 0],
            R.m_vs.at[1, 0],
            s,
            t2,
            z,
        ).start()

    def side_work():
        loop(0, 4, norm_sums)
        peers(s_send)
        R.VR[t] = R.VS[:, pl.ds(lane_of(t), 128)]
        R.WQ[...] = tn(R.DQKV[...], R.A1[...]).astype(BF)
        weight_send(cols, R.WQ, R.WQR, 4)
        qkv_sum = jnp.sum(R.DQKV[...].astype(F32), axis=0, keepdims=True)
        R.FV[7:8, 0:64] = qkv_sum[:, 0:64]
        R.FV[7:8, 64:128] = qkv_sum[:, 128:192]
        gather_forward(dh_piece, sized, R.m_dh, chips_by_arrival)
        finish_rows(R.DHF, R.m_dh, 4)
        R.WG[...] = tn(R.O[...], R.DHF[...]).astype(BF)
        weight_send(cols, R.WG, R.WGR, 6)

    @pl.when(s == 1)
    def _():
        o_wide_finish(a_piece, R.m_ga)

        def forward_units(q):
            unpack(R.GA, q, put_o)
            mid_norm(q)
            expand(q)

        loop(0, 4, forward_units)
        mlp_grads()

    @pl.when(s == 0)
    def _():
        side_work()
        vector_sums()
        emit_finish(R.EA, R.m_ea, R.o_act)

    da1 = reduce_finish(1, R.m_r2)
    xhat1, rstd1 = norm(R.BUF[0, me_rows, :].astype(F32))
    R.IGR[...] = (R.DHID[...] + norm_back(da1, xhat1, rstd1, gain1)).astype(BF)
    g_own = lambda n: R.IGR.at[pl.ds(0, n)]

    @pl.when(s == 1)
    def _():
        gather_start(g_own, g_piece, sized, R.m_g, 0, quad_chips)
        gather_start(g_own, g_piece, sized, R.m_g, 0, rest_chips)

    emit(R.IGR, R.EI, R.m_ei)

    @pl.when(s == 1)
    def _():
        acc = None
        for g in range(4):
            term = nn(R.ZQ[g], R.WDQ[g])
            acc = term if acc is None else acc + term
        R.PQ[0] = acc.astype(BF)
        quad_start(0, R.m_q0)
        dh_start()
        total = quad_finish(0, R.m_q0)
        R.YR[...] = (R.HIDQ[me_quad, :] + total + down_bias).astype(BF)
        emit(R.YR, R.EA, R.m_ea)
        side_work()
        vector_sums()
        emit_finish(R.EA, R.m_ea, R.o_act)

    for f in drains:
        f()
    drain_rows(R.DHF, R.m_dh, 7)
    drain_forward_rows(R.DHF, R.m_dh)
    quad_drain(1, R.m_q1)
    quad_weights_drain()

    @pl.when(s == 0)
    def _():
        reduce_drain(R.P0, 0, R.m_r0)
        left(R.GX.at[pl.ds(0, 7)], R.m_go.at[0, 0])
        left(R.GX.at[pl.ds(0, 8)], R.m_go.at[2, 0])
        drain_rows(R.BUF.at[0], R.m_y, 8)
        drain_forward_rows(R.BUF.at[1], R.m_g)
        emit_drain(R.YR, R.m_ea)

    @pl.when(s == 1)
    def _():
        left(R.GO.at[pl.ds(0, 15), 0], R.m_o.at[0, 0])
        drain_forward_rows(R.BUF.at[0], R.m_y)

    weight_finish(R.WUR, 0, R.o_up)
    weight_finish(R.WDR, 2, R.o_dn)
    weight_finish(R.WQR, 4, R.o_qkv)
    weight_finish(R.WGR, 6, R.o_wo)

    def f_wait(d):
        z2 = lax.rem(z + d, 4)
        arrived(R.FR.at[z2], R.m_f.at[1, z2])

    loop(1, 4, f_wait)
    R.o_sums[...] = R.FR[0] + R.FR[1] + R.FR[2] + R.FR[3]
    reduce_drain(R.P2, 1, R.m_r2)
    left(R.VR.at[pl.ds(0, 15)], R.m_vs.at[0, 0])
    loop(1, 4, lambda d: left(R.FV, R.m_f.at[0, d]))
    weight_drain(lines, R.WU, 0)
    weight_drain(cols, R.WD, 2)
    weight_drain(cols, R.WQ, 4)
    weight_drain(cols, R.WG, 6)

    @pl.when(s == 1)
    def _():
        quad_drain(0, R.m_q0)
        left(R.GX.at[pl.ds(0, 7)], R.m_ga.at[0, 0])
        left(R.GX.at[pl.ds(0, 8)], R.m_ga.at[2, 0])
        drain_rows(R.BUF.at[1], R.m_g, 8)
        emit_drain(R.YR, R.m_ea)

    emit_finish(R.EI, R.m_ei, R.o_ig)
    emit_drain(R.IGR, R.m_ei)


def finish(*refs):
    act, ig, sums, qkv, wo, up, dn = refs[:7]
    act2, ig2, g1, b1, qkv2, qvb, wo2, outb, g2, b2, up2, upb, dn2, downb = refs[7:]
    z = lax.axis_index("dp")

    def own(row, width):
        out = sums[row : row + 1, 0:width]
        for z2 in range(1, 4):
            out = jnp.where(z == z2, sums[row : row + 1, z2 * width : (z2 + 1) * width], out)
        return out

    for row, out in enumerate((g1, b1, g2, b2, outb, downb)):
        out[...] = own(row, 16)
    upb[...] = own(6, 64)
    qvb[...] = own(7, 32)
    for a, b in ((act, act2), (ig, ig2), (qkv, qkv2), (wo, wo2), (up, up2), (dn, dn2)):
        b[...] = a[...]


def body(images, cot, g1, b1, wqkv, qvb, wo, outb, g2, b2, wup, upb, wdn, downb):
    flat = ((1, 16), F32)
    act = ((4, 64, CHUNK), BF)
    square = ((256, 256), F32)
    qkv, owo = ((192, 256), F32), ((64, 256), F32)
    kept = [act, act, ((8, 256), F32), qkv, owo, square, square]
    final = [act, act, flat, flat, qkv, ((1, 32), F32), owo]
    final += [flat, flat, flat, square, ((1, 64), F32), square, flat]
    space = pl.BlockSpec(memory_space=pltpu.VMEM)
    outs = pl.pallas_call(
        kernel,
        name="two_layers",
        out_shape=[jax.ShapeDtypeStruct(*x) for x in kept],
        in_specs=[space] * 14,
        out_specs=[space] * 7,
        scratch_shapes=list(SCRATCH.values()),
        compiler_params=pltpu.CompilerParams(
            collective_id=0, has_side_effects=True, vmem_limit_bytes=60 * 1024 * 1024
        ),
    )(
        images.reshape(4, CHUNK, 64).transpose(0, 2, 1),
        cot.reshape(4, CHUNK, 64).transpose(0, 2, 1),
        g1,
        b1,
        wqkv.reshape(D, 192).T,
        qvb.reshape(1, 128),
        wo.reshape(64, D),
        outb,
        g2,
        b2,
        wup.reshape(D, 256),
        upb,
        wdn.reshape(256, D),
        downb,
    )
    outs = pl.pallas_call(
        finish,
        name="finish",
        out_shape=[jax.ShapeDtypeStruct(*x) for x in final],
        in_specs=[space] * 7,
        out_specs=[space] * 14,
    )(*outs)
    act, ig, og1, ob1, oqkv, oqvb, owo, ooutb, og2, ob2, oup, oupb, odn, odownb = outs
    return (
        act.transpose(0, 2, 1).reshape(1, 4, 1, CHUNK, 64),
        ig.transpose(0, 2, 1).reshape(1, 4, 1, CHUNK, 64),
        og1,
        ob1,
        oqkv.T.reshape(1, 256, 1, 192),
        oqvb.reshape(1, 1, 32),
        owo.reshape(1, 1, 64, 256),
        ooutb,
        og2,
        ob2,
        oup.reshape(1, 256, 256),
        oupb,
        odn.reshape(1, 256, 256),
        odownb,
    )


def solution(mesh):
    in_specs = (
        P(None, None, "dp", "tensor"),
        P(None, None, "dp", "tensor"),
        P("section", "tensor"),
        P("section", "tensor"),
        P("section", None, "tensor", None),
        P("section", "tensor", None),
        P("section", "tensor", None, None),
        P("section", "tensor"),
        P("section", "tensor"),
        P("section", "tensor"),
        P("section", None, "tensor"),
        P("section", "tensor"),
        P("section", "tensor", None),
        P("section", "tensor"),
    )
    out_specs = (
        P("section", None, None, "dp", "tensor"),
        P("section", None, None, "dp", "tensor"),
        P("section", ("tensor", "dp")),
        P("section", ("tensor", "dp")),
        P("section", "dp", "tensor", None),
        P("section", "tensor", "dp"),
        P("section", "tensor", None, "dp"),
        P("section", ("tensor", "dp")),
        P("section", ("tensor", "dp")),
        P("section", ("tensor", "dp")),
        P("section", "dp", "tensor"),
        P("section", ("tensor", "dp")),
        P("section", "tensor", "dp"),
        P("section", ("tensor", "dp")),
    )
    return jax.shard_map(body, mesh=mesh, in_specs=in_specs, out_specs=out_specs, check_vma=False)
```

```python
import jax
import jax.numpy as jnp
from jax import lax
from jax.experimental import pallas as pl
from jax.experimental.pallas import tpu as pltpu
from jax.sharding import PartitionSpec as P

BF = jnp.bfloat16
F32 = jnp.float32
D = 1024
TOK = 576
CHUNK = 144
epsilon = 1e-06

INPUTS = (
    "images",
    "cot",
    "g1",
    "b1",
    "wqkv",
    "qvb",
    "wo",
    "outb",
    "g2",
    "b2",
    "wup",
    "upb",
    "wdn",
    "downb",
)
OUTPUTS = ("o_act", "o_ig", "o_sums", "o_qkv", "o_wo", "o_up", "o_dn")


def vm(*shape, dtype=BF):
    return pltpu.VMEM(shape, dtype)


def dma(*shape):
    return pltpu.SemaphoreType.DMA(shape)


SCRATCH = dict(
    FB=vm(4, 80, 128),
    GX=vm(16, 4, 80, 128),
    BUF=vm(2, TOK, D),
    VB=vm(8, 128, dtype=F32),
    VG=vm(16, 8, 128, dtype=F32),
    VA=vm(8, D, dtype=F32),
    WO=vm(8, 2, 4, 16, D),
    A1=vm(TOK, D),
    Q=vm(TOK, 64),
    K=vm(TOK, 64),
    V=vm(TOK, 64),
    PR=vm(TOK, TOK, dtype=F32),
    PH=vm(TOK, TOK),
    DS=vm(TOK, TOK),
    O=vm(TOK, 64),
    GO=vm(16, 4, 80, 128),
    GA=vm(16, 4, 80, 128),
    OA=vm(TOK, D),
    HIDQ=vm(CHUNK, D, dtype=F32),
    WUQ=vm(4, D, 256),
    WDQ=vm(4, 256, D),
    WUT=vm(4, 256, D),
    WDT=vm(4, D, 256),
    WOT=vm(D, D),
    UBQ=vm(4, 1, 256, dtype=F32),
    GPQ=vm(4, CHUNK, 256, dtype=F32),
    ZQ=vm(4, CHUNK, 256),
    DZQ=vm(4, CHUNK, 256, dtype=F32),
    PQ=vm(2, CHUNK, D),
    RQ=vm(2, 4, 48, D),
    A2=vm(TOK, D),
    GP=vm(TOK, 256, dtype=F32),
    Z=vm(TOK, 256),
    DU=vm(TOK, 256),
    YR=vm(48, D),
    P0=vm(TOK, D),
    P2=vm(TOK, D),
    SB=vm(2, 8, 48, D),
    PB=vm(2, 8, 48, D),
    RB=vm(2, 8, 48, D),
    DHID=vm(48, D, dtype=F32),
    DHR=vm(48, D),
    DOR=vm(48, D),
    DB=vm(TOK, 128),
    DO=vm(TOK, 64),
    DHF=vm(TOK, D),
    DQKV=vm(TOK, 192),
    IGR=vm(48, D),
    WU=vm(D, 256),
    WD=vm(256, D),
    WQ=vm(192, D),
    WG=vm(64, D),
    WUR=vm(4, 256, 256),
    WDR=vm(4, 256, 256),
    WQR=vm(4, 192, 256),
    WGR=vm(4, 64, 256),
    EA=vm(4, CHUNK, 128),
    EI=vm(4, CHUNK, 128),
    VS=vm(8, D, dtype=F32),
    VR=vm(16, 8, 128, dtype=F32),
    FV=vm(8, 256, dtype=F32),
    FR=vm(4, 8, 256, dtype=F32),
    m_z=dma(2, 4),
    m_x=dma(4, 8),
    m_v=dma(2, 16),
    m_wo=dma(4, 8),
    m_o=dma(2, 16),
    m_ga=dma(4, 8),
    m_go=dma(4, 8),
    m_wq=dma(4, 4),
    m_q0=dma(2, 4),
    m_q1=dma(2, 4),
    m_r0=dma(4, 8),
    m_r2=dma(4, 8),
    m_y=dma(4, 8),
    m_g=dma(4, 8),
    m_do=dma(2, 16),
    m_dh=dma(4, 8),
    m_ea=dma(2, 16),
    m_ei=dma(2, 16),
    m_vs=dma(2, 16),
    m_w=dma(8, 4),
    m_f=dma(2, 4),
    clear=pltpu.SemaphoreType.REGULAR,
)


def nn(a, b):
    return lax.dot_general(a, b, (((1,), (0,)), ((), ())), preferred_element_type=F32)


def nt(a, b):
    return lax.dot_general(a, b, (((1,), (1,)), ((), ())), preferred_element_type=F32)


def tn(a, b):
    return lax.dot_general(a, b, (((0,), (0,)), ((), ())), preferred_element_type=F32)


def loop(low, high, f):
    pl.loop(low, high)(f)


def quad_of(j):
    return lax.div(lax.rem(j, 8), 2)


def place_of(j):
    return 2 * lax.div(j, 8) + lax.rem(j, 2)


def member(quad, place):
    return 8 * lax.div(place, 2) + 2 * quad + lax.rem(place, 2)


def row_of(j):
    return pl.multiple_of(144 * quad_of(j) + 32 * place_of(j), 16)


def lane_of(j):
    return pl.multiple_of(128 * lax.div(j, 2), 128)


def sized(j, f):
    big = place_of(j) == 3
    pl.when(big)(lambda: f(48))
    pl.when(jnp.logical_not(big))(lambda: f(32))


def whole(j, f):
    f(None)


def norm(v):
    mu = jnp.mean(v, -1, keepdims=True)
    var = jnp.mean(v * v, -1, keepdims=True) - mu * mu
    rstd = lax.rsqrt(var + epsilon)
    return (v - mu) * rstd, rstd


def norm_back(g, xhat, rstd, gain):
    w = g * gain
    return rstd * (
        w - jnp.mean(w, -1, keepdims=True) - xhat * jnp.mean(w * xhat, -1, keepdims=True)
    )


class Refs:
    pass


def kernel(*refs):
    R = Refs()
    for name, ref in zip((*INPUTS, *OUTPUTS, *SCRATCH), refs):
        setattr(R, name, ref)
    s = lax.axis_index("section")
    t = lax.axis_index("tensor")
    z = lax.axis_index("dp")
    k = lax.div(t, 2)
    c = lax.rem(t, 2)
    zq = quad_of(t)
    p = place_of(t)
    me_row = row_of(t)
    drains = []

    def rc(src, dst, ss, rs, s2, t2, z2):
        return pltpu.make_async_remote_copy(
            src_ref=src,
            dst_ref=dst,
            send_sem=ss,
            recv_sem=rs,
            device_id={"section": s2, "tensor": t2, "dp": z2},
            device_id_type=pl.DeviceIdType.MESH,
        )

    def arrived(dst, rs):
        rc(dst, dst, rs, rs, s, 2 * k + 1 - c, z).wait_recv()

    def left(src, ss):
        rc(src, src, ss, ss, s, 2 * k + 1 - c, z).wait_send()

    def peers(f):
        def far(d):
            f(d, 8 * (1 - lax.div(t, 8)) + lax.rem(t + d, 8))

        def near(d):
            f(8 + d, 8 * lax.div(t, 8) + lax.rem(t + d, 8))

        loop(0, 8, far)
        loop(1, 8, near)

    def far_chips(f):
        loop(0, 4, lambda d: f(4 * (1 - lax.div(k, 4)) + lax.rem(k + d, 4)))

    def near_chips(f):
        loop(1, 4, lambda d: f(4 * lax.div(k, 4) + lax.rem(k + d, 4)))

    def other_chips(f):
        far_chips(f)
        near_chips(f)

    def chips_by_arrival(f):
        near_chips(f)
        far_chips(f)

    def all_chips(f):
        loop(0, 8, f)

    def quad_chips(f):
        loop(0, 2, lambda d: f(4 * d + zq))

    def rest_chips(f):
        loop(0, 6, lambda d: f(4 * lax.div(d, 3) + lax.rem(zq + 1 + lax.rem(d, 3), 4)))

    def per_core(f):
        pl.when(c == 0)(lambda: f(64, 80))
        pl.when(c == 1)(lambda: f(80, 64))

    def gather_start(src, dst, size, m, s2, chips):
        def go(k2):
            size(t, lambda n: rc(src(n), dst(t, n), m.at[0, 0], m.at[1, k], s2, 2 * k2 + c, z).start())

        chips(go)

    def forward_own(dst, m):
        here = dst(t, None)
        rc(here, here, m.at[2, 0], m.at[3, 0], s, 2 * k + 1 - c, z).start()

    def gather_forward(dst, size, m, chips, part=0):
        def go(k2):
            j = 2 * k2 + c

            def send(n):
                here = dst(j, n)
                arrived(here, m.at[1, k2])
                rc(here, here, m.at[2, 0], m.at[3, part], s, 2 * k + 1 - c, z).start()

            size(j, send)

        chips(go)

    def finish_rows(buf, m, quads, part=0):
        per_core(lambda mine, other: arrived(buf.at[pl.ds(0, other * quads)], m.at[3, part]))

    def drain_rows(buf, m, count):
        sized(t, lambda n: left(R.SB.at[0, pl.ds(0, count), pl.ds(0, n)], m.at[0, 0]))

    def drain_forward_rows(buf, m):
        per_core(lambda mine, other: left(buf.at[pl.ds(0, mine * 4)], m.at[2, 0]))

    def quad_start(i, m):
        def go(p2):
            t2 = member(zq, p2)
            sized(
                t2,
                lambda n: rc(
                    R.PQ.at[i, pl.ds(pl.multiple_of(32 * p2, 16), n)],
                    R.RQ.at[i, p, pl.ds(0, n)],
                    m.at[0, p2],
                    m.at[1, p],
                    s,
                    t2,
                    z,
                ).start(),
            )

        far = 2 - 2 * lax.div(p, 2)
        loop(0, 2, lambda d: go(far + lax.rem(c + d, 2)))
        go(2 - far + 1 - c)
        R.RQ[i, p] = R.PQ[i, pl.ds(pl.multiple_of(32 * p, 16), 48), :]

    def quad_finish(i, m):
        def go(d):
            p2 = lax.rem(p + d, 4)
            sized(t, lambda n: arrived(R.RQ.at[i, p2, pl.ds(0, n)], m.at[1, p2]))

        loop(1, 4, go)
        total = R.RQ[i, 0].astype(F32)
        for p2 in range(1, 4):
            total = total + R.RQ[i, p2].astype(F32)
        return total

    def quad_drain(i, m):
        def go(d):
            p2 = lax.rem(p + d, 4)
            sized(member(zq, p2), lambda n: left(R.PQ.at[i, pl.ds(0, n)], m.at[0, p2]))

        loop(1, 4, go)

    def reduce_over(part, i, m, compute):
        def sibling(q, d):
            k2 = 4 * d + q
            j = 2 * k2 + 1 - c
            sized(
                j,
                lambda n: rc(
                    part.at[pl.ds(row_of(j), n)],
                    R.SB.at[i, k2, pl.ds(0, n)],
                    m.at[0, 0],
                    m.at[1, k2],
                    s,
                    2 * k + 1 - c,
                    z,
                ).start(),
            )

        def mid(q, d):
            k2 = 4 * d + q
            j = 2 * k2 + c
            sized(j, lambda n: arrived(R.SB.at[i, k2, pl.ds(0, n)], m.at[1, k2]))
            both = part[pl.ds(row_of(j), 48), :].astype(F32) + R.SB[i, k2].astype(F32)
            R.PB[i, k2] = both.astype(BF)

            def send(n):
                rc(
                    R.PB.at[i, k2, pl.ds(0, n)],
                    R.RB.at[i, k, pl.ds(0, n)],
                    m.at[2, 0],
                    m.at[3, 0],
                    s,
                    j,
                    z,
                ).start()

            pl.when(k2 != k)(lambda: sized(j, send))

        def go(a):
            q = lax.rem(zq + 1 + a, 4)
            compute(q)
            loop(0, 2, lambda d: sibling(q, d))
            pl.when(a > 0)(lambda: loop(0, 2, lambda d: mid(lax.rem(zq + a, 4), d)))

        loop(0, 4, go)
        loop(0, 2, lambda d: mid(zq, d))

    def reduce_finish(i, m):
        sized(t, lambda n: arrived(R.RB.at[i, pl.ds(0, 7), pl.ds(0, n)], m.at[3, 0]))
        R.RB[i, k] = R.PB[i, k]
        total = R.RB[i, 0].astype(F32)
        for k2 in range(1, 8):
            total = total + R.RB[i, k2].astype(F32)
        return total

    def reduce_drain(part, i, m):
        per_core(lambda mine, other: left(part.at[pl.ds(0, other * 4)], m.at[0, 0]))
        per_core(
            lambda mine, other: sized(t, lambda n: left(part.at[pl.ds(0, mine * 4 - n)], m.at[2, 0]))
        )

    def emit(rows, E, m):
        def go(d, t2):
            def send(n):
                rc(
                    rows.at[pl.ds(0, n), pl.ds(lane_of(t2), 128)],
                    E.at[z, pl.ds(pl.multiple_of(32 * p, 16), n)],
                    m.at[0, 0],
                    m.at[1, 0],
                    s,
                    t2,
                    zq,
                ).start()

            sized(t, send)

        peers(go)
        pl.when(zq != z)(lambda: go(8, t))

        def local():
            def put(n):
                E[z, pl.ds(pl.multiple_of(32 * p, 16), n), :] = rows[
                    pl.ds(0, n), pl.ds(lane_of(t), 128)
                ]

            sized(t, put)

        pl.when(zq == z)(local)

    def emit_drain(rows, m):
        def taken(count):
            sized(t, lambda n: left(R.GX.at[pl.ds(0, count), 0, pl.ds(0, n)], m.at[0, 0]))

        pl.when(zq != z)(lambda: taken(16))
        pl.when(zq == z)(lambda: taken(15))

    def emit_finish(E, m, out):
        pl.when(zq != z)(lambda: arrived(E, m.at[1, 0]))
        pl.when(zq == z)(
            lambda: sized(t, lambda n: arrived(R.DB.at[pl.ds(0, TOK - n)], m.at[1, 0]))
        )

        @pl.when(c == 0)
        def _():
            for i in range(4):
                out[i] = E[i, :, 0:64].T

        @pl.when(c == 1)
        def _():
            for i in range(4):
                out[i] = E[i, :, 64:128].T

    bar = pltpu.get_barrier_semaphore()

    def greet(s2, t2, z2):
        pl.semaphore_signal(
            bar,
            inc=1,
            device_id={"section": s2, "tensor": t2, "dp": z2},
            device_id_type=pl.DeviceIdType.MESH,
        )

    loop(1, 16, lambda d: greet(s, lax.rem(t + d, 16), z))
    loop(1, 4, lambda d: greet(s, t, lax.rem(z + d, 4)))
    loop(0, 8, lambda d: greet(1 - s, 2 * d + c, z))

    def pack(src):
        for m in range(4):
            R.FB[m, 64:80, :] = jnp.zeros((16, 128), BF)
            rows = src[m].T
            R.FB[m, :, 0:64] = rows[0:80, :]
            R.FB[m, 0:64, 64:128] = rows[80:144, :]

    pl.when(s == 0)(lambda: pack(R.images))
    pl.when(s == 1)(lambda: pack(R.cot))
    R.VB[...] = jnp.zeros((8, 128), F32)
    vecs = (R.g1, R.b1, R.g2, R.b2, R.outb, R.downb)

    @pl.when(c == 0)
    def _():
        for i, v in enumerate(vecs):
            R.VB[i : i + 1, 0:64] = v[...]

    @pl.when(c == 1)
    def _():
        for i, v in enumerate(vecs):
            R.VB[i : i + 1, 64:128] = v[...]

    R.VB[6:7, :] = R.upb[:, 0:128]
    R.VB[7:8, :] = R.upb[:, 128:256]
    R.VG[t] = R.VB[...]
    R.GX[t, z] = R.FB[z]
    R.WO[k, c, z] = R.wo[pl.ds(pl.multiple_of(16 * z, 16), 16), :]
    R.WUQ[zq] = R.wup[...]
    R.WDQ[zq] = R.wdn[...]
    R.FV[...] = jnp.zeros((8, 256), F32)
    R.VS[...] = jnp.zeros((8, D), F32)
    for i in range(4):
        R.GO[t, i, 64:80, :] = jnp.zeros((16, 128), BF)

    pl.semaphore_wait(bar, 26)

    def z_send(d):
        z2 = lax.rem(z + d, 4)
        rc(R.FB.at[z2], R.GX.at[t, z], R.m_z.at[0, d], R.m_z.at[1, z], s, t, z2).start()

    loop(1, 4, z_send)

    def z_wait(d):
        z2 = lax.rem(z + d, 4)
        arrived(R.GX.at[t, z2], R.m_z.at[1, z2])

    loop(1, 4, z_wait)
    drains.append(lambda: loop(1, 4, lambda d: left(R.FB.at[0], R.m_z.at[0, d])))
    x_piece = lambda j, n: R.GX.at[j]
    def by_plane(f):
        pl.when(lax.rem(z, 2) == 0)(lambda: f(R.wup, R.WUQ, R.WDQ, 512))
        pl.when(lax.rem(z, 2) == 1)(lambda: f(R.wdn, R.WDQ, R.WUQ, 128))

    def quad_weights():
        def fetch(src, own, other, half):
            def go(d):
                t2 = member(lax.rem(zq + d, 4), p)
                rc(src, own.at[zq], R.m_wq.at[0, 0], R.m_wq.at[1, zq], s, t2, z).start()

            loop(1, 4, go)

        by_plane(fetch)

    def quad_weights_pass():
        def give(src, own, other, half):
            def go(d):
                g2 = lax.rem(zq + d, 4)
                arrived(own.at[g2], R.m_wq.at[1, g2])
                for first, z2 in ((0, lax.rem(z + 1, 4)), (half, lax.rem(z + 3, 4))):
                    piece = own.at[g2, pl.ds(first, half)]
                    rc(piece, piece, R.m_wq.at[2, 0], R.m_wq.at[3, 0], s, t, z2).start()

            loop(1, 4, go)

        by_plane(give)

    def quad_weights_wait():
        by_plane(lambda src, own, other, half: arrived(other.at[pl.ds(0, 3)], R.m_wq.at[3, 0]))

    def quad_weights_drain():
        def sent(src, own, other, half):
            left(own.at[pl.ds(0, 3)], R.m_wq.at[0, 0])
            left(own.at[pl.ds(0, 3)], R.m_wq.at[2, 0])

        by_plane(sent)

    def v_send(d, t2):
        rc(R.VB, R.VG.at[t], R.m_v.at[0, 0], R.m_v.at[1, 0], s, t2, z).start()

    @pl.when(s == 1)
    def _():
        quad_weights()
        quad_weights_pass()
        pl.semaphore_wait(R.clear, 1)

    gather_start(lambda n: R.GX.at[t], x_piece, whole, R.m_x, s, other_chips)
    forward_own(x_piece, R.m_x)
    peers(v_send)
    drains.append(lambda: left(R.VG.at[pl.ds(0, 15)], R.m_v.at[0, 0]))

    def wo_send(k2):
        here = R.WO.at[k, c, z]
        rc(here, here, R.m_wo.at[0, 0], R.m_wo.at[1, 0], s, 2 * k2 + c, z).start()

    other_chips(wo_send)
    gather_forward(x_piece, whole, R.m_x, chips_by_arrival)
    arrived(R.GX.at[pl.ds(0, 8)], R.m_x.at[3, 0])
    arrived(R.WO.at[pl.ds(0, 7), 0, 0], R.m_wo.at[1, 0])

    def wo_planes(d):
        here = R.WO.at[:, c, z]
        rc(here, here, R.m_wo.at[0, 1], R.m_wo.at[1, 1], s, t, lax.rem(z + d, 4)).start()

    loop(1, 4, wo_planes)
    arrived(R.VG.at[pl.ds(0, 15)], R.m_v.at[1, 0])
    for kk in range(8):
        R.VA[:, 128 * kk : 128 * kk + 128] = R.VG[2 * kk] + R.VG[2 * kk + 1]
    for g in range(4):
        R.UBQ[g, :, 0:128] = R.VG[member(g, p), 6:7, :]
        R.UBQ[g, :, 128:256] = R.VG[member(g, p), 7:8, :]
    gain1, bias1 = R.VA[0:1, :], R.VA[1:2, :]
    gain2, bias2 = R.VA[2:3, :], R.VA[3:4, :]
    out_bias, down_bias = R.VA[4:5, :], R.VA[5:6, :]

    def unpack(G, q, put):
        row = pl.multiple_of(144 * q, 16)
        for kk in range(8):
            a, b = G[2 * kk, q], G[2 * kk + 1, q]
            lanes = slice(128 * kk, 128 * kk + 128)
            put(pl.ds(row, 80), lanes, jnp.concatenate([a[:, :64], b[:, :64]], axis=1))
            put(
                pl.ds(row + 80, 64),
                lanes,
                jnp.concatenate([a[:64, 64:], b[:64, 64:]], axis=1),
            )

    def put_first(rows, lanes, v):
        R.BUF[s, rows, lanes] = v

    loop(0, 4, lambda q: unpack(R.GX, q, put_first))
    drains.append(lambda: left(R.GX.at[pl.ds(0, 7)], R.m_x.at[0, 0]))
    drains.append(lambda: left(R.GX.at[pl.ds(0, 8)], R.m_x.at[2, 0]))

    y_piece = lambda j, n: R.BUF.at[0, pl.ds(row_of(j), n)]
    g_piece = lambda j, n: R.BUF.at[1, pl.ds(row_of(j), n)]

    def quad_dz(g):
        dy = R.BUF[1, pl.ds(pl.multiple_of(CHUNK * zq, 16), CHUNK), :]
        R.DZQ[g] = nn(dy, R.WDT[g])

    def turn(g):
        R.WUT[g] = R.WUQ[g].T
        R.WDT[g] = R.WDQ[g].T

    @pl.when(s == 1)
    def _():
        quad_weights_wait()
        loop(0, 4, turn)
        loop(0, 4, quad_dz)
        gather_forward(y_piece, sized, R.m_y, all_chips)
        finish_rows(R.BUF.at[0], R.m_y, 4)

    def rows_at(i):
        return pl.ds(pl.multiple_of(CHUNK * i, 16), CHUNK)

    def project(i):
        rows = rows_at(i)
        xhat, _ = norm(R.BUF[0, rows, :].astype(F32))
        a = (xhat * gain1 + bias1).astype(BF)
        R.A1[rows, :] = a
        mixed = nt(a, R.wqkv[...])
        R.Q[rows, :] = (mixed[:, 0:64] + R.qvb[:, 0:64]).astype(BF) * jnp.asarray(0.125, BF)
        R.K[rows, :] = mixed[:, 64:128].astype(BF)
        R.V[rows, :] = (mixed[:, 128:192] + R.qvb[:, 64:128]).astype(BF)

    loop(0, 4, project)

    def attend(i):
        rows = rows_at(i)
        sc = nt(R.Q[rows, :], R.K[...])
        e = jnp.exp(sc - jnp.max(sc, -1, keepdims=True))
        prob = e * (1.0 / jnp.sum(e, -1, keepdims=True))
        R.PR[rows, :] = prob
        ph = prob.astype(BF)
        R.PH[rows, :] = ph
        o = nn(ph, R.V[...]).astype(BF)
        R.O[rows, :] = o
        R.GO[t, i, :, 0:64] = o[0:80, :]
        R.GO[t, i, 0:64, 64:128] = o[80:144, :]

    loop(0, 4, attend)
    o_piece = lambda j, n: R.GO.at[j]
    a_piece = lambda j, n: R.GA.at[j]

    def put_o(rows, lanes, v):
        R.OA[rows, lanes] = v

    def mid_norm(i):
        rows = rows_at(i)
        hidden = R.BUF[0, rows, :].astype(F32) + nn(R.OA[rows, :], R.WO[...].reshape(D, D)) + out_bias
        xhat, _ = norm(hidden)
        R.A2[rows, :] = (xhat * gain2 + bias2).astype(BF)

        @pl.when(i == zq)
        def _():
            R.HIDQ[...] = hidden

    def wo_cores():
        arrived(R.WO.at[:, 0, pl.ds(0, 3)], R.m_wo.at[1, 1])
        here = R.WO.at[:, c]
        rc(here, here, R.m_wo.at[2, 0], R.m_wo.at[3, 0], s, 2 * k + 1 - c, z).start()

    drains.append(lambda: left(R.WO.at[pl.ds(0, 7), 0, 0], R.m_wo.at[0, 0]))
    drains.append(lambda: left(R.WO.at[:, 0, pl.ds(0, 3)], R.m_wo.at[0, 1]))
    drains.append(lambda: left(R.WO.at[:, 0], R.m_wo.at[2, 0]))

    def expand(i):
        rows = rows_at(i)
        u = nn(R.A2[rows, :], R.wup[...]) + R.upb[...]
        half = 0.5 * (1.0 + lax.erf(u * 0.7071067811865476))
        R.Z[rows, :] = (u * half).astype(BF)
        R.GP[rows, :] = half + u * (0.3989422804014327 * jnp.exp(-0.5 * u * u))

    def quad_expand(g):
        u = nn(R.A2[rows_at(zq), :], R.WUQ[g]) + R.UBQ[g]
        half = 0.5 * (1.0 + lax.erf(u * 0.7071067811865476))
        R.ZQ[g] = (u * half).astype(BF)
        R.GPQ[g] = half + u * (0.3989422804014327 * jnp.exp(-0.5 * u * u))

    y_own = lambda n: R.YR.at[pl.ds(0, n)]
    me_quad = pl.ds(pl.multiple_of(32 * p, 16), 48)

    def contract(i):
        rows = rows_at(i)
        R.P0[rows, :] = nn(R.Z[rows, :], R.wdn[...]).astype(BF)

    def o_wide_start(piece, m):
        gather_start(lambda n: piece(t, n), piece, whole, m, s, other_chips)
        forward_own(piece, m)

    def o_wide_finish(piece, m):
        gather_forward(piece, whole, m, chips_by_arrival)
        arrived(R.GX.at[pl.ds(0, 8)], m.at[3, 0])

    @pl.when(s == 0)
    def _():
        o_wide_start(o_piece, R.m_go)
        wo_cores()
        o_wide_finish(o_piece, R.m_go)
        pl.semaphore_signal(
            R.clear,
            inc=1,
            device_id={"section": 1, "tensor": t, "dp": z},
            device_id_type=pl.DeviceIdType.MESH,
        )
        arrived(R.WO.at[:, 0], R.m_wo.at[3, 0])

        def forward_quad(q):
            unpack(R.GO, q, put_o)
            mid_norm(q)
            expand(q)
            contract(q)

        reduce_over(R.P0, 0, R.m_r0, forward_quad)
        total = reduce_finish(0, R.m_r0)
        R.YR[...] = (R.HIDQ[me_quad, :] + total + down_bias).astype(BF)
        gather_start(y_own, y_piece, sized, R.m_y, 1, all_chips)
        emit(R.YR, R.EA, R.m_ea)
        quad_weights()
        quad_weights_pass()
        quad_weights_wait()
        loop(0, 4, turn)
        loop(0, 4, quad_expand)
        gather_forward(g_piece, sized, R.m_g, quad_chips)
        finish_rows(R.BUF.at[1], R.m_g, 1)
        loop(0, 4, quad_dz)

    @pl.when(s == 1)
    def _():
        def send(d, t2):
            g2 = quad_of(t2)
            rc(
                R.GO.at[t, g2], R.GO.at[t, g2], R.m_o.at[0, 0], R.m_o.at[1, 0], s, t2, z
            ).start()

        peers(send)
        wo_cores()
        arrived(R.WO.at[:, 0], R.m_wo.at[3, 0])
        arrived(R.GO.at[pl.ds(0, 15), 0], R.m_o.at[1, 0])
        unpack(R.GO, zq, put_o)
        mid_norm(zq)
        loop(0, 4, quad_expand)

    partial = None
    for g in range(4):
        du = (R.DZQ[g] * R.GPQ[g]).astype(BF)
        term = nn(du, R.WUT[g])
        partial = term if partial is None else partial + term
    R.PQ[1] = partial.astype(BF)
    quad_start(1, R.m_q1)
    R.WOT[...] = R.WO[...].reshape(D, D).T

    def cols(ref, z2):
        return ref.at[:, pl.ds(pl.multiple_of(256 * z2, 256), 256)]

    def lines(ref, z2):
        return ref.at[pl.ds(pl.multiple_of(256 * z2, 256), 256)]

    def weight_send(cut, stage, land, row):
        def go(d):
            z2 = lax.rem(z + d, 4)
            rc(
                cut(stage, z2), land.at[z], R.m_w.at[row, d], R.m_w.at[row + 1, z], s, t, z2
            ).start()

        loop(1, 4, go)
        land[z] = cut(stage, z)[...]

    def weight_drain(cut, stage, row):
        loop(1, 4, lambda d: left(cut(stage, 0), R.m_w.at[row, d]))

    def weight_finish(land, row, out):
        def go(d):
            z2 = lax.rem(z + d, 4)
            arrived(land.at[z2], R.m_w.at[row + 1, z2])

        loop(1, 4, go)
        total = land[0].astype(F32)
        for z2 in range(1, 4):
            total = total + land[z2].astype(F32)
        out[...] = total

    def back_units(i):
        rows = rows_at(i)
        R.DU[rows, :] = (nt(R.BUF[1, rows, :], R.wdn[...]) * R.GP[rows, :]).astype(BF)

    def mlp_grads():
        loop(0, 4, back_units)
        R.WU[...] = tn(R.A2[...], R.DU[...]).astype(BF)
        weight_send(lines, R.WU, R.WUR, 0)
        R.WD[...] = tn(R.Z[...], R.BUF[1]).astype(BF)
        weight_send(cols, R.WD, R.WDR, 2)
        R.FV[6:7, :] = jnp.sum(R.DU[...].astype(F32), axis=0, keepdims=True)

    valid = lax.broadcasted_iota(jnp.int32, (48, 1), 0) < jnp.where(p == 3, 48, 32)

    def over_rows(v):
        return jnp.sum(jnp.where(valid, v, 0.0), axis=0, keepdims=True)

    me_rows = pl.ds(me_row, 48)
    da2 = quad_finish(1, R.m_q1)
    xhat2b, rstd2 = norm(R.HIDQ[me_quad, :])
    R.VS[2:3, :] = over_rows(da2 * xhat2b)
    R.VS[3:4, :] = over_rows(da2)
    dhid = R.BUF[1, me_rows, :].astype(F32) + norm_back(da2, xhat2b, rstd2, gain2)
    R.DHID[...] = dhid
    R.DHR[...] = dhid.astype(BF)
    R.DOR[...] = nn(R.DHR[...], R.WOT[...]).astype(BF)

    def do_send(d, t2):
        sized(
            t,
            lambda n: rc(
                R.DOR.at[pl.ds(0, n), pl.ds(lane_of(t2), 128)],
                R.DB.at[pl.ds(me_row, n)],
                R.m_do.at[0, 0],
                R.m_do.at[1, 0],
                s,
                t2,
                z,
            ).start(),
        )

    peers(do_send)

    drains.append(
        lambda: sized(t, lambda n: left(R.GX.at[pl.ds(0, 15), 0, pl.ds(0, n)], R.m_do.at[0, 0]))
    )

    def own_do(n):
        R.DB[pl.ds(me_row, n), :] = R.DOR[0:n, pl.ds(lane_of(t), 128)]
        R.DHF[pl.ds(me_row, n), :] = R.DHR[0:n, :]

    sized(t, own_do)
    dh_piece = lambda j, n: R.DHF.at[pl.ds(row_of(j), n)]
    dh_own = lambda n: R.DHR.at[pl.ds(0, n)]

    def forward_dh(n):
        here = dh_piece(t, n)
        rc(here, here, R.m_dh.at[2, 0], R.m_dh.at[3, 0], s, 2 * k + 1 - c, z).start()

    def dh_start():
        gather_start(dh_own, dh_piece, sized, R.m_dh, s, other_chips)
        sized(t, forward_dh)

    @pl.when(s == 1)
    def _():
        R.GA[t] = R.GO[t]
        o_wide_start(a_piece, R.m_ga)

    @pl.when(s == 0)
    def _():
        dh_start()
        gather_forward(g_piece, sized, R.m_g, rest_chips, 1)
        finish_rows(R.BUF.at[1], R.m_g, 3, 1)
        mlp_grads()

    sized(t, lambda n: arrived(R.DB.at[pl.ds(0, TOK - n)], R.m_do.at[1, 0]))
    @pl.when(c == 0)
    def _():
        R.DO[...] = R.DB[:, 0:64]

    @pl.when(c == 1)
    def _():
        R.DO[...] = R.DB[:, 64:128]

    def back_attend(i):
        rows = rows_at(i)
        dp = nt(R.DO[rows, :], R.V[...])
        prob = R.PR[rows, :]
        ds = (prob * (dp - jnp.sum(prob * dp, -1, keepdims=True))).astype(BF)
        R.DS[rows, :] = ds
        R.DQKV[rows, 0:64] = (nn(ds, R.K[...]) * 0.125).astype(BF)

    loop(0, 4, back_attend)
    R.DQKV[:, 64:128] = tn(R.Q[...], R.DS[...]).T.astype(BF)
    R.DQKV[:, 128:192] = tn(R.DO[...], R.PH[...]).T.astype(BF)

    def back_qkv(i):
        rows = rows_at(i)
        R.P2[rows, :] = nn(R.DQKV[rows, :], R.wqkv[...]).astype(BF)

    reduce_over(R.P2, 1, R.m_r2, back_qkv)

    def norm_sums(i):
        rows = rows_at(i)
        xhat, _ = norm(R.BUF[0, rows, :].astype(F32))
        g = R.P2[rows, :].astype(F32)
        R.VS[0:1, :] += jnp.sum(g * xhat, axis=0, keepdims=True)
        R.VS[1:2, :] += jnp.sum(g, axis=0, keepdims=True)

    def vector_sums():
        arrived(R.VR.at[pl.ds(0, 15)], R.m_vs.at[1, 0])
        mine = pl.ds(lane_of(t), 128)
        vec = R.VR[0]
        for t2 in range(1, 16):
            vec = vec + R.VR[t2]
        out_sum = jnp.sum(R.DHF[:, mine].astype(F32), axis=0, keepdims=True)
        down_sum = jnp.sum(R.BUF[1, :, mine].astype(F32), axis=0, keepdims=True)

        def place(lanes):
            R.FV[0:4, 0:64] = vec[0:4, lanes]
            R.FV[4:5, 0:64] = out_sum[:, lanes]
            R.FV[5:6, 0:64] = down_sum[:, lanes]

        pl.when(c == 0)(lambda: place(slice(0, 64)))
        pl.when(c == 1)(lambda: place(slice(64, 128)))

        def f_send(d):
            z2 = lax.rem(z + d, 4)
            rc(R.FV, R.FR.at[z], R.m_f.at[0, d], R.m_f.at[1, z], s, t, z2).start()

        loop(1, 4, f_send)
        R.FR[z] = R.FV[...]


    def s_send(d, t2):
        rc(
            R.VS.at[:, pl.ds(lane_of(t2), 128)],
            R.VR.at[t],
            R.m_vs.at[0, 0],
            R.m_vs.at[1, 0],
            s,
            t2,
            z,
        ).start()

    def side_work():
        loop(0, 4, norm_sums)
        peers(s_send)
        R.VR[t] = R.VS[:, pl.ds(lane_of(t), 128)]
        R.WQ[...] = tn(R.DQKV[...], R.A1[...]).astype(BF)
        weight_send(cols, R.WQ, R.WQR, 4)
        qkv_sum = jnp.sum(R.DQKV[...].astype(F32), axis=0, keepdims=True)
        R.FV[7:8, 0:64] = qkv_sum[:, 0:64]
        R.FV[7:8, 64:128] = qkv_sum[:, 128:192]
        gather_forward(dh_piece, sized, R.m_dh, chips_by_arrival)
        finish_rows(R.DHF, R.m_dh, 4)
        R.WG[...] = tn(R.O[...], R.DHF[...]).astype(BF)
        weight_send(cols, R.WG, R.WGR, 6)

    @pl.when(s == 1)
    def _():
        o_wide_finish(a_piece, R.m_ga)

        def forward_units(q):
            unpack(R.GA, q, put_o)
            mid_norm(q)
            expand(q)

        loop(0, 4, forward_units)
        mlp_grads()

    @pl.when(s == 0)
    def _():
        side_work()
        vector_sums()
        emit_finish(R.EA, R.m_ea, R.o_act)

    da1 = reduce_finish(1, R.m_r2)
    xhat1, rstd1 = norm(R.BUF[0, me_rows, :].astype(F32))
    R.IGR[...] = (R.DHID[...] + norm_back(da1, xhat1, rstd1, gain1)).astype(BF)
    g_own = lambda n: R.IGR.at[pl.ds(0, n)]

    @pl.when(s == 1)
    def _():
        gather_start(g_own, g_piece, sized, R.m_g, 0, quad_chips)
        gather_start(g_own, g_piece, sized, R.m_g, 0, rest_chips)

    emit(R.IGR, R.EI, R.m_ei)

    @pl.when(s == 1)
    def _():
        acc = None
        for g in range(4):
            term = nn(R.ZQ[g], R.WDQ[g])
            acc = term if acc is None else acc + term
        R.PQ[0] = acc.astype(BF)
        quad_start(0, R.m_q0)
        dh_start()
        total = quad_finish(0, R.m_q0)
        R.YR[...] = (R.HIDQ[me_quad, :] + total + down_bias).astype(BF)
        emit(R.YR, R.EA, R.m_ea)
        side_work()
        vector_sums()
        emit_finish(R.EA, R.m_ea, R.o_act)

    for f in drains:
        f()
    drain_rows(R.DHF, R.m_dh, 7)
    drain_forward_rows(R.DHF, R.m_dh)
    quad_drain(1, R.m_q1)
    quad_weights_drain()

    @pl.when(s == 0)
    def _():
        reduce_drain(R.P0, 0, R.m_r0)
        left(R.GX.at[pl.ds(0, 7)], R.m_go.at[0, 0])
        left(R.GX.at[pl.ds(0, 8)], R.m_go.at[2, 0])
        drain_rows(R.BUF.at[0], R.m_y, 8)
        drain_forward_rows(R.BUF.at[1], R.m_g)
        emit_drain(R.YR, R.m_ea)

    @pl.when(s == 1)
    def _():
        left(R.GO.at[pl.ds(0, 15), 0], R.m_o.at[0, 0])
        drain_forward_rows(R.BUF.at[0], R.m_y)

    weight_finish(R.WUR, 0, R.o_up)
    weight_finish(R.WDR, 2, R.o_dn)
    weight_finish(R.WQR, 4, R.o_qkv)
    weight_finish(R.WGR, 6, R.o_wo)

    def f_wait(d):
        z2 = lax.rem(z + d, 4)
        arrived(R.FR.at[z2], R.m_f.at[1, z2])

    loop(1, 4, f_wait)
    R.o_sums[...] = R.FR[0] + R.FR[1] + R.FR[2] + R.FR[3]
    reduce_drain(R.P2, 1, R.m_r2)
    left(R.VR.at[pl.ds(0, 15)], R.m_vs.at[0, 0])
    loop(1, 4, lambda d: left(R.FV, R.m_f.at[0, d]))
    weight_drain(lines, R.WU, 0)
    weight_drain(cols, R.WD, 2)
    weight_drain(cols, R.WQ, 4)
    weight_drain(cols, R.WG, 6)

    @pl.when(s == 1)
    def _():
        quad_drain(0, R.m_q0)
        left(R.GX.at[pl.ds(0, 7)], R.m_ga.at[0, 0])
        left(R.GX.at[pl.ds(0, 8)], R.m_ga.at[2, 0])
        drain_rows(R.BUF.at[1], R.m_g, 8)
        emit_drain(R.YR, R.m_ea)

    emit_finish(R.EI, R.m_ei, R.o_ig)
    emit_drain(R.IGR, R.m_ei)


def finish(*refs):
    act, ig, sums, qkv, wo, up, dn = refs[:7]
    act2, ig2, g1, b1, qkv2, qvb, wo2, outb, g2, b2, up2, upb, dn2, downb = refs[7:]
    z = lax.axis_index("dp")

    def own(row, width):
        out = sums[row : row + 1, 0:width]
        for z2 in range(1, 4):
            out = jnp.where(z == z2, sums[row : row + 1, z2 * width : (z2 + 1) * width], out)
        return out

    for row, out in enumerate((g1, b1, g2, b2, outb, downb)):
        out[...] = own(row, 16)
    upb[...] = own(6, 64)
    qvb[...] = own(7, 32)
    for a, b in ((act, act2), (ig, ig2), (qkv, qkv2), (wo, wo2), (up, up2), (dn, dn2)):
        b[...] = a[...]


def body(images, cot, g1, b1, wqkv, qvb, wo, outb, g2, b2, wup, upb, wdn, downb):
    flat = ((1, 16), F32)
    act = ((4, 64, CHUNK), BF)
    square = ((256, 256), F32)
    qkv, owo = ((192, 256), F32), ((64, 256), F32)
    kept = [act, act, ((8, 256), F32), qkv, owo, square, square]
    final = [act, act, flat, flat, qkv, ((1, 32), F32), owo]
    final += [flat, flat, flat, square, ((1, 64), F32), square, flat]
    space = pl.BlockSpec(memory_space=pltpu.VMEM)
    outs = pl.pallas_call(
        kernel,
        name="two_layers",
        out_shape=[jax.ShapeDtypeStruct(*x) for x in kept],
        in_specs=[space] * 14,
        out_specs=[space] * 7,
        scratch_shapes=list(SCRATCH.values()),
        compiler_params=pltpu.CompilerParams(
            collective_id=0, has_side_effects=True, vmem_limit_bytes=60 * 1024 * 1024
        ),
    )(
        images.reshape(4, CHUNK, 64).transpose(0, 2, 1),
        cot.reshape(4, CHUNK, 64).transpose(0, 2, 1),
        g1,
        b1,
        wqkv.reshape(D, 192).T,
        qvb.reshape(1, 128),
        wo.reshape(64, D),
        outb,
        g2,
        b2,
        wup.reshape(D, 256),
        upb,
        wdn.reshape(256, D),
        downb,
    )
    outs = pl.pallas_call(
        finish,
        name="finish",
        out_shape=[jax.ShapeDtypeStruct(*x) for x in final],
        in_specs=[space] * 7,
        out_specs=[space] * 14,
    )(*outs)
    act, ig, og1, ob1, oqkv, oqvb, owo, ooutb, og2, ob2, oup, oupb, odn, odownb = outs
    return (
        act.transpose(0, 2, 1).reshape(1, 4, 1, CHUNK, 64),
        ig.transpose(0, 2, 1).reshape(1, 4, 1, CHUNK, 64),
        og1,
        ob1,
        oqkv.T.reshape(1, 256, 1, 192),
        oqvb.reshape(1, 1, 32),
        owo.reshape(1, 1, 64, 256),
        ooutb,
        og2,
        ob2,
        oup.reshape(1, 256, 256),
        oupb,
        odn.reshape(1, 256, 256),
        odownb,
    )


def solution(mesh):
    in_specs = (
        P(None, None, "dp", "tensor"),
        P(None, None, "dp", "tensor"),
        P("section", "tensor"),
        P("section", "tensor"),
        P("section", None, "tensor", None),
        P("section", "tensor", None),
        P("section", "tensor", None, None),
        P("section", "tensor"),
        P("section", "tensor"),
        P("section", "tensor"),
        P("section", None, "tensor"),
        P("section", "tensor"),
        P("section", "tensor", None),
        P("section", "tensor"),
    )
    out_specs = (
        P("section", None, None, "dp", "tensor"),
        P("section", None, None, "dp", "tensor"),
        P("section", ("tensor", "dp")),
        P("section", ("tensor", "dp")),
        P("section", "dp", "tensor", None),
        P("section", "tensor", "dp"),
        P("section", "tensor", None, "dp"),
        P("section", ("tensor", "dp")),
        P("section", ("tensor", "dp")),
        P("section", ("tensor", "dp")),
        P("section", "dp", "tensor"),
        P("section", ("tensor", "dp")),
        P("section", "tensor", "dp"),
        P("section", ("tensor", "dp")),
    )
    return jax.shard_map(body, mesh=mesh, in_specs=in_specs, out_specs=out_specs, check_vma=False)
```
